256 devices in a mesh: dp: 64 (over z, y, core), head: 4 (over x).
Axes of the slice: x: 4, y: 4, z: 8, core: 2. Of those that a mesh axis runs over, the one named last changes fastest.
Arguments:
- queries: bfloat16 [16384, 8192], P('dp', 'head'), may hold values from -128 to 128
- answer_keys: bfloat16 [16384, 1024], P('dp', 'head'), may hold values from -5 to 5
- answer_values: bfloat16 [16384, 1024], P('dp', 'head'), may hold values from -6 to 6
- prompt_keys: bfloat16 [64, 256, 1024], P('dp', 'head'), may hold values from -6 to 6
- prompt_values: bfloat16 [64, 256, 1024], P('dp', 'head'), may hold values from -6 to 6
- output_gradient: bfloat16 [16384, 8192], P('dp', 'head'), may hold values from -6 to 6
- prompt_len: int32 [64], replicated, may hold values from 64 to 256
- response_len: int32 [256], P('dp'), may hold values from 1 to 64
- response_prompt: int32 [256], P('dp'), may hold values from 0 to 63, as said below
Outputs:
- attended: bfloat16 [16384, 8192], P('dp', 'head')
- grad_query: bfloat16 [16384, 8192], P('dp', 'head')
- grad_response_keys: bfloat16 [16384, 1024], P('dp', 'head')
- grad_response_values: bfloat16 [16384, 1024], P('dp', 'head')
- grad_prompt_keys: float32 [64, 256, 1024], P('dp', 'head')
- grad_prompt_values: float32 [64, 256, 1024], P('dp', 'head')
The draws below stay inside these ranges and needn't reach their ends.
Inputs may be any that keep to these rules, and one draw needn't show every extreme that they name: `response_prompt`: prompt p is the one at dp index p; the prompt of a slot at dp index i lies at most 2 indices from i, counted cyclically over 64, and both distances 2 occur.
All inputs are finite; a program needn't handle non-finite values.
Results may differ from the reference program's by a relative error of at most 0.035.
Values may be sent and summed in bfloat16 or wider, within the bound.
A program may use at most 64 MiB of HBM per device.

```python
import math
import jax
import jax.numpy as jnp
from jax import lax

QH = 64
KEY_VALUE_HEADS = 8
HEAD_SIZE = 128
PLEN = 256
RESPONSE_ROWS = 64
SLOTS_PER_RANK = 4
MAX_SPREAD = 2
PROMPT_COUNT = 64
TOTAL_SLOTS = 256
RESP_TOK = 16384


def shared_base(key):
    return jnp.clip(jax.random.normal(key, (RESP_TOK, KEY_VALUE_HEADS * HEAD_SIZE), jnp.float32), -5.0, 5.0)


def draw_queries(key, part):
    key = jax.random.fold_in(key, 1)
    drawn = jnp.clip(jax.random.normal(key, (RESP_TOK, QH * HEAD_SIZE), jnp.float32), -5.0, 5.0)
    return drawn.astype(jnp.bfloat16)


def draw_answer_keys(key, part):
    shared = shared_base(key)
    return shared.astype(jnp.bfloat16)


def draw_prompt_len(key, part):
    key = jax.random.fold_in(key, 3)
    length_list = jax.random.randint(key, (PROMPT_COUNT,), PLEN // 4, PLEN + 1, jnp.int32)
    where_long = jax.random.randint(jax.random.fold_in(key, 1), (), 0, PROMPT_COUNT, jnp.int32)
    length_list = length_list.at[where_long].set(PLEN)
    length_list = length_list.at[(where_long + 1) % PROMPT_COUNT].set(PLEN // 4)
    return length_list


def draw_response_len(key, part):
    key = jax.random.fold_in(key, 4)
    keepers = TOTAL_SLOTS // SLOTS_PER_RANK
    device_limits = jax.random.randint(key, (keepers, 1), RESPONSE_ROWS // 2, RESPONSE_ROWS + 1, jnp.int32)
    lower_limit = jnp.maximum(device_limits // 2, 1)
    length_list = jax.random.randint(jax.random.fold_in(key, 1), (keepers, SLOTS_PER_RANK), lower_limit, device_limits + 1, jnp.int32).reshape(TOTAL_SLOTS)
    picked_slot = jax.random.randint(jax.random.fold_in(key, 2), (), 0, TOTAL_SLOTS, jnp.int32)
    length_list = length_list.at[picked_slot].set(RESPONSE_ROWS)
    length_list = length_list.at[(picked_slot + 1) % TOTAL_SLOTS].set(1)
    return length_list


def draw_response_prompt(key, part):
    key = jax.random.fold_in(key, 5)
    keeper = jnp.arange(TOTAL_SLOTS, dtype=jnp.int32) // SLOTS_PER_RANK
    start_positions = jax.random.randint(key, (TOTAL_SLOTS,), -MAX_SPREAD, MAX_SPREAD + 1, jnp.int32)
    start_positions = start_positions.at[0].set(MAX_SPREAD)
    start_positions = start_positions.at[1].set(-MAX_SPREAD)
    prompt_numbers = jnp.mod(keeper + start_positions, PROMPT_COUNT)
    prompt_numbers = prompt_numbers.at[2].set(0)
    prompt_numbers = prompt_numbers.at[TOTAL_SLOTS - 1].set(PROMPT_COUNT - 1)
    return prompt_numbers.astype(jnp.int32)


def block_scale(rng, shape, pieces, low, largest):
    factor_of, own = 1.0, jax.random.fold_in(rng, 6)
    for axis_at, parts in pieces:
        heights = jnp.exp(jax.random.uniform(jax.random.fold_in(own, axis_at), (parts,), jnp.float32, low / len(pieces), largest / len(pieces)))
        factor_of = factor_of * jnp.repeat(heights, shape[axis_at] // parts).reshape([-1 if axis == axis_at else 1 for axis in range(len(shape))])
    return factor_of


def bell_draw(stream_key, shape, deviation, reach, pieces=(), kind=jnp.bfloat16):
    entries = deviation * jax.random.normal(stream_key, shape, jnp.float32)
    if pieces:
        entries = entries * block_scale(stream_key, shape, pieces, -0.22, 0.18)
    return jnp.clip(entries, -reach, reach).astype(kind)


def setup_inputs(seed: int = 0) -> dict:
    key_list = jax.random.split(jax.random.key(seed), 10)
    queries = draw_queries(jax.random.fold_in(key_list[9], 71), 0)
    answer_keys = draw_answer_keys(jax.random.fold_in(key_list[9], 71), 0)
    answer_values = bell_draw(key_list[2], (RESP_TOK, KEY_VALUE_HEADS * HEAD_SIZE), 1.0, 6.0, ((0, 64), (1, 4)))
    prompt_keys = bell_draw(key_list[3], (PROMPT_COUNT, PLEN, KEY_VALUE_HEADS * HEAD_SIZE), 1.0, 6.0, ((0, 64), (1, 4)))
    prompt_values = bell_draw(key_list[4], (PROMPT_COUNT, PLEN, KEY_VALUE_HEADS * HEAD_SIZE), 1.0, 6.0, ((0, 64), (1, 4)))
    output_gradient = bell_draw(key_list[5], (RESP_TOK, QH * HEAD_SIZE), 1.0, 6.0, ((0, 64), (1, 4)))
    prompt_len = draw_prompt_len(jax.random.fold_in(key_list[9], 71), 0)
    response_len = draw_response_len(jax.random.fold_in(key_list[9], 71), 0)
    response_prompt = draw_response_prompt(jax.random.fold_in(key_list[9], 71), 0)
    return {"queries": queries, "answer_keys": answer_keys, "answer_values": answer_values, "prompt_keys": prompt_keys, "prompt_values": prompt_values, "output_gradient": output_gradient, "prompt_len": prompt_len, "response_len": response_len, "response_prompt": response_prompt}


def attention_grads(slot_query, all_keys, all_values, output_gradient, prompt_size, answer_size):
    scaling = 1.0 / math.sqrt(HEAD_SIZE)
    query_wide = slot_query.astype(jnp.float32)
    keys_wide = all_keys.astype(jnp.float32)
    values_wide = all_values.astype(jnp.float32)
    scores = jnp.einsum('tkgd,jkd->kgtj', query_wide, keys_wide) * scaling
    rows_at = jnp.arange(RESPONSE_ROWS, dtype=jnp.int32)[:, None]
    cols_at = jnp.arange(PLEN + RESPONSE_ROWS, dtype=jnp.int32)[None, :]
    visible = jnp.where(cols_at < PLEN, cols_at < prompt_size, cols_at - PLEN <= rows_at)
    row_max = lax.optimization_barrier(jnp.max(jnp.where(visible, scores, -jnp.inf), axis=-1, keepdims=True))
    exponent = jnp.where(visible, jnp.exp(scores - row_max), 0.0)
    probability = exponent / lax.optimization_barrier(jnp.sum(exponent, axis=-1, keepdims=True))
    weights = lax.optimization_barrier(probability.astype(jnp.bfloat16)).astype(jnp.float32)
    live_scale = (jnp.arange(RESPONSE_ROWS, dtype=jnp.int32) < answer_size).astype(jnp.float32)[:, None, None, None]
    attended = (jnp.einsum('kgtj,jkd->tkgd', weights, values_wide) * live_scale).astype(jnp.bfloat16)
    attended_wide = lax.optimization_barrier(attended).astype(jnp.float32)
    grad_live = output_gradient.astype(jnp.float32) * live_scale
    row_delta = jnp.einsum('tkgd,tkgd->kgt', grad_live, attended_wide)[..., None]
    grad_values = jnp.einsum('kgtj,tkgd->jkd', weights, grad_live)
    grad_probs = jnp.einsum('tkgd,jkd->kgtj', grad_live, values_wide)
    grad_scores = (probability * (grad_probs - row_delta)).astype(jnp.bfloat16)
    grad_scores = lax.optimization_barrier(grad_scores).astype(jnp.float32)
    grad_query = (jnp.einsum('kgtj,jkd->tkgd', grad_scores, keys_wide) * scaling).astype(jnp.bfloat16)
    grad_keys = jnp.einsum('kgtj,tkgd->jkd', grad_scores, query_wide) * scaling
    return (attended, grad_query, grad_keys, grad_values)

def reference(queries, answer_keys, answer_values, prompt_keys, prompt_values, output_gradient, prompt_len, response_len, response_prompt):
    group_width = QH // KEY_VALUE_HEADS
    slot_queries = queries.reshape(TOTAL_SLOTS, RESPONSE_ROWS, KEY_VALUE_HEADS, group_width, HEAD_SIZE)
    slot_gradients = output_gradient.reshape(TOTAL_SLOTS, RESPONSE_ROWS, KEY_VALUE_HEADS, group_width, HEAD_SIZE)
    slot_keys = answer_keys.reshape(TOTAL_SLOTS, RESPONSE_ROWS, KEY_VALUE_HEADS, HEAD_SIZE)
    slot_values = answer_values.reshape(TOTAL_SLOTS, RESPONSE_ROWS, KEY_VALUE_HEADS, HEAD_SIZE)
    prompt_k = prompt_keys.reshape(PROMPT_COUNT, PLEN, KEY_VALUE_HEADS, HEAD_SIZE)
    prompt_v = prompt_values.reshape(PROMPT_COUNT, PLEN, KEY_VALUE_HEADS, HEAD_SIZE)

    def one_slot(carried, inputs):
        sum_keys, sum_values = carried
        slot_query, new_keys, new_values, slot_grad, owner_id, answer_size = inputs
        all_keys = jnp.concatenate([prompt_k[owner_id], new_keys], axis=0)
        all_values = jnp.concatenate([prompt_v[owner_id], new_values], axis=0)
        attended, grad_query, grad_keys, grad_values = attention_grads(slot_query, all_keys, all_values, slot_grad, prompt_len[owner_id], answer_size)
        sum_keys = sum_keys.at[owner_id].add(grad_keys[:PLEN])
        sum_values = sum_values.at[owner_id].add(grad_values[:PLEN])
        outputs = (attended, grad_query, grad_keys[PLEN:].astype(jnp.bfloat16), grad_values[PLEN:].astype(jnp.bfloat16))
        return ((sum_keys, sum_values), outputs)
    empty_sums = jnp.zeros((PROMPT_COUNT, PLEN, KEY_VALUE_HEADS, HEAD_SIZE), jnp.float32)
    sums, outputs = lax.scan(one_slot, (empty_sums, empty_sums), (slot_queries, slot_keys, slot_values, slot_gradients, response_prompt, response_len))
    attended, grad_query, grad_rkeys, grad_rvalues = outputs
    return (attended.reshape(RESP_TOK, QH * HEAD_SIZE), grad_query.reshape(RESP_TOK, QH * HEAD_SIZE), grad_rkeys.reshape(RESP_TOK, KEY_VALUE_HEADS * HEAD_SIZE), grad_rvalues.reshape(RESP_TOK, KEY_VALUE_HEADS * HEAD_SIZE), sums[0].reshape(PROMPT_COUNT, PLEN, KEY_VALUE_HEADS * HEAD_SIZE), sums[1].reshape(PROMPT_COUNT, PLEN, KEY_VALUE_HEADS * HEAD_SIZE))
```

```python
import functools
import math

import jax
import jax.numpy as jnp
from jax import lax
from jax.experimental import pallas as pl
from jax.experimental.pallas import tpu as pltpu
from jax.sharding import PartitionSpec as P

HEAD_SIZE = 128
PLEN = 256
MAX_SPREAD = 2
REACH = 2 * MAX_SPREAD + 1
MESH = pl.DeviceIdType.MESH
SCALING = 1.0 / math.sqrt(HEAD_SIZE)
F32 = jnp.float32
BF16 = jnp.bfloat16


def dot(a, b, dims):
    return lax.dot_general(a, b, (dims, ((), ())), preferred_element_type=F32)


NN = ((1,), (0,))
NT = ((1,), (1,))
TN = ((0,), (0,))


def kernel(sizes, *refs):
    devices, heads, slots, rows, kvh, group = sizes
    (plen_hbm, rlen_hbm, rprompt_hbm, q_hbm, do_hbm, ak_hbm, av_hbm, pk_hbm, pv_hbm,
     o_v, dq_v, gak_v, gav_v, gpk_out, gpv_out,
     plen_ref, rlen_ref, rprompt_ref,
     q_v, do_v, ak_v, av_v, qt_v, dot_v, p_v, w_v, ds_v) = refs[:27]
    pairs = [(hd, w) for hd in range(kvh) for w in range(2)]
    per_pair = refs[27:27 + 8 * len(pairs)]
    (kv, part, sib_out, sib_in, y_out, y_in, own, x_out) = [
        dict(zip(pairs, per_pair[i * len(pairs):(i + 1) * len(pairs)])) for i in range(8)
    ]
    (in_sem, x_send, x_recv, x_own, y_send, y_recv, s_send, s_recv,
     bs_send, bs_recv, by_send, by_recv, bx_send, bx_recv, bx_own) = refs[27 + 8 * len(pairs):]

    me = lax.axis_index("dp")
    h = lax.axis_index("head")
    core = lax.rem(me, 2)
    sibling = me + 1 - 2 * core
    up = lax.rem(me + 2, devices)
    down = lax.rem(me + devices - 2, devices)
    span = PLEN // heads
    width = kvh * HEAD_SIZE
    lanes = group * rows
    chunk = min(256, lanes)
    per = chunk // rows
    all_rows = PLEN + rows

    own_in = {}
    for hd, w in pairs:
        src = (pk_hbm, pv_hbm)[w]
        cols = pl.ds(pl.multiple_of(h * width + hd * HEAD_SIZE, HEAD_SIZE), HEAD_SIZE)
        mine = pl.ds(pl.multiple_of(h * span, span), span)
        own_in[hd, w] = pltpu.make_async_copy(
            src.at[:, cols], kv[hd, w].at[MAX_SPREAD, mine], x_own.at[hd, w])
        own_in[hd, w].start()
    loads = [
        pltpu.make_async_copy(src, dst, in_sem.at[i])
        for i, (src, dst) in enumerate(
            [(q_hbm, q_v), (do_hbm, do_v), (ak_hbm, ak_v), (av_hbm, av_v),
             (plen_hbm, plen_ref), (rlen_hbm, rlen_ref), (rprompt_hbm, rprompt_ref)])
    ]
    for load in loads:
        load.start()

    def remote(src, dst, send, recv, **where):
        return pltpu.make_async_remote_copy(
            src_ref=src, dst_ref=dst, send_sem=send, recv_sem=recv,
            device_id=where, device_id_type=MESH)

    peers = [lax.rem(h + p, heads) for p in range(1, heads)]
    order = [p for p in range(1, heads) if p != heads // 2] + [heads // 2]

    barrier = pltpu.get_barrier_semaphore()
    for p in peers:
        pl.semaphore_signal(barrier, inc=1, device_id={"head": p}, device_id_type=MESH)
    for d in (sibling, up, down):
        pl.semaphore_signal(barrier, inc=1, device_id={"dp": d}, device_id_type=MESH)
    pl.semaphore_wait(barrier, len(peers) + 3)

    x_in = {}
    for hd, w in pairs:
        src = (pk_hbm, pv_hbm)[w]
        for p in order:
            to = peers[p - 1]
            cols = pl.ds(pl.multiple_of(to * width + hd * HEAD_SIZE, HEAD_SIZE), HEAD_SIZE)
            x_in[hd, w, p] = remote(
                src.at[:, cols], kv[hd, w].at[MAX_SPREAD, mine],
                x_send.at[hd, w, p - 1], x_recv.at[hd, w, p - 1], head=to)
            x_in[hd, w, p].start()

    y_copies, s_copies, r_copies = {}, {}, {}

    def forward(hd, w, piece, span_rows):
        ref = kv[hd, w]
        src = ref.at[MAX_SPREAD, span_rows]
        y_copies[hd, w, piece] = [
            remote(src, ref.at[0, span_rows], y_send.at[hd, w, piece, 0],
                   y_recv.at[hd, w, piece, 0], dp=up),
            remote(src, ref.at[4, span_rows], y_send.at[hd, w, piece, 1],
                   y_recv.at[hd, w, piece, 1], dp=down),
        ]
        s_copies[hd, w, piece] = remote(
            src, ref.at[1 + 2 * core, span_rows], s_send.at[hd, w, piece, 0],
            s_recv.at[hd, w, piece, 0], dp=sibling)
        r_copies[hd, w, piece] = remote(
            ref.at[4 - 4 * core, span_rows], ref.at[3 - 2 * core, span_rows],
            s_send.at[hd, w, piece, 1], s_recv.at[hd, w, piece, 1], dp=sibling)
        for c in y_copies[hd, w, piece]:
            c.start()
        s_copies[hd, w, piece].start()

    pieces = {pair: [0] for pair in pairs}
    pieces[0, 0] = [0] + order

    def forward_all(hd, w):
        if len(pieces[hd, w]) > 1:
            for p in pieces[hd, w]:
                if p == 0:
                    own_in[hd, w].wait()
                else:
                    x_in[hd, w, p].wait_recv()
                source = lax.rem(h + heads - p, heads)
                forward(hd, w, p, pl.ds(pl.multiple_of(source * span, span), span))
        else:
            own_in[hd, w].wait()
            for p in order:
                x_in[hd, w, p].wait_recv()
            forward(hd, w, 0, pl.ds(0, PLEN))

    def relay_in(hd, w):
        for p in pieces[hd, w]:
            for c in y_copies[hd, w, p]:
                c.wait_recv()
            r_copies[hd, w, p].start()

    def arrived(hd, w):
        for p in pieces[hd, w]:
            s_copies[hd, w, p].wait_recv()
            r_copies[hd, w, p].wait_recv()

    def rows_of(s):
        return pl.ds(pl.multiple_of(s * rows, rows), rows)

    def columns(hd, c):
        first = hd * group + c * per
        return [slice((first + g) * HEAD_SIZE, (first + g + 1) * HEAD_SIZE) for g in range(per)]

    def stacked(ref, hd, s, c):
        return jnp.concatenate([ref[rows_of(s), col] for col in columns(hd, c)], axis=0)

    def relative(s):
        return lax.rem(rprompt_ref[s] - me + (devices + MAX_SPREAD), devices)

    def both(hd, w, s):
        rel = jnp.minimum(relative(s), REACH - 1)
        tail = (ak_v, av_v)[w][rows_of(s), hd * HEAD_SIZE:(hd + 1) * HEAD_SIZE]
        return jnp.concatenate([kv[hd, w][rel], tail], axis=0)

    def lanes_of(c):
        return slice(c * chunk, (c + 1) * chunk)

    def prepare(hd, s):
        for c in range(lanes // chunk):
            qt_v[hd, s, :, lanes_of(c)] = stacked(q_v, hd, s, c).T
            dot_v[hd, s, :, lanes_of(c)] = stacked(do_v, hd, s, c).T

    def probabilities(hd, s):
        psize = plen_ref[rprompt_ref[s]]
        rlen = rlen_ref[s]
        keys = both(hd, 0, s)
        live = (lax.rem(lax.broadcasted_iota(jnp.int32, (1, chunk), 1), rows) < rlen).astype(F32)
        head_seen = lax.broadcasted_iota(jnp.int32, (PLEN, chunk), 0) < psize
        tail_seen = lax.broadcasted_iota(jnp.int32, (rows, chunk), 0) <= lax.rem(
            lax.broadcasted_iota(jnp.int32, (rows, chunk), 1), rows)
        dv = jnp.zeros((all_rows, HEAD_SIZE), F32)
        for c in range(lanes // chunk):
            scores = dot(keys, qt_v[hd, s, :, lanes_of(c)], NN)
            masked = jnp.concatenate([
                jnp.where(head_seen, scores[:PLEN], -jnp.inf),
                jnp.where(tail_seen, scores[PLEN:], -jnp.inf)], axis=0)
            top = jnp.max(masked, axis=0, keepdims=True)
            e = jnp.exp2((masked - top) * (SCALING * math.log2(math.e)))
            prob = e * (live / jnp.sum(e, axis=0, keepdims=True))
            p_v[s, :, lanes_of(c)] = prob
            weights = prob.astype(BF16)
            w_v[hd, s, :, lanes_of(c)] = weights
            dv += dot(weights, stacked(do_v, hd, s, c), NN)
        part[hd, 1][s] = dv[:PLEN]
        gav_v[rows_of(s), hd * HEAD_SIZE:(hd + 1) * HEAD_SIZE] = dv[PLEN:].astype(BF16)

    def gradients(hd, s):
        values = both(hd, 1, s)
        dk = jnp.zeros((all_rows, HEAD_SIZE), F32)
        for c in range(lanes // chunk):
            prob = p_v[s, :, lanes_of(c)]
            gprob = dot(values, dot_v[hd, s, :, lanes_of(c)], NN)
            delta = jnp.sum(prob * gprob, axis=0, keepdims=True)
            gscores = (prob * (gprob - delta)).astype(BF16)
            ds_v[hd, s, :, lanes_of(c)] = gscores
            dk += dot(gscores, stacked(q_v, hd, s, c), NN)
        dk = dk * SCALING
        part[hd, 0][s] = dk[:PLEN]
        gak_v[rows_of(s), hd * HEAD_SIZE:(hd + 1) * HEAD_SIZE] = dk[PLEN:].astype(BF16)

    def row_outputs(hd, s):
        keys_t = both(hd, 0, s).T
        values_t = both(hd, 1, s).T
        for c in range(lanes // chunk):
            out = dot(values_t, w_v[hd, s, :, lanes_of(c)], NN).astype(BF16).T
            dq = (dot(keys_t, ds_v[hd, s, :, lanes_of(c)], NN) * SCALING).astype(BF16).T
            for g, col in enumerate(columns(hd, c)):
                o_v[rows_of(s), col] = out[g * rows:(g + 1) * rows]
                dq_v[rows_of(s), col] = dq[g * rows:(g + 1) * rows]

    def summed(pair, offset):
        total = None
        for s in range(slots):
            pick = jnp.where(relative(s) == offset, 1.0, 0.0).astype(F32)
            term = part[pair][s] * pick
            total = term if total is None else total + term
        return total

    direct, relayed = 4 * core, 4 - 4 * core
    direct_to = lax.rem(me + devices - 2 + 4 * core, devices)
    relay_to = lax.rem(me + devices + 2 - 4 * core, devices)
    b_sib, b_direct, b_relay, b_x, b_own = {}, {}, {}, {}, {}
    for pair in pairs:
        hd, w = pair
        b_sib[pair] = [
            remote(sib_out[pair].at[i], sib_in[pair].at[i], bs_send.at[hd, w, i],
                   bs_recv.at[hd, w, i], dp=sibling) for i in range(2)
        ]
        b_direct[pair] = remote(y_out[pair].at[0], y_in[pair].at[core], by_send.at[hd, w, 0],
                                by_recv.at[hd, w, core], dp=direct_to)
        b_relay[pair] = remote(y_out[pair].at[1], y_in[pair].at[1 - core],
                               by_send.at[hd, w, 1], by_recv.at[hd, w, 1 - core], dp=relay_to)
        dst = (gpk_out, gpv_out)[w]
        cols = pl.ds(pl.multiple_of(h * width + hd * HEAD_SIZE, HEAD_SIZE), HEAD_SIZE)
        b_x[pair] = []
        for p in order:
            to = peers[p - 1]
            theirs = pl.ds(pl.multiple_of(to * span, span), span)
            b_x[pair].append(remote(
                x_out[pair].at[theirs], dst.at[:, cols],
                bx_send.at[hd, w, p - 1], bx_recv.at[hd, w, p - 1], head=to))
        b_own[pair] = pltpu.make_async_copy(
            x_out[pair].at[mine], dst.at[:, cols], bx_own.at[hd, w])

    def back_first(pair):
        for i in range(2):
            sib_out[pair][i] = summed(pair, 1 + 2 * i).astype(BF16)
            b_sib[pair][i].start()
        y_out[pair][0] = summed(pair, direct).astype(BF16)
        b_direct[pair].start()

    def back_relay(pair):
        carry = summed(pair, relayed)
        own[pair][...] = summed(pair, MAX_SPREAD)
        for c in b_sib[pair]:
            c.wait_recv()
        y_out[pair][1] = (carry + sib_in[pair][1 - core].astype(F32)).astype(BF16)
        b_relay[pair].start()
        own[pair][...] += sib_in[pair][core].astype(F32)

    def back_last(pair):
        b_direct[pair].wait_recv()
        b_relay[pair].wait_recv()
        x_out[pair][...] = (own[pair][...] + y_in[pair][0].astype(F32)
                            + y_in[pair][1].astype(F32)).astype(BF16)
        for c in b_x[pair]:
            c.start()
        b_own[pair].start()

    def each_slot(work, hd, at=()):
        def step(s, carry):
            for when, what, *args in at:
                pl.when(s == when)(functools.partial(what, *args))
            work(hd, s)
            return carry

        lax.fori_loop(0, slots, step, 0)

    last = slots - 1
    forward_all(0, 0)
    forward_all(0, 1)
    for load in loads:
        load.wait()
    each_slot(prepare, 0)
    for hd, w in pairs[2:]:
        forward_all(hd, w)
    relay_in(0, 0)
    for hd in range(1, kvh):
        each_slot(prepare, hd)
    arrived(0, 0)

    back_steps = []

    for hd in range(kvh):
        at = []
        if hd == 0:
            at.append((1, relay_in, 0, 1))
        else:
            at.append((0, back_last, (hd - 1, 1)))
            at.append((1, back_relay, (hd - 1, 0)))
        if hd + 1 < kvh:
            at.append((last, relay_in, hd + 1, 0))
        each_slot(probabilities, hd, at)
        back_first((hd, 1))
        arrived(hd, 1)
        at = [(1, back_relay, (hd, 1))]
        if hd > 0:
            at.append((0, back_last, (hd - 1, 0)))
        if hd + 1 < kvh:
            at.append((last, relay_in, hd + 1, 1))
        each_slot(gradients, hd, at)
        back_first((hd, 0))
        if hd + 1 < kvh:
            arrived(hd + 1, 0)

    end = kvh - 1
    for hd in range(kvh):
        at = []
        if hd == 0:
            at = [(1, back_last, (end, 1)), (min(2, last), back_relay, (end, 0))]
        if hd == end:
            at.append((min(2, last), back_last, (end, 0)))
        each_slot(row_outputs, hd, at)

    for pair in pairs:
        hd, w = pair
        for p in order:
            x_in[hd, w, p].wait_send()
        for p in pieces[pair]:
            for c in y_copies[hd, w, p] + [s_copies[hd, w, p], r_copies[hd, w, p]]:
                c.wait_send()
        for c in b_sib[pair] + [b_direct[pair], b_relay[pair]]:
            c.wait_send()
        for c in b_x[pair]:
            c.wait()
        b_own[pair].wait()


def finish(o, dq, gak, gav, gpk, gpv, o_out, dq_out, gak_out, gav_out, gpk_out, gpv_out,
           wide_k, wide_v, sem):
    copies = [
        pltpu.make_async_copy(src, dst, sem.at[i])
        for i, (src, dst) in enumerate(
            [(o, o_out), (dq, dq_out), (gak, gak_out), (gav, gav_out),
             (wide_k, gpk_out.at[0]), (wide_v, gpv_out.at[0])])
    ]
    for copy in copies[:4]:
        copy.start()
    wide_k[...] = gpk[...].astype(F32)
    copies[4].start()
    wide_v[...] = gpv[...].astype(F32)
    copies[5].start()
    for copy in copies:
        copy.wait()


def on_device(queries, answer_keys, answer_values, prompt_keys, prompt_values,
              output_gradient, prompt_len, response_len, response_prompt):
    devices, heads = lax.axis_size("dp"), lax.axis_size("head")
    slots = response_len.shape[0]
    token_rows, q_width = queries.shape
    rows = token_rows // slots
    width = answer_keys.shape[1]
    kvh = width // HEAD_SIZE
    group = q_width // width
    lanes = group * rows
    span, full = prompt_keys.shape[1:]
    dma = pltpu.SemaphoreType.DMA
    anywhere = pl.BlockSpec(memory_space=pl.ANY)
    hbm = pl.BlockSpec(memory_space=pltpu.HBM)
    vmem = pl.BlockSpec(memory_space=pltpu.VMEM)
    vm, sm = pltpu.VMEM, pltpu.SMEM
    block = (PLEN, HEAD_SIZE)
    wide = vm((token_rows, q_width), BF16)
    narrow = vm((token_rows, width), BF16)
    turned = vm((kvh, slots, HEAD_SIZE, lanes), BF16)
    square = (PLEN + rows, lanes)
    per_pair = [
        vm((REACH,) + block, BF16), vm((slots,) + block, F32),
        vm((2,) + block, BF16), vm((2,) + block, BF16),
        vm((2,) + block, BF16), vm((2,) + block, BF16),
        vm(block, F32), vm(block, BF16),
    ]
    scratch = [
        sm(prompt_len.shape, jnp.int32), sm(response_len.shape, jnp.int32),
        sm(response_prompt.shape, jnp.int32),
        wide, wide, narrow, narrow, turned, turned, vm((slots,) + square, F32),
        vm((kvh, slots) + square, BF16), vm((kvh, slots) + square, BF16),
    ]
    for shape in per_pair:
        scratch += [shape] * (kvh * 2)
    scratch += [
        dma((7,)),
        dma((kvh, 2, heads - 1)), dma((kvh, 2, heads - 1)), dma((kvh, 2)),
        dma((kvh, 2, heads, 2)), dma((kvh, 2, heads, 2)),
        dma((kvh, 2, heads, 2)), dma((kvh, 2, heads, 2)),
        dma((kvh, 2, 2)), dma((kvh, 2, 2)), dma((kvh, 2, 2)), dma((kvh, 2, 2)),
        dma((kvh, 2, heads - 1)), dma((kvh, 2, heads - 1)), dma((kvh, 2)),
    ]
    sds = jax.ShapeDtypeStruct
    rows_out = [
        sds((token_rows, q_width), BF16), sds((token_rows, q_width), BF16),
        sds((token_rows, width), BF16), sds((token_rows, width), BF16),
    ]
    results = pl.pallas_call(
        functools.partial(kernel, (devices, heads, slots, rows, kvh, group)),
        out_shape=rows_out + [sds((span, full), BF16), sds((span, full), BF16)],
        in_specs=[hbm] * 9,
        out_specs=[vmem] * 4 + [anywhere] * 2,
        scratch_shapes=scratch,
        compiler_params=pltpu.CompilerParams(
            collective_id=0, has_side_effects=True, vmem_limit_bytes=48 * 1024 * 1024),
    )(prompt_len, response_len, response_prompt, queries, output_gradient,
      answer_keys, answer_values, prompt_keys.reshape(span, full),
      prompt_values.reshape(span, full))
    return pl.pallas_call(
        finish,
        out_shape=rows_out + [sds((1, span, full), F32), sds((1, span, full), F32)],
        in_specs=[anywhere] * 4 + [vmem] * 2,
        out_specs=[anywhere] * 6,
        scratch_shapes=[vm((span, full), F32), vm((span, full), F32), dma((6,))],
    )(*results)


def solution(mesh):
    in_specs = (
        P("dp", "head"),
        P("dp", "head"),
        P("dp", "head"),
        P("dp", "head", None),
        P("dp", "head", None),
        P("dp", "head"),
        P(),
        P("dp"),
        P("dp"),
    )
    out_specs = (
        P("dp", "head"),
        P("dp", "head"),
        P("dp", "head"),
        P("dp", "head"),
        P("dp", "head", None),
        P("dp", "head", None),
    )
    return jax.shard_map(
        on_device, mesh=mesh, in_specs=in_specs, out_specs=out_specs, check_vma=False
    )
```

```python
import functools
import math

import jax
import jax.numpy as jnp
from jax import lax
from jax.experimental import pallas as pl
from jax.experimental.pallas import tpu as pltpu
from jax.sharding import PartitionSpec as P

HEAD_SIZE = 128
PLEN = 256
MAX_SPREAD = 2
REACH = 2 * MAX_SPREAD + 1
MESH = pl.DeviceIdType.MESH
SCALING = 1.0 / math.sqrt(HEAD_SIZE)
F32 = jnp.float32
BF16 = jnp.bfloat16


def dot(a, b, dims):
    return lax.dot_general(a, b, (dims, ((), ())), preferred_element_type=F32)


NN = ((1,), (0,))
NT = ((1,), (1,))
TN = ((0,), (0,))


def kernel(sizes, *refs):
    devices, heads, slots, rows, kvh, group = sizes
    (plen_hbm, rlen_hbm, rprompt_hbm, q_hbm, do_hbm, ak_hbm, av_hbm, pk_hbm, pv_hbm,
     o_v, dq_v, gak_v, gav_v, gpk_out, gpv_out,
     plen_ref, rlen_ref, rprompt_ref,
     q_v, do_v, ak_v, av_v, p_v, w_v, ds_v) = refs[:25]
    pairs = [(hd, w) for hd in range(kvh) for w in range(2)]
    per_pair = refs[25:25 + 8 * len(pairs)]
    (kv, part, sib_out, sib_in, y_out, y_in, own, x_out) = [
        dict(zip(pairs, per_pair[i * len(pairs):(i + 1) * len(pairs)])) for i in range(8)
    ]
    (in_sem, x_send, x_recv, x_own, y_send, y_recv, s_send, s_recv,
     bs_send, bs_recv, by_send, by_recv, bx_send, bx_recv, bx_own) = refs[25 + 8 * len(pairs):]

    me = lax.axis_index("dp")
    h = lax.axis_index("head")
    core = lax.rem(me, 2)
    sibling = me + 1 - 2 * core
    up = lax.rem(me + 2, devices)
    down = lax.rem(me + devices - 2, devices)
    span = PLEN // heads
    width = kvh * HEAD_SIZE
    lanes = group * rows
    chunk = min(256, lanes)
    per = chunk // rows
    all_rows = PLEN + rows

    own_in = {}
    for hd, w in pairs:
        src = (pk_hbm, pv_hbm)[w]
        cols = pl.ds(pl.multiple_of(h * width + hd * HEAD_SIZE, HEAD_SIZE), HEAD_SIZE)
        mine = pl.ds(pl.multiple_of(h * span, span), span)
        own_in[hd, w] = pltpu.make_async_copy(
            src.at[:, cols], kv[hd, w].at[MAX_SPREAD, mine], x_own.at[hd, w])
        own_in[hd, w].start()
    loads = [
        pltpu.make_async_copy(src, dst, in_sem.at[i])
        for i, (src, dst) in enumerate(
            [(q_hbm, q_v), (do_hbm, do_v), (ak_hbm, ak_v), (av_hbm, av_v),
             (plen_hbm, plen_ref), (rlen_hbm, rlen_ref), (rprompt_hbm, rprompt_ref)])
    ]
    for load in loads:
        load.start()

    def remote(src, dst, send, recv, **where):
        return pltpu.make_async_remote_copy(
            src_ref=src, dst_ref=dst, send_sem=send, recv_sem=recv,
            device_id=where, device_id_type=MESH)

    peers = [lax.rem(h + p, heads) for p in range(1, heads)]
    order = [p for p in range(1, heads) if p != heads // 2] + [heads // 2]

    barrier = pltpu.get_barrier_semaphore()
    for p in peers:
        pl.semaphore_signal(barrier, inc=1, device_id={"head": p}, device_id_type=MESH)
    for d in (sibling, up, down):
        pl.semaphore_signal(barrier, inc=1, device_id={"dp": d}, device_id_type=MESH)
    pl.semaphore_wait(barrier, len(peers) + 3)

    x_in = {}
    for hd, w in pairs:
        src = (pk_hbm, pv_hbm)[w]
        for p in order:
            to = peers[p - 1]
            cols = pl.ds(pl.multiple_of(to * width + hd * HEAD_SIZE, HEAD_SIZE), HEAD_SIZE)
            x_in[hd, w, p] = remote(
                src.at[:, cols], kv[hd, w].at[MAX_SPREAD, mine],
                x_send.at[hd, w, p - 1], x_recv.at[hd, w, p - 1], head=to)
            x_in[hd, w, p].start()

    y_copies, s_copies, r_copies = {}, {}, {}

    def forward(hd, w, piece, span_rows):
        ref = kv[hd, w]
        src = ref.at[MAX_SPREAD, span_rows]
        y_copies[hd, w, piece] = [
            remote(src, ref.at[0, span_rows], y_send.at[hd, w, piece, 0],
                   y_recv.at[hd, w, piece, 0], dp=up),
            remote(src, ref.at[4, span_rows], y_send.at[hd, w, piece, 1],
                   y_recv.at[hd, w, piece, 1], dp=down),
        ]
        s_copies[hd, w, piece] = remote(
            src, ref.at[1 + 2 * core, span_rows], s_send.at[hd, w, piece, 0],
            s_recv.at[hd, w, piece, 0], dp=sibling)
        r_copies[hd, w, piece] = remote(
            ref.at[4 - 4 * core, span_rows], ref.at[3 - 2 * core, span_rows],
            s_send.at[hd, w, piece, 1], s_recv.at[hd, w, piece, 1], dp=sibling)
        for c in y_copies[hd, w, piece]:
            c.start()
        s_copies[hd, w, piece].start()

    pieces = {pair: [0] for pair in pairs}
    pieces[0, 0] = [0] + order

    def forward_all(hd, w):
        if len(pieces[hd, w]) > 1:
            for p in pieces[hd, w]:
                if p == 0:
                    own_in[hd, w].wait()
                else:
                    x_in[hd, w, p].wait_recv()
                source = lax.rem(h + heads - p, heads)
                forward(hd, w, p, pl.ds(pl.multiple_of(source * span, span), span))
        else:
            own_in[hd, w].wait()
            for p in order:
                x_in[hd, w, p].wait_recv()
            forward(hd, w, 0, pl.ds(0, PLEN))

    def relay_in(hd, w):
        for p in pieces[hd, w]:
            for c in y_copies[hd, w, p]:
                c.wait_recv()
            r_copies[hd, w, p].start()

    def arrived(hd, w):
        for p in pieces[hd, w]:
            s_copies[hd, w, p].wait_recv()
            r_copies[hd, w, p].wait_recv()

    def rows_of(s):
        return pl.ds(pl.multiple_of(s * rows, rows), rows)

    def columns(hd, c):
        first = hd * group + c * per
        return [slice((first + g) * HEAD_SIZE, (first + g + 1) * HEAD_SIZE) for g in range(per)]

    def stacked(ref, hd, s, c):
        return jnp.concatenate([ref[rows_of(s), col] for col in columns(hd, c)], axis=0)

    def relative(s):
        return lax.rem(rprompt_ref[s] - me + (devices + MAX_SPREAD), devices)

    def both(hd, w, s):
        rel = jnp.minimum(relative(s), REACH - 1)
        tail = (ak_v, av_v)[w][rows_of(s), hd * HEAD_SIZE:(hd + 1) * HEAD_SIZE]
        return jnp.concatenate([kv[hd, w][rel], tail], axis=0)

    def lanes_of(c):
        return slice(c * chunk, (c + 1) * chunk)

    def probabilities(hd, s):
        psize = plen_ref[rprompt_ref[s]]
        rlen = rlen_ref[s]
        keys = both(hd, 0, s)
        live = (lax.rem(lax.broadcasted_iota(jnp.int32, (1, chunk), 1), rows) < rlen).astype(F32)
        head_seen = lax.broadcasted_iota(jnp.int32, (PLEN, chunk), 0) < psize
        tail_seen = lax.broadcasted_iota(jnp.int32, (rows, chunk), 0) <= lax.rem(
            lax.broadcasted_iota(jnp.int32, (rows, chunk), 1), rows)
        dv = jnp.zeros((all_rows, HEAD_SIZE), F32)
        for c in range(lanes // chunk):
            scores = dot(keys, stacked(q_v, hd, s, c), NT)
            masked = jnp.concatenate([
                jnp.where(head_seen, scores[:PLEN], -jnp.inf),
                jnp.where(tail_seen, scores[PLEN:], -jnp.inf)], axis=0)
            top = jnp.max(masked, axis=0, keepdims=True)
            e = jnp.exp2((masked - top) * (SCALING * math.log2(math.e)))
            prob = e * (live / jnp.sum(e, axis=0, keepdims=True))
            p_v[s, :, lanes_of(c)] = prob
            weights = prob.astype(BF16)
            w_v[hd, s, :, lanes_of(c)] = weights
            dv += dot(weights, stacked(do_v, hd, s, c), NN)
        part[hd, 1][s] = dv[:PLEN]
        gav_v[rows_of(s), hd * HEAD_SIZE:(hd + 1) * HEAD_SIZE] = dv[PLEN:].astype(BF16)

    def gradients(hd, s):
        values = both(hd, 1, s)
        dk = jnp.zeros((all_rows, HEAD_SIZE), F32)
        for c in range(lanes // chunk):
            prob = p_v[s, :, lanes_of(c)]
            gprob = dot(values, stacked(do_v, hd, s, c), NT)
            delta = jnp.sum(prob * gprob, axis=0, keepdims=True)
            gscores = (prob * (gprob - delta)).astype(BF16)
            ds_v[hd, s, :, lanes_of(c)] = gscores
            dk += dot(gscores, stacked(q_v, hd, s, c), NN)
        dk = dk * SCALING
        part[hd, 0][s] = dk[:PLEN]
        gak_v[rows_of(s), hd * HEAD_SIZE:(hd + 1) * HEAD_SIZE] = dk[PLEN:].astype(BF16)

    def row_outputs(hd, s):
        keys_t = both(hd, 0, s).T
        values_t = both(hd, 1, s).T
        for c in range(lanes // chunk):
            out = dot(values_t, w_v[hd, s, :, lanes_of(c)], NN).astype(BF16).T
            dq = (dot(keys_t, ds_v[hd, s, :, lanes_of(c)], NN) * SCALING).astype(BF16).T
            for g, col in enumerate(columns(hd, c)):
                o_v[rows_of(s), col] = out[g * rows:(g + 1) * rows]
                dq_v[rows_of(s), col] = dq[g * rows:(g + 1) * rows]

    def summed(pair, offset):
        total = None
        for s in range(slots):
            pick = jnp.where(relative(s) == offset, 1.0, 0.0).astype(F32)
            term = part[pair][s] * pick
            total = term if total is None else total + term
        return total

    direct, relayed = 4 * core, 4 - 4 * core
    direct_to = lax.rem(me + devices - 2 + 4 * core, devices)
    relay_to = lax.rem(me + devices + 2 - 4 * core, devices)
    b_sib, b_direct, b_relay, b_x, b_own = {}, {}, {}, {}, {}
    for pair in pairs:
        hd, w = pair
        b_sib[pair] = [
            remote(sib_out[pair].at[i], sib_in[pair].at[i], bs_send.at[hd, w, i],
                   bs_recv.at[hd, w, i], dp=sibling) for i in range(2)
        ]
        b_direct[pair] = remote(y_out[pair].at[0], y_in[pair].at[core], by_send.at[hd, w, 0],
                                by_recv.at[hd, w, core], dp=direct_to)
        b_relay[pair] = remote(y_out[pair].at[1], y_in[pair].at[1 - core],
                               by_send.at[hd, w, 1], by_recv.at[hd, w, 1 - core], dp=relay_to)
        dst = (gpk_out, gpv_out)[w]
        cols = pl.ds(pl.multiple_of(h * width + hd * HEAD_SIZE, HEAD_SIZE), HEAD_SIZE)
        b_x[pair] = []
        for p in order:
            to = peers[p - 1]
            theirs = pl.ds(pl.multiple_of(to * span, span), span)
            b_x[pair].append(remote(
                x_out[pair].at[theirs], dst.at[:, cols],
                bx_send.at[hd, w, p - 1], bx_recv.at[hd, w, p - 1], head=to))
        b_own[pair] = pltpu.make_async_copy(
            x_out[pair].at[mine], dst.at[:, cols], bx_own.at[hd, w])

    def back_first(pair):
        for i in range(2):
            sib_out[pair][i] = summed(pair, 1 + 2 * i).astype(BF16)
            b_sib[pair][i].start()
        y_out[pair][0] = summed(pair, direct).astype(BF16)
        b_direct[pair].start()

    def back_relay(pair):
        carry = summed(pair, relayed)
        own[pair][...] = summed(pair, MAX_SPREAD)
        for c in b_sib[pair]:
            c.wait_recv()
        y_out[pair][1] = (carry + sib_in[pair][1 - core].astype(F32)).astype(BF16)
        b_relay[pair].start()
        own[pair][...] += sib_in[pair][core].astype(F32)

    def back_last(pair):
        b_direct[pair].wait_recv()
        b_relay[pair].wait_recv()
        x_out[pair][...] = (own[pair][...] + y_in[pair][0].astype(F32)
                            + y_in[pair][1].astype(F32)).astype(BF16)
        for c in b_x[pair]:
            c.start()
        b_own[pair].start()

    def each_slot(work, hd, at=()):
        def step(s, carry):
            for when, what, *args in at:
                pl.when(s == when)(functools.partial(what, *args))
            work(hd, s)
            return carry

        lax.fori_loop(0, slots, step, 0)

    last = slots - 1
    for hd, w in pairs:
        forward_all(hd, w)
    for load in loads:
        load.wait()
    relay_in(0, 0)
    arrived(0, 0)

    for hd in range(kvh):
        at = []
        if hd == 0:
            at.append((1, relay_in, 0, 1))
        else:
            at.append((0, back_last, (hd - 1, 1)))
            at.append((1, back_relay, (hd - 1, 0)))
        if hd + 1 < kvh:
            at.append((last, relay_in, hd + 1, 0))
        each_slot(probabilities, hd, at)
        back_first((hd, 1))
        arrived(hd, 1)
        at = [(1, back_relay, (hd, 1))]
        if hd > 0:
            at.append((0, back_last, (hd - 1, 0)))
        if hd + 1 < kvh:
            at.append((last, relay_in, hd + 1, 1))
        each_slot(gradients, hd, at)
        back_first((hd, 0))
        if hd + 1 < kvh:
            arrived(hd + 1, 0)

    end = kvh - 1
    for hd in range(kvh):
        at = []
        if hd == 0:
            at = [(1, back_last, (end, 1)), (min(2, last), back_relay, (end, 0))]
        if hd == end:
            at.append((min(2, last), back_last, (end, 0)))
        each_slot(row_outputs, hd, at)

    for pair in pairs:
        hd, w = pair
        for p in order:
            x_in[hd, w, p].wait_send()
        for p in pieces[pair]:
            for c in y_copies[hd, w, p] + [s_copies[hd, w, p], r_copies[hd, w, p]]:
                c.wait_send()
        for c in b_sib[pair] + [b_direct[pair], b_relay[pair]]:
            c.wait_send()
        for c in b_x[pair]:
            c.wait()
        b_own[pair].wait()


def finish(o, dq, gak, gav, gpk, gpv, o_out, dq_out, gak_out, gav_out, gpk_out, gpv_out,
           wide_k, wide_v, sem):
    copies = [
        pltpu.make_async_copy(src, dst, sem.at[i])
        for i, (src, dst) in enumerate(
            [(o, o_out), (dq, dq_out), (gak, gak_out), (gav, gav_out),
             (wide_k, gpk_out.at[0]), (wide_v, gpv_out.at[0])])
    ]
    for copy in copies[:4]:
        copy.start()
    wide_k[...] = gpk[...].astype(F32)
    copies[4].start()
    wide_v[...] = gpv[...].astype(F32)
    copies[5].start()
    for copy in copies:
        copy.wait()


def on_device(queries, answer_keys, answer_values, prompt_keys, prompt_values,
              output_gradient, prompt_len, response_len, response_prompt):
    devices, heads = lax.axis_size("dp"), lax.axis_size("head")
    slots = response_len.shape[0]
    token_rows, q_width = queries.shape
    rows = token_rows // slots
    width = answer_keys.shape[1]
    kvh = width // HEAD_SIZE
    group = q_width // width
    lanes = group * rows
    span, full = prompt_keys.shape[1:]
    dma = pltpu.SemaphoreType.DMA
    anywhere = pl.BlockSpec(memory_space=pl.ANY)
    hbm = pl.BlockSpec(memory_space=pltpu.HBM)
    vmem = pl.BlockSpec(memory_space=pltpu.VMEM)
    vm, sm = pltpu.VMEM, pltpu.SMEM
    block = (PLEN, HEAD_SIZE)
    wide = vm((token_rows, q_width), BF16)
    narrow = vm((token_rows, width), BF16)
    square = (PLEN + rows, lanes)
    per_pair = [
        vm((REACH,) + block, BF16), vm((slots,) + block, F32),
        vm((2,) + block, BF16), vm((2,) + block, BF16),
        vm((2,) + block, BF16), vm((2,) + block, BF16),
        vm(block, F32), vm(block, BF16),
    ]
    scratch = [
        sm(prompt_len.shape, jnp.int32), sm(response_len.shape, jnp.int32),
        sm(response_prompt.shape, jnp.int32),
        wide, wide, narrow, narrow, vm((slots,) + square, F32),
        vm((kvh, slots) + square, BF16), vm((kvh, slots) + square, BF16),
    ]
    for shape in per_pair:
        scratch += [shape] * (kvh * 2)
    scratch += [
        dma((7,)),
        dma((kvh, 2, heads - 1)), dma((kvh, 2, heads - 1)), dma((kvh, 2)),
        dma((kvh, 2, heads, 2)), dma((kvh, 2, heads, 2)),
        dma((kvh, 2, heads, 2)), dma((kvh, 2, heads, 2)),
        dma((kvh, 2, 2)), dma((kvh, 2, 2)), dma((kvh, 2, 2)), dma((kvh, 2, 2)),
        dma((kvh, 2, heads - 1)), dma((kvh, 2, heads - 1)), dma((kvh, 2)),
    ]
    sds = jax.ShapeDtypeStruct
    rows_out = [
        sds((token_rows, q_width), BF16), sds((token_rows, q_width), BF16),
        sds((token_rows, width), BF16), sds((token_rows, width), BF16),
    ]
    results = pl.pallas_call(
        functools.partial(kernel, (devices, heads, slots, rows, kvh, group)),
        out_shape=rows_out + [sds((span, full), BF16), sds((span, full), BF16)],
        in_specs=[hbm] * 9,
        out_specs=[vmem] * 4 + [anywhere] * 2,
        scratch_shapes=scratch,
        compiler_params=pltpu.CompilerParams(
            collective_id=0, has_side_effects=True, vmem_limit_bytes=48 * 1024 * 1024),
    )(*[pltpu.with_memory_space_constraint(x, pltpu.HBM) for x in (
        prompt_len, response_len, response_prompt, queries, output_gradient,
        answer_keys, answer_values, prompt_keys.reshape(span, full),
        prompt_values.reshape(span, full))])
    return pl.pallas_call(
        finish,
        out_shape=rows_out + [sds((1, span, full), F32), sds((1, span, full), F32)],
        in_specs=[vmem] * 6,
        out_specs=[anywhere] * 6,
        scratch_shapes=[vm((span, full), F32), vm((span, full), F32), dma((6,))],
    )(*results)


def solution(mesh):
    in_specs = (
        P("dp", "head"),
        P("dp", "head"),
        P("dp", "head"),
        P("dp", "head", None),
        P("dp", "head", None),
        P("dp", "head"),
        P(),
        P("dp"),
        P("dp"),
    )
    out_specs = (
        P("dp", "head"),
        P("dp", "head"),
        P("dp", "head"),
        P("dp", "head"),
        P("dp", "head", None),
        P("dp", "head", None),
    )
    return jax.shard_map(
        on_device, mesh=mesh, in_specs=in_specs, out_specs=out_specs, check_vma=False
    )
```

```python
import functools
import math

import jax
import jax.numpy as jnp
from jax import lax
from jax.experimental import pallas as pl
from jax.experimental.pallas import tpu as pltpu
from jax.sharding import PartitionSpec as P

HEAD_SIZE = 128
PLEN = 256
MAX_SPREAD = 2
REACH = 2 * MAX_SPREAD + 1
MESH = pl.DeviceIdType.MESH
SCALING = 1.0 / math.sqrt(HEAD_SIZE)
F32 = jnp.float32
BF16 = jnp.bfloat16


def dot(a, b, dims):
    return lax.dot_general(a, b, (dims, ((), ())), preferred_element_type=F32)


NN = ((1,), (0,))
NT = ((1,), (1,))
TN = ((0,), (0,))


def kernel(sizes, *refs):
    devices, heads, slots, rows, kvh, group = sizes
    (plen_hbm, rlen_hbm, rprompt_hbm, q_hbm, do_hbm, ak_hbm, av_hbm, pk_hbm, pv_hbm,
     o_v, dq_v, gak_v, gav_v, gpk_out, gpv_out,
     plen_ref, rlen_ref, rprompt_ref,
     q_v, do_v, ak_v, av_v, p_v, w_v, ds_v) = refs[:25]
    pairs = [(hd, w) for hd in range(kvh) for w in range(2)]
    per_pair = refs[25:25 + 8 * len(pairs)]
    (kv, part, sib_out, sib_in, y_out, y_in, own, x_out) = [
        dict(zip(pairs, per_pair[i * len(pairs):(i + 1) * len(pairs)])) for i in range(8)
    ]
    (in_sem, x_send, x_recv, x_own, y_send, y_recv, s_send, s_recv,
     bs_send, bs_recv, by_send, by_recv, bx_send, bx_recv, bx_own) = refs[25 + 8 * len(pairs):]

    me = lax.axis_index("dp")
    h = lax.axis_index("head")
    core = lax.rem(me, 2)
    sibling = me + 1 - 2 * core
    up = lax.rem(me + 2, devices)
    down = lax.rem(me + devices - 2, devices)
    offsets = [-2, 2, -1, 1]
    near = [lax.rem(me + devices + o, devices) for o in offsets]
    span = PLEN // heads
    width = kvh * HEAD_SIZE
    lanes = group * rows
    chunk = min(256, lanes)
    per = chunk // rows
    all_rows = PLEN + rows

    own_in = {}
    for hd, w in pairs:
        src = (pk_hbm, pv_hbm)[w]
        cols = pl.ds(pl.multiple_of(h * width + hd * HEAD_SIZE, HEAD_SIZE), HEAD_SIZE)
        mine = pl.ds(pl.multiple_of(h * span, span), span)
        own_in[hd, w] = pltpu.make_async_copy(
            src.at[:, cols], kv[hd, w].at[MAX_SPREAD, mine], x_own.at[hd, w])
        own_in[hd, w].start()
    loads = [
        pltpu.make_async_copy(src, dst, in_sem.at[i])
        for i, (src, dst) in enumerate(
            [(q_hbm, q_v), (do_hbm, do_v), (ak_hbm, ak_v), (av_hbm, av_v),
             (plen_hbm, plen_ref), (rlen_hbm, rlen_ref), (rprompt_hbm, rprompt_ref)])
    ]
    for load in loads:
        load.start()

    def remote(src, dst, send, recv, **where):
        return pltpu.make_async_remote_copy(
            src_ref=src, dst_ref=dst, send_sem=send, recv_sem=recv,
            device_id=where, device_id_type=MESH)

    peers = [lax.rem(h + p, heads) for p in range(1, heads)]
    order = [p for p in range(1, heads) if p != heads // 2] + [heads // 2]

    barrier = pltpu.get_barrier_semaphore()
    for p in peers:
        pl.semaphore_signal(barrier, inc=1, device_id={"head": p}, device_id_type=MESH)
    for d in near:
        pl.semaphore_signal(barrier, inc=1, device_id={"dp": d}, device_id_type=MESH)
    pl.semaphore_wait(barrier, len(peers) + len(near))

    x_in = {}
    for hd, w in pairs:
        src = (pk_hbm, pv_hbm)[w]
        for p in order:
            to = peers[p - 1]
            cols = pl.ds(pl.multiple_of(to * width + hd * HEAD_SIZE, HEAD_SIZE), HEAD_SIZE)
            x_in[hd, w, p] = remote(
                src.at[:, cols], kv[hd, w].at[MAX_SPREAD, mine],
                x_send.at[hd, w, p - 1], x_recv.at[hd, w, p - 1], head=to)
            x_in[hd, w, p].start()

    first_in, last_back = (0, 0), (kvh - 1, 0)
    y_copies, s_copies, r_copies = {}, {}, {}

    def forward(hd, w, piece, span_rows):
        ref = kv[hd, w]
        src = ref.at[MAX_SPREAD, span_rows]
        if (hd, w) == first_in:
            y_copies[hd, w, piece] = [
                remote(src, ref.at[MAX_SPREAD - o, span_rows], y_send.at[hd, w, piece, i],
                       y_recv.at[hd, w, piece, i], dp=near[i]) for i, o in enumerate(offsets)
            ]
            for c in y_copies[hd, w, piece]:
                c.start()
            return
        y_copies[hd, w, piece] = [
            remote(src, ref.at[0, span_rows], y_send.at[hd, w, piece, 0],
                   y_recv.at[hd, w, piece, 0], dp=up),
            remote(src, ref.at[4, span_rows], y_send.at[hd, w, piece, 1],
                   y_recv.at[hd, w, piece, 1], dp=down),
        ]
        s_copies[hd, w, piece] = remote(
            src, ref.at[1 + 2 * core, span_rows], s_send.at[hd, w, piece, 0],
            s_recv.at[hd, w, piece, 0], dp=sibling)
        r_copies[hd, w, piece] = remote(
            ref.at[4 - 4 * core, span_rows], ref.at[3 - 2 * core, span_rows],
            s_send.at[hd, w, piece, 1], s_recv.at[hd, w, piece, 1], dp=sibling)
        for c in y_copies[hd, w, piece]:
            c.start()
        s_copies[hd, w, piece].start()

    pieces = {pair: [0] for pair in pairs}
    pieces[0, 0] = [0] + order

    def forward_all(hd, w):
        if len(pieces[hd, w]) > 1:
            for p in pieces[hd, w]:
                if p == 0:
                    own_in[hd, w].wait()
                else:
                    x_in[hd, w, p].wait_recv()
                source = lax.rem(h + heads - p, heads)
                forward(hd, w, p, pl.ds(pl.multiple_of(source * span, span), span))
        else:
            own_in[hd, w].wait()
            for p in order:
                x_in[hd, w, p].wait_recv()
            forward(hd, w, 0, pl.ds(0, PLEN))

    def relay_in(hd, w):
        if (hd, w) == first_in:
            return
        for p in pieces[hd, w]:
            for c in y_copies[hd, w, p]:
                c.wait_recv()
            r_copies[hd, w, p].start()

    def arrived(hd, w):
        for p in pieces[hd, w]:
            if (hd, w) == first_in:
                for c in y_copies[hd, w, p]:
                    c.wait_recv()
                continue
            s_copies[hd, w, p].wait_recv()
            r_copies[hd, w, p].wait_recv()

    def rows_of(s):
        return slice(s * rows, (s + 1) * rows)

    def columns(hd, c):
        first = hd * group + c * per
        return [slice((first + g) * HEAD_SIZE, (first + g + 1) * HEAD_SIZE) for g in range(per)]

    def stacked(ref, hd, s, c):
        return jnp.concatenate([ref[rows_of(s), col] for col in columns(hd, c)], axis=0)

    def relative(s):
        return lax.rem(rprompt_ref[s] - me + (devices + MAX_SPREAD), devices)

    def both(hd, w, s):
        rel = jnp.minimum(relative(s), REACH - 1)
        tail = (ak_v, av_v)[w][rows_of(s), hd * HEAD_SIZE:(hd + 1) * HEAD_SIZE]
        return jnp.concatenate([kv[hd, w][rel], tail], axis=0)

    def lanes_of(c):
        return slice(c * chunk, (c + 1) * chunk)

    def probabilities(hd, s):
        psize = plen_ref[rprompt_ref[s]]
        rlen = rlen_ref[s]
        keys = both(hd, 0, s)
        live = ((lax.broadcasted_iota(jnp.int32, (1, chunk), 1) & (rows - 1)) < rlen).astype(F32)
        head_seen = lax.broadcasted_iota(jnp.int32, (PLEN, chunk), 0) < psize
        tail_seen = lax.broadcasted_iota(jnp.int32, (rows, chunk), 0) <= (
            lax.broadcasted_iota(jnp.int32, (rows, chunk), 1) & (rows - 1))
        dv = jnp.zeros((all_rows, HEAD_SIZE), F32)
        for c in range(lanes // chunk):
            scores = dot(keys, stacked(q_v, hd, s, c), NT)
            masked = jnp.concatenate([
                jnp.where(head_seen, scores[:PLEN], -jnp.inf),
                jnp.where(tail_seen, scores[PLEN:], -jnp.inf)], axis=0)
            top = jnp.max(masked, axis=0, keepdims=True)
            e = jnp.exp2((masked - top) * (SCALING * math.log2(math.e)))
            prob = e * (live / jnp.sum(e, axis=0, keepdims=True))
            p_v[s, :, lanes_of(c)] = prob
            weights = prob.astype(BF16)
            w_v[hd, s, :, lanes_of(c)] = weights
            dv += dot(weights, stacked(do_v, hd, s, c), NN)
        part[hd, 1][s] = dv[:PLEN]
        gav_v[rows_of(s), hd * HEAD_SIZE:(hd + 1) * HEAD_SIZE] = dv[PLEN:].astype(BF16)

    def gradients(hd, s):
        values = both(hd, 1, s)
        dk = jnp.zeros((all_rows, HEAD_SIZE), F32)
        for c in range(lanes // chunk):
            prob = p_v[s, :, lanes_of(c)]
            gprob = dot(values, stacked(do_v, hd, s, c), NT)
            delta = jnp.sum(prob * gprob, axis=0, keepdims=True)
            gscores = (prob * (gprob - delta)).astype(BF16)
            ds_v[hd, s, :, lanes_of(c)] = gscores
            dk += dot(gscores, stacked(q_v, hd, s, c), NN)
        dk = dk * SCALING
        part[hd, 0][s] = dk[:PLEN]
        gak_v[rows_of(s), hd * HEAD_SIZE:(hd + 1) * HEAD_SIZE] = dk[PLEN:].astype(BF16)

    def row_outputs(hd, s):
        keys_t = both(hd, 0, s).T
        values_t = both(hd, 1, s).T
        for c in range(lanes // chunk):
            out = dot(values_t, w_v[hd, s, :, lanes_of(c)], NN).astype(BF16).T
            dq = (dot(keys_t, ds_v[hd, s, :, lanes_of(c)], NN) * SCALING).astype(BF16).T
            for g, col in enumerate(columns(hd, c)):
                o_v[rows_of(s), col] = out[g * rows:(g + 1) * rows]
                dq_v[rows_of(s), col] = dq[g * rows:(g + 1) * rows]

    def summed(pair, offset):
        total = None
        for s in range(slots):
            pick = jnp.where(relative(s) == offset, 1.0, 0.0).astype(F32)
            term = part[pair][s] * pick
            total = term if total is None else total + term
        return total

    direct, relayed = 4 * core, 4 - 4 * core
    direct_to = lax.rem(me + devices - 2 + 4 * core, devices)
    relay_to = lax.rem(me + devices + 2 - 4 * core, devices)
    b_all, b_sib, b_direct, b_relay, b_x, b_own = {}, {}, {}, {}, {}, {}
    for pair in pairs:
        hd, w = pair
        b_all[pair] = [
            remote(y_out[pair].at[i], y_in[pair].at[i], by_send.at[hd, w, i],
                   by_recv.at[hd, w, i], dp=near[i]) for i in range(len(near))
        ]
        b_sib[pair] = [
            remote(sib_out[pair].at[i], sib_in[pair].at[i], bs_send.at[hd, w, i],
                   bs_recv.at[hd, w, i], dp=sibling) for i in range(2)
        ]
        b_direct[pair] = remote(y_out[pair].at[0], y_in[pair].at[core], by_send.at[hd, w, 0],
                                by_recv.at[hd, w, core], dp=direct_to)
        b_relay[pair] = remote(y_out[pair].at[1], y_in[pair].at[1 - core],
                               by_send.at[hd, w, 1], by_recv.at[hd, w, 1 - core], dp=relay_to)
        dst = (gpk_out, gpv_out)[w]
        cols = pl.ds(pl.multiple_of(h * width + hd * HEAD_SIZE, HEAD_SIZE), HEAD_SIZE)
        b_x[pair] = []
        for p in order:
            to = peers[p - 1]
            theirs = pl.ds(pl.multiple_of(to * span, span), span)
            b_x[pair].append(remote(
                x_out[pair].at[theirs], dst.at[:, cols],
                bx_send.at[hd, w, p - 1], bx_recv.at[hd, w, p - 1], head=to))
        b_own[pair] = pltpu.make_async_copy(
            x_out[pair].at[mine], dst.at[:, cols], bx_own.at[hd, w])

    def back_first(pair):
        if pair == last_back:
            for i, o in enumerate(offsets):
                y_out[pair][i] = summed(pair, MAX_SPREAD + o).astype(BF16)
                b_all[pair][i].start()
            own[pair][...] = summed(pair, MAX_SPREAD)
            return
        for i in range(2):
            sib_out[pair][i] = summed(pair, 1 + 2 * i).astype(BF16)
            b_sib[pair][i].start()
        y_out[pair][0] = summed(pair, direct).astype(BF16)
        b_direct[pair].start()

    def back_relay(pair):
        if pair == last_back:
            return
        carry = summed(pair, relayed)
        own[pair][...] = summed(pair, MAX_SPREAD)
        for c in b_sib[pair]:
            c.wait_recv()
        y_out[pair][1] = (carry + sib_in[pair][1 - core].astype(F32)).astype(BF16)
        b_relay[pair].start()
        own[pair][...] += sib_in[pair][core].astype(F32)

    def back_last(pair):
        came = b_all[pair] if pair == last_back else [b_direct[pair], b_relay[pair]]
        for c in came:
            c.wait_recv()
        total = own[pair][...]
        for i in range(len(came)):
            total = total + y_in[pair][i].astype(F32)
        x_out[pair][...] = total.astype(BF16)
        for c in b_x[pair]:
            c.start()
        b_own[pair].start()

    def each_slot(work, hd, at=()):
        for s in range(slots):
            for when, what, *args in at:
                if when == s:
                    what(*args)
            work(hd, s)

    last = slots - 1
    for hd, w in pairs:
        forward_all(hd, w)
    for load in loads:
        load.wait()
    arrived(0, 0)
    for hd in range(kvh):
        at = []
        if hd == 0:
            at.append((last, relay_in, 0, 1))
        else:
            at.append((1, back_relay, (hd - 1, 0)))
        each_slot(probabilities, hd, at)
        back_first((hd, 1))
        if hd + 1 < kvh:
            relay_in(hd + 1, 0)
        arrived(hd, 1)
        at = [(min(2, last), back_relay, (hd, 1))]
        if hd + 1 < kvh:
            at.append((last, relay_in, hd + 1, 1))
        each_slot(gradients, hd, at)
        back_first((hd, 0))
        if hd + 1 < kvh:
            arrived(hd + 1, 0)

    end = kvh - 1
    for hd in range(kvh):
        at = []
        if hd == 0:
            at += [(1, back_last, pair) for pair in pairs if pair[0] < end]
        if hd == end:
            at += [(0, back_last, (end, 1)), (1, back_last, (end, 0))]
        each_slot(row_outputs, hd, at)

    for pair in pairs:
        hd, w = pair
        for p in order:
            x_in[hd, w, p].wait_send()
        for p in pieces[pair]:
            for c in y_copies[hd, w, p]:
                c.wait_send()
            if pair != first_in:
                s_copies[hd, w, p].wait_send()
                r_copies[hd, w, p].wait_send()
        gone = b_sib[pair] + [b_direct[pair], b_relay[pair]]
        for c in b_all[pair] if pair == last_back else gone:
            c.wait_send()
        for c in b_x[pair]:
            c.wait()
        b_own[pair].wait()


def finish(o, dq, gak, gav, gpk, gpv, o_out, dq_out, gak_out, gav_out, gpk_out, gpv_out,
           wide_k, wide_v, sem):
    copies = [
        pltpu.make_async_copy(src, dst, sem.at[i])
        for i, (src, dst) in enumerate(
            [(o, o_out), (dq, dq_out), (gak, gak_out), (gav, gav_out),
             (wide_k, gpk_out.at[0]), (wide_v, gpv_out.at[0])])
    ]
    for copy in copies[:4]:
        copy.start()
    wide_k[...] = gpk[...].astype(F32)
    copies[4].start()
    wide_v[...] = gpv[...].astype(F32)
    copies[5].start()
    for copy in copies:
        copy.wait()


def on_device(queries, answer_keys, answer_values, prompt_keys, prompt_values,
              output_gradient, prompt_len, response_len, response_prompt):
    devices, heads = lax.axis_size("dp"), lax.axis_size("head")
    slots = response_len.shape[0]
    token_rows, q_width = queries.shape
    rows = token_rows // slots
    width = answer_keys.shape[1]
    kvh = width // HEAD_SIZE
    group = q_width // width
    lanes = group * rows
    span, full = prompt_keys.shape[1:]
    dma = pltpu.SemaphoreType.DMA
    anywhere = pl.BlockSpec(memory_space=pl.ANY)
    hbm = pl.BlockSpec(memory_space=pltpu.HBM)
    vmem = pl.BlockSpec(memory_space=pltpu.VMEM)
    vm, sm = pltpu.VMEM, pltpu.SMEM
    block = (PLEN, HEAD_SIZE)
    wide = vm((token_rows, q_width), BF16)
    narrow = vm((token_rows, width), BF16)
    square = (PLEN + rows, lanes)
    per_pair = [
        vm((REACH,) + block, BF16), vm((slots,) + block, F32),
        vm((2,) + block, BF16), vm((2,) + block, BF16),
        vm((4,) + block, BF16), vm((4,) + block, BF16),
        vm(block, F32), vm(block, BF16),
    ]
    scratch = [
        sm(prompt_len.shape, jnp.int32), sm(response_len.shape, jnp.int32),
        sm(response_prompt.shape, jnp.int32),
        wide, wide, narrow, narrow, vm((slots,) + square, F32),
        vm((kvh, slots) + square, BF16), vm((kvh, slots) + square, BF16),
    ]
    for shape in per_pair:
        scratch += [shape] * (kvh * 2)
    scratch += [
        dma((7,)),
        dma((kvh, 2, heads - 1)), dma((kvh, 2, heads - 1)), dma((kvh, 2)),
        dma((kvh, 2, heads, 4)), dma((kvh, 2, heads, 4)),
        dma((kvh, 2, heads, 2)), dma((kvh, 2, heads, 2)),
        dma((kvh, 2, 2)), dma((kvh, 2, 2)), dma((kvh, 2, 4)), dma((kvh, 2, 4)),
        dma((kvh, 2, heads - 1)), dma((kvh, 2, heads - 1)), dma((kvh, 2)),
    ]
    sds = jax.ShapeDtypeStruct
    rows_out = [
        sds((token_rows, q_width), BF16), sds((token_rows, q_width), BF16),
        sds((token_rows, width), BF16), sds((token_rows, width), BF16),
    ]
    results = pl.pallas_call(
        functools.partial(kernel, (devices, heads, slots, rows, kvh, group)),
        out_shape=rows_out + [sds((span, full), BF16), sds((span, full), BF16)],
        in_specs=[hbm] * 9,
        out_specs=[vmem] * 4 + [anywhere] * 2,
        scratch_shapes=scratch,
        compiler_params=pltpu.CompilerParams(
            collective_id=0, has_side_effects=True, vmem_limit_bytes=48 * 1024 * 1024),
    )(*[pltpu.with_memory_space_constraint(x, pltpu.HBM) for x in (
        prompt_len, response_len, response_prompt, queries, output_gradient,
        answer_keys, answer_values, prompt_keys.reshape(span, full),
        prompt_values.reshape(span, full))])
    return pl.pallas_call(
        finish,
        out_shape=rows_out + [sds((1, span, full), F32), sds((1, span, full), F32)],
        in_specs=[vmem] * 6,
        out_specs=[anywhere] * 6,
        scratch_shapes=[vm((span, full), F32), vm((span, full), F32), dma((6,))],
        compiler_params=pltpu.CompilerParams(vmem_limit_bytes=4 * 1024 * 1024),
    )(*[pltpu.with_memory_space_constraint(x, pltpu.VMEM) for x in results])


def solution(mesh):
    in_specs = (
        P("dp", "head"),
        P("dp", "head"),
        P("dp", "head"),
        P("dp", "head", None),
        P("dp", "head", None),
        P("dp", "head"),
        P(),
        P("dp"),
        P("dp"),
    )
    out_specs = (
        P("dp", "head"),
        P("dp", "head"),
        P("dp", "head"),
        P("dp", "head"),
        P("dp", "head", None),
        P("dp", "head", None),
    )
    return jax.shard_map(
        on_device, mesh=mesh, in_specs=in_specs, out_specs=out_specs, check_vma=False
    )
```

```python
import functools
import math

import jax
import jax.numpy as jnp
from jax import lax
from jax.experimental import pallas as pl
from jax.experimental.pallas import tpu as pltpu
from jax.sharding import PartitionSpec as P

HEAD_SIZE = 128
PLEN = 256
MAX_SPREAD = 2
REACH = 2 * MAX_SPREAD + 1
MESH = pl.DeviceIdType.MESH
SCALING = 1.0 / math.sqrt(HEAD_SIZE)
F32 = jnp.float32
BF16 = jnp.bfloat16


def dot(a, b, dims):
    return lax.dot_general(a, b, (dims, ((), ())), preferred_element_type=F32)


NN = ((1,), (0,))
NT = ((1,), (1,))
TN = ((0,), (0,))


def kernel(sizes, *refs):
    devices, heads, slots, rows, kvh, group = sizes
    pairs = [(hd, w) for hd in range(kvh) for w in range(2)]
    bundles = [[(0, 0)], [(0, 1)]] + [[(hd, 0), (hd, 1)] for hd in range(1, kvh)]
    place = {pair: (b, j) for b, bundle in enumerate(bundles) for j, pair in enumerate(bundle)}
    refs = list(refs)
    (plen_hbm, rlen_hbm, rprompt_hbm, q_hbm, do_hbm, ak_hbm, av_hbm, pk_hbm, pv_hbm,
     o_v, dq_v, gak_v, gav_v, gpk_out, gpv_out,
     plen_ref, rlen_ref, rprompt_ref,
     q_v, do_v, ak_v, av_v, p_v, w_v, ds_v) = refs[:25]
    kv, refs = refs[25:25 + len(bundles)], refs[25 + len(bundles):]
    (part, y_out, y_in, own, x_out) = [
        dict(zip(pairs, refs[i * len(pairs):(i + 1) * len(pairs)])) for i in range(5)
    ]
    (in_sem, x_send, x_recv, x_own, y_send, y_recv,
     by_send, by_recv, bx_send, bx_recv, bx_own) = refs[5 * len(pairs):]

    me = lax.axis_index("dp")
    h = lax.axis_index("head")
    offsets = [-2, 2, -1, 1]
    near = [lax.rem(me + devices + o, devices) for o in offsets]
    span = PLEN // heads
    width = kvh * HEAD_SIZE
    lanes = group * rows
    chunk = min(256, lanes)
    per = chunk // rows
    all_rows = PLEN + rows
    peers = [lax.rem(h + p, heads) for p in range(1, heads)]
    order = [p for p in range(1, heads) if p != heads // 2] + [heads // 2]
    mine = pl.ds(pl.multiple_of(h * span, span), span)

    own_in = {}
    for hd, w in pairs:
        b, j = place[hd, w]
        cols = pl.ds(pl.multiple_of(h * width + hd * HEAD_SIZE, HEAD_SIZE), HEAD_SIZE)
        own_in[hd, w] = pltpu.make_async_copy(
            (pk_hbm, pv_hbm)[w].at[:, cols], kv[b].at[MAX_SPREAD, j, mine], x_own.at[hd, w])
        own_in[hd, w].start()
    loads = [
        pltpu.make_async_copy(src, dst, in_sem.at[i])
        for i, (src, dst) in enumerate(
            [(q_hbm, q_v), (do_hbm, do_v), (ak_hbm, ak_v), (av_hbm, av_v),
             (plen_hbm, plen_ref), (rlen_hbm, rlen_ref), (rprompt_hbm, rprompt_ref)])
    ]
    for load in loads:
        load.start()

    def remote(src, dst, send, recv, **where):
        return pltpu.make_async_remote_copy(
            src_ref=src, dst_ref=dst, send_sem=send, recv_sem=recv,
            device_id=where, device_id_type=MESH)

    barrier = pltpu.get_barrier_semaphore()
    for p in peers:
        pl.semaphore_signal(barrier, inc=1, device_id={"head": p}, device_id_type=MESH)
    for d in near:
        pl.semaphore_signal(barrier, inc=1, device_id={"dp": d}, device_id_type=MESH)
    pl.semaphore_wait(barrier, len(peers) + len(near))

    x_in = {}

    def exchange(hd, w):
        b, j = place[hd, w]
        for p in order:
            to = peers[p - 1]
            cols = pl.ds(pl.multiple_of(to * width + hd * HEAD_SIZE, HEAD_SIZE), HEAD_SIZE)
            x_in[hd, w, p] = remote(
                (pk_hbm, pv_hbm)[w].at[:, cols], kv[b].at[MAX_SPREAD, j, mine],
                x_send.at[hd, w, p - 1], x_recv.at[hd, w, p - 1], head=to)
            x_in[hd, w, p].start()

    y_in_copies = {}

    def forward(b, piece):
        for pair in bundles[b]:
            if piece == 0:
                own_in[pair].wait()
            else:
                x_in[(*pair, piece)].wait_recv()
        source = lax.rem(h + heads - piece, heads)
        at = pl.ds(pl.multiple_of(source * span, span), span)
        for i, o in enumerate(offsets):
            copy = remote(
                kv[b].at[MAX_SPREAD, :, at], kv[b].at[MAX_SPREAD - o, :, at],
                y_send.at[b, piece, i], y_recv.at[b, piece, i], dp=near[i])
            y_in_copies[b, piece, i] = copy
            copy.start()

    def arrived(b):
        for piece in range(heads):
            for i in range(len(near)):
                y_in_copies[b, piece, i].wait_recv()

    exchange(*pairs[0])
    forward(0, 0)
    for pair in pairs[1:]:
        exchange(*pair)
    for b in range(1, len(bundles)):
        forward(b, 0)
    for b in range(len(bundles)):
        for p in order:
            forward(b, p)
    for load in loads:
        load.wait()

    def rows_of(s):
        return slice(s * rows, (s + 1) * rows)

    def columns(hd, c):
        first = hd * group + c * per
        return [slice((first + g) * HEAD_SIZE, (first + g + 1) * HEAD_SIZE) for g in range(per)]

    def stacked(ref, hd, s, c):
        return jnp.concatenate([ref[rows_of(s), col] for col in columns(hd, c)], axis=0)

    def relative(s):
        return lax.rem(rprompt_ref[s] - me + (devices + MAX_SPREAD), devices)

    def both(hd, w, s):
        rel = jnp.minimum(relative(s), REACH - 1)
        tail = (ak_v, av_v)[w][rows_of(s), hd * HEAD_SIZE:(hd + 1) * HEAD_SIZE]
        b, j = place[hd, w]
        return jnp.concatenate([kv[b][rel, j], tail], axis=0)

    def lanes_of(c):
        return slice(c * chunk, (c + 1) * chunk)

    def probabilities(hd, s):
        psize = plen_ref[rprompt_ref[s]]
        rlen = rlen_ref[s]
        keys = both(hd, 0, s)
        live = ((lax.broadcasted_iota(jnp.int32, (1, chunk), 1) & (rows - 1)) < rlen).astype(F32)
        head_seen = lax.broadcasted_iota(jnp.int32, (PLEN, chunk), 0) < psize
        tail_seen = lax.broadcasted_iota(jnp.int32, (rows, chunk), 0) <= (
            lax.broadcasted_iota(jnp.int32, (rows, chunk), 1) & (rows - 1))
        dv = jnp.zeros((all_rows, HEAD_SIZE), F32)
        for c in range(lanes // chunk):
            scores = dot(keys, stacked(q_v, hd, s, c), NT)
            masked = jnp.concatenate([
                jnp.where(head_seen, scores[:PLEN], -jnp.inf),
                jnp.where(tail_seen, scores[PLEN:], -jnp.inf)], axis=0)
            top = jnp.max(masked, axis=0, keepdims=True)
            e = jnp.exp2((masked - top) * (SCALING * math.log2(math.e)))
            prob = e * (live / jnp.sum(e, axis=0, keepdims=True))
            p_v[s, :, lanes_of(c)] = prob
            weights = prob.astype(BF16)
            w_v[hd, s, :, lanes_of(c)] = weights
            dv += dot(weights, stacked(do_v, hd, s, c), NN)
        part[hd, 1][s] = dv[:PLEN]
        gav_v[rows_of(s), hd * HEAD_SIZE:(hd + 1) * HEAD_SIZE] = dv[PLEN:].astype(BF16)

    def gradients(hd, s):
        values = both(hd, 1, s)
        dk = jnp.zeros((all_rows, HEAD_SIZE), F32)
        for c in range(lanes // chunk):
            prob = p_v[s, :, lanes_of(c)]
            gprob = dot(values, stacked(do_v, hd, s, c), NT)
            delta = jnp.sum(prob * gprob, axis=0, keepdims=True)
            gscores = (prob * (gprob - delta)).astype(BF16)
            ds_v[hd, s, :, lanes_of(c)] = gscores
            dk += dot(gscores, stacked(q_v, hd, s, c), NN)
        dk = dk * SCALING
        part[hd, 0][s] = dk[:PLEN]
        gak_v[rows_of(s), hd * HEAD_SIZE:(hd + 1) * HEAD_SIZE] = dk[PLEN:].astype(BF16)

    def row_outputs(hd, s):
        keys_t = both(hd, 0, s).T
        values_t = both(hd, 1, s).T
        for c in range(lanes // chunk):
            out = dot(values_t, w_v[hd, s, :, lanes_of(c)], NN).astype(BF16).T
            dq = (dot(keys_t, ds_v[hd, s, :, lanes_of(c)], NN) * SCALING).astype(BF16).T
            for g, col in enumerate(columns(hd, c)):
                o_v[rows_of(s), col] = out[g * rows:(g + 1) * rows]
                dq_v[rows_of(s), col] = dq[g * rows:(g + 1) * rows]

    def summed(pair, offset):
        total = None
        for s in range(slots):
            pick = jnp.where(relative(s) == offset, 1.0, 0.0).astype(F32)
            term = part[pair][s] * pick
            total = term if total is None else total + term
        return total

    back_y, back_x, back_own = {}, {}, {}
    for hd, w in pairs:
        pair = hd, w
        back_y[pair] = [
            remote(y_out[pair].at[i], y_in[pair].at[i], by_send.at[hd, w, i],
                   by_recv.at[hd, w, i], dp=near[i]) for i in range(len(near))
        ]
        dst = (gpk_out, gpv_out)[w]
        cols = pl.ds(pl.multiple_of(h * width + hd * HEAD_SIZE, HEAD_SIZE), HEAD_SIZE)
        back_x[pair] = []
        for p in order:
            to = peers[p - 1]
            theirs = pl.ds(pl.multiple_of(to * span, span), span)
            back_x[pair].append(remote(
                x_out[pair].at[theirs], dst.at[:, cols],
                bx_send.at[hd, w, p - 1], bx_recv.at[hd, w, p - 1], head=to))
        back_own[pair] = pltpu.make_async_copy(
            x_out[pair].at[mine], dst.at[:, cols], bx_own.at[hd, w])

    def send_back(pair):
        for i, o in enumerate(offsets):
            y_out[pair][i] = summed(pair, MAX_SPREAD + o).astype(BF16)
            back_y[pair][i].start()
        own[pair][...] = summed(pair, MAX_SPREAD)

    def take_back(pair):
        total = own[pair][...]
        for i, copy in enumerate(back_y[pair]):
            copy.wait_recv()
            total = total + y_in[pair][i].astype(F32)
        x_out[pair][...] = total.astype(BF16)
        for copy in back_x[pair]:
            copy.start()
        back_own[pair].start()

    def each_slot(work, hd, at={}):
        for s in range(slots):
            work(hd, s)
            for pair in at.get(s, ()):
                take_back(pair)

    for hd in range(kvh):
        if hd == 0:
            arrived(0)
        else:
            arrived(hd + 1)
        each_slot(probabilities, hd)
        send_back((hd, 1))
        if hd == 0:
            arrived(1)
        each_slot(gradients, hd)
        send_back((hd, 0))

    end = kvh - 1
    for hd in range(kvh):
        if hd < end:
            each_slot(row_outputs, hd, {slots - 1: [(hd, 1), (hd, 0)]})
        else:
            each_slot(row_outputs, hd, {0: [(end, 1)], slots // 2: [(end, 0)]})

    for pair in pairs:
        for p in order:
            x_in[(*pair, p)].wait_send()
        for copy in back_y[pair]:
            copy.wait_send()
        for copy in back_x[pair]:
            copy.wait()
        back_own[pair].wait()
    for copy in y_in_copies.values():
        copy.wait_send()


def finish(o, dq, gak, gav, gpk, gpv, o_out, dq_out, gak_out, gav_out, gpk_out, gpv_out,
           wide_k, wide_v, sem):
    copies = [
        pltpu.make_async_copy(src, dst, sem.at[i])
        for i, (src, dst) in enumerate(
            [(o, o_out), (dq, dq_out), (gak, gak_out), (gav, gav_out),
             (wide_k, gpk_out.at[0]), (wide_v, gpv_out.at[0])])
    ]
    for copy in copies[:4]:
        copy.start()
    wide_k[...] = gpk[...].astype(F32)
    copies[4].start()
    wide_v[...] = gpv[...].astype(F32)
    copies[5].start()
    for copy in copies:
        copy.wait()


def on_device(queries, answer_keys, answer_values, prompt_keys, prompt_values,
              output_gradient, prompt_len, response_len, response_prompt):
    devices, heads = lax.axis_size("dp"), lax.axis_size("head")
    slots = response_len.shape[0]
    token_rows, q_width = queries.shape
    rows = token_rows // slots
    width = answer_keys.shape[1]
    kvh = width // HEAD_SIZE
    group = q_width // width
    lanes = group * rows
    span, full = prompt_keys.shape[1:]
    dma = pltpu.SemaphoreType.DMA
    anywhere = pl.BlockSpec(memory_space=pl.ANY)
    hbm = pl.BlockSpec(memory_space=pltpu.HBM)
    vmem = pl.BlockSpec(memory_space=pltpu.VMEM)
    vm, sm = pltpu.VMEM, pltpu.SMEM
    block = (PLEN, HEAD_SIZE)
    wide = vm((token_rows, q_width), BF16)
    narrow = vm((token_rows, width), BF16)
    square = (PLEN + rows, lanes)
    bundle = [1, 1] + [2] * (kvh - 1)
    scratch = [
        sm(prompt_len.shape, jnp.int32), sm(response_len.shape, jnp.int32),
        sm(response_prompt.shape, jnp.int32),
        wide, wide, narrow, narrow, vm((slots,) + square, F32),
        vm((kvh, slots) + square, BF16), vm((kvh, slots) + square, BF16),
    ]
    scratch += [vm((REACH, count) + block, BF16) for count in bundle]
    for shape in [vm((slots,) + block, F32), vm((REACH - 1,) + block, BF16),
                  vm((REACH - 1,) + block, BF16), vm(block, F32), vm(block, BF16)]:
        scratch += [shape] * (kvh * 2)
    scratch += [
        dma((7,)),
        dma((kvh, 2, heads - 1)), dma((kvh, 2, heads - 1)), dma((kvh, 2)),
        dma((kvh + 1, heads, REACH - 1)), dma((kvh + 1, heads, REACH - 1)),
        dma((kvh, 2, REACH - 1)), dma((kvh, 2, REACH - 1)),
        dma((kvh, 2, heads - 1)), dma((kvh, 2, heads - 1)), dma((kvh, 2)),
    ]
    sds = jax.ShapeDtypeStruct
    rows_out = [
        sds((token_rows, q_width), BF16), sds((token_rows, q_width), BF16),
        sds((token_rows, width), BF16), sds((token_rows, width), BF16),
    ]
    results = pl.pallas_call(
        functools.partial(kernel, (devices, heads, slots, rows, kvh, group)),
        out_shape=rows_out + [sds((span, full), BF16), sds((span, full), BF16)],
        in_specs=[hbm] * 9,
        out_specs=[vmem] * 4 + [anywhere] * 2,
        scratch_shapes=scratch,
        compiler_params=pltpu.CompilerParams(
            collective_id=0, has_side_effects=True, vmem_limit_bytes=48 * 1024 * 1024),
    )(*[pltpu.with_memory_space_constraint(x, pltpu.HBM) for x in (
        prompt_len, response_len, response_prompt, queries, output_gradient,
        answer_keys, answer_values, prompt_keys.reshape(span, full),
        prompt_values.reshape(span, full))])
    return pl.pallas_call(
        finish,
        out_shape=rows_out + [sds((1, span, full), F32), sds((1, span, full), F32)],
        in_specs=[vmem] * 6,
        out_specs=[anywhere] * 6,
        scratch_shapes=[vm((span, full), F32), vm((span, full), F32), dma((6,))],
        compiler_params=pltpu.CompilerParams(vmem_limit_bytes=4 * 1024 * 1024),
    )(*[pltpu.with_memory_space_constraint(x, pltpu.VMEM) for x in results])


def solution(mesh):
    in_specs = (
        P("dp", "head"),
        P("dp", "head"),
        P("dp", "head"),
        P("dp", "head", None),
        P("dp", "head", None),
        P("dp", "head"),
        P(),
        P("dp"),
        P("dp"),
    )
    out_specs = (
        P("dp", "head"),
        P("dp", "head"),
        P("dp", "head"),
        P("dp", "head"),
        P("dp", "head", None),
        P("dp", "head", None),
    )
    return jax.shard_map(
        on_device, mesh=mesh, in_specs=in_specs, out_specs=out_specs, check_vma=False
    )
```

```python
import functools
import math

import jax
import jax.numpy as jnp
from jax import lax
from jax.experimental import pallas as pl
from jax.experimental.pallas import tpu as pltpu
from jax.sharding import PartitionSpec as P

HEAD_SIZE = 128
PLEN = 256
MAX_SPREAD = 2
REACH = 2 * MAX_SPREAD + 1
MESH = pl.DeviceIdType.MESH
SCALING = 1.0 / math.sqrt(HEAD_SIZE)
F32 = jnp.float32
BF16 = jnp.bfloat16


def dot(a, b, dims):
    return lax.dot_general(a, b, (dims, ((), ())), preferred_element_type=F32)


NN = ((1,), (0,))
NT = ((1,), (1,))
TN = ((0,), (0,))


def kernel(sizes, *refs):
    devices, heads, slots, rows, kvh, group = sizes
    pairs = [(hd, w) for hd in range(kvh) for w in range(2)]
    bundles = [[(0, 0)], [(0, 1)]] + [[(hd, 0), (hd, 1)] for hd in range(1, kvh)]
    place = {pair: (b, j) for b, bundle in enumerate(bundles) for j, pair in enumerate(bundle)}
    refs = list(refs)
    (plen_hbm, rlen_hbm, rprompt_hbm, q_hbm, do_hbm, ak_hbm, av_hbm, pk_hbm, pv_hbm,
     o_v, dq_v, gak_v, gav_v, gpk_out, gpv_out,
     plen_ref, rlen_ref, rprompt_ref,
     q_v, do_v, ak_v, av_v, p_v, w_v, ds_v, pk_v, pv_v) = refs[:27]
    kv, refs = refs[27:27 + len(bundles)], refs[27 + len(bundles):]
    (part, y_out, y_in, own, x_out) = [
        dict(zip(pairs, refs[i * len(pairs):(i + 1) * len(pairs)])) for i in range(5)
    ]
    (in_sem, x_send, x_recv, x_own, y_send, y_recv,
     by_send, by_recv, bx_send, bx_recv, bx_own) = refs[5 * len(pairs):]

    me = lax.axis_index("dp")
    h = lax.axis_index("head")
    offsets = [-2, 2, -1, 1]
    near = [lax.rem(me + devices + o, devices) for o in offsets]
    span = PLEN // heads
    width = kvh * HEAD_SIZE
    lanes = group * rows
    chunk = min(512, lanes)
    per = chunk // rows
    all_rows = PLEN + rows
    peers = [lax.rem(h + p, heads) for p in range(1, heads)]
    order = [p for p in range(1, heads) if p != heads // 2] + [heads // 2]
    mine = pl.ds(pl.multiple_of(h * span, span), span)

    prompt_loads = [
        pltpu.make_async_copy(src, dst, x_own.at[i])
        for i, (src, dst) in enumerate([(pk_hbm, pk_v), (pv_hbm, pv_v)])
    ]
    loads = [
        pltpu.make_async_copy(src, dst, in_sem.at[i])
        for i, (src, dst) in enumerate(
            [(q_hbm, q_v), (do_hbm, do_v), (ak_hbm, ak_v), (av_hbm, av_v),
             (plen_hbm, plen_ref), (rlen_hbm, rlen_ref), (rprompt_hbm, rprompt_ref)])
    ]
    for load in prompt_loads + loads:
        load.start()

    def remote(src, dst, send, recv, **where):
        return pltpu.make_async_remote_copy(
            src_ref=src, dst_ref=dst, send_sem=send, recv_sem=recv,
            device_id=where, device_id_type=MESH)

    barrier = pltpu.get_barrier_semaphore()
    for p in peers:
        pl.semaphore_signal(barrier, inc=1, device_id={"head": p}, device_id_type=MESH)
    for d in near:
        pl.semaphore_signal(barrier, inc=1, device_id={"dp": d}, device_id_type=MESH)
    for load in prompt_loads:
        load.wait()
    for hd, w in pairs:
        b, j = place[hd, w]
        cols = pl.ds(pl.multiple_of(h * width + hd * HEAD_SIZE, HEAD_SIZE), HEAD_SIZE)
        kv[b][MAX_SPREAD, j, mine] = (pk_v, pv_v)[w][:, cols]
    pl.semaphore_wait(barrier, len(peers) + len(near))

    x_in = {}

    def exchange(hd, w):
        b, j = place[hd, w]
        for p in order:
            to = peers[p - 1]
            cols = pl.ds(pl.multiple_of(to * width + hd * HEAD_SIZE, HEAD_SIZE), HEAD_SIZE)
            x_in[hd, w, p] = remote(
                (pk_v, pv_v)[w].at[:, cols], kv[b].at[MAX_SPREAD, j, mine],
                x_send.at[hd, w, p - 1], x_recv.at[hd, w, p - 1], head=to)
            x_in[hd, w, p].start()

    y_in_copies = {}

    def forward(b, piece):
        if piece > 0:
            for pair in bundles[b]:
                x_in[(*pair, piece)].wait_recv()
        source = lax.rem(h + heads - piece, heads)
        at = pl.ds(pl.multiple_of(source * span, span), span)
        for i, o in enumerate(offsets):
            copy = remote(
                kv[b].at[MAX_SPREAD, :, at], kv[b].at[MAX_SPREAD - o, :, at],
                y_send.at[b, piece, i], y_recv.at[b, piece, i], dp=near[i])
            y_in_copies[b, piece, i] = copy
            copy.start()

    def arrived(b):
        for piece in range(heads):
            for i in range(len(near)):
                y_in_copies[b, piece, i].wait_recv()

    exchange(*pairs[0])
    forward(0, 0)
    for pair in pairs[1:]:
        exchange(*pair)
    for b in range(1, len(bundles)):
        forward(b, 0)
    for b in range(len(bundles)):
        for p in order:
            forward(b, p)
    for load in loads:
        load.wait()

    def rows_of(s):
        return slice(s * rows, (s + 1) * rows)

    def columns(hd, c):
        first = hd * group + c * per
        return [slice((first + g) * HEAD_SIZE, (first + g + 1) * HEAD_SIZE) for g in range(per)]

    def stacked(ref, hd, s, c):
        return jnp.concatenate([ref[rows_of(s), col] for col in columns(hd, c)], axis=0)

    def relative(s):
        return lax.rem(rprompt_ref[s] - me + (devices + MAX_SPREAD), devices)

    def both(hd, w, s):
        rel = jnp.minimum(relative(s), REACH - 1)
        tail = (ak_v, av_v)[w][rows_of(s), hd * HEAD_SIZE:(hd + 1) * HEAD_SIZE]
        b, j = place[hd, w]
        return jnp.concatenate([kv[b][rel, j], tail], axis=0)

    def lanes_of(c):
        return slice(c * chunk, (c + 1) * chunk)

    def probabilities(hd, s):
        psize = plen_ref[rprompt_ref[s]]
        rlen = rlen_ref[s]
        keys = both(hd, 0, s)
        live = ((lax.broadcasted_iota(jnp.int32, (1, chunk), 1) & (rows - 1)) < rlen).astype(F32)
        head_seen = lax.broadcasted_iota(jnp.int32, (PLEN, chunk), 0) < psize
        tail_seen = lax.broadcasted_iota(jnp.int32, (rows, chunk), 0) <= (
            lax.broadcasted_iota(jnp.int32, (rows, chunk), 1) & (rows - 1))
        dv = jnp.zeros((all_rows, HEAD_SIZE), F32)
        for c in range(lanes // chunk):
            scores = dot(keys, stacked(q_v, hd, s, c), NT)
            masked = jnp.concatenate([
                jnp.where(head_seen, scores[:PLEN], -jnp.inf),
                jnp.where(tail_seen, scores[PLEN:], -jnp.inf)], axis=0)
            top = jnp.max(masked, axis=0, keepdims=True)
            e = jnp.exp2((masked - top) * (SCALING * math.log2(math.e)))
            prob = e * (live / jnp.sum(e, axis=0, keepdims=True))
            p_v[s, :, lanes_of(c)] = prob
            weights = prob.astype(BF16)
            w_v[hd, s, :, lanes_of(c)] = weights
            dv += dot(weights, stacked(do_v, hd, s, c), NN)
        part[hd, 1][s] = dv[:PLEN]
        gav_v[rows_of(s), hd * HEAD_SIZE:(hd + 1) * HEAD_SIZE] = dv[PLEN:].astype(BF16)

    def gradients(hd, s):
        values = both(hd, 1, s)
        dk = jnp.zeros((all_rows, HEAD_SIZE), F32)
        for c in range(lanes // chunk):
            prob = p_v[s, :, lanes_of(c)]
            gprob = dot(values, stacked(do_v, hd, s, c), NT)
            delta = jnp.sum(prob * gprob, axis=0, keepdims=True)
            gscores = (prob * (gprob - delta)).astype(BF16)
            ds_v[hd, s, :, lanes_of(c)] = gscores
            dk += dot(gscores, stacked(q_v, hd, s, c), NN)
        dk = dk * SCALING
        part[hd, 0][s] = dk[:PLEN]
        gak_v[rows_of(s), hd * HEAD_SIZE:(hd + 1) * HEAD_SIZE] = dk[PLEN:].astype(BF16)

    def row_outputs(hd, s):
        keys_t = both(hd, 0, s).T
        values_t = both(hd, 1, s).T
        for c in range(lanes // chunk):
            out = dot(values_t, w_v[hd, s, :, lanes_of(c)], NN).astype(BF16).T
            dq = (dot(keys_t, ds_v[hd, s, :, lanes_of(c)], NN) * SCALING).astype(BF16).T
            for g, col in enumerate(columns(hd, c)):
                o_v[rows_of(s), col] = out[g * rows:(g + 1) * rows]
                dq_v[rows_of(s), col] = dq[g * rows:(g + 1) * rows]

    def summed(pair, offset):
        total = None
        for s in range(slots):
            pick = jnp.where(relative(s) == offset, 1.0, 0.0).astype(F32)
            term = part[pair][s] * pick
            total = term if total is None else total + term
        return total

    back_y, back_x, back_own = {}, {}, {}
    for hd, w in pairs:
        pair = hd, w
        back_y[pair] = [
            remote(y_out[pair].at[i], y_in[pair].at[i], by_send.at[hd, w, i],
                   by_recv.at[hd, w, i], dp=near[i]) for i in range(len(near))
        ]
        dst = (gpk_out, gpv_out)[w]
        cols = pl.ds(pl.multiple_of(h * width + hd * HEAD_SIZE, HEAD_SIZE), HEAD_SIZE)
        back_x[pair] = []
        for p in order:
            to = peers[p - 1]
            theirs = pl.ds(pl.multiple_of(to * span, span), span)
            back_x[pair].append(remote(
                x_out[pair].at[theirs], dst.at[:, cols],
                bx_send.at[hd, w, p - 1], bx_recv.at[hd, w, p - 1], head=to))
        back_own[pair] = pltpu.make_async_copy(
            x_out[pair].at[mine], dst.at[:, cols], bx_own.at[hd, w])

    def send_back(pair):
        for i, o in enumerate(offsets):
            y_out[pair][i] = summed(pair, MAX_SPREAD + o).astype(BF16)
            back_y[pair][i].start()
        own[pair][...] = summed(pair, MAX_SPREAD)

    def take_back(pair):
        for copy in back_y[pair]:
            copy.wait_recv()
        for p, copy in zip(order + [0], back_x[pair] + [back_own[pair]]):
            at = pl.ds(pl.multiple_of(lax.rem(h + p, heads) * span, span), span)
            total = own[pair][at]
            for i in range(len(near)):
                total = total + y_in[pair][i, at].astype(F32)
            x_out[pair][at] = total.astype(BF16)
            copy.start()

    def each_slot(work, hd, at={}):
        for s in range(slots):
            work(hd, s)
            for pair in at.get(s, ()):
                take_back(pair)

    for hd in range(kvh):
        if hd == 0:
            arrived(0)
        else:
            arrived(hd + 1)
        each_slot(probabilities, hd)
        send_back((hd, 1))
        if hd == 0:
            arrived(1)
        each_slot(gradients, hd)
        send_back((hd, 0))

    end = kvh - 1
    for hd in range(kvh):
        if hd < end:
            each_slot(row_outputs, hd, {slots - 1: [(hd, 1), (hd, 0)]})
        else:
            each_slot(row_outputs, hd, {0: [(end, 1)], slots // 2: [(end, 0)]})

    for pair in pairs:
        for p in order:
            x_in[(*pair, p)].wait_send()
        for copy in back_y[pair]:
            copy.wait_send()
        for copy in back_x[pair]:
            copy.wait()
        back_own[pair].wait()
    for copy in y_in_copies.values():
        copy.wait_send()


def finish(o, dq, gak, gav, gpk, gpv, o_out, dq_out, gak_out, gav_out, gpk_out, gpv_out,
           wide_k, wide_v, sem):
    copies = [
        pltpu.make_async_copy(src, dst, sem.at[i])
        for i, (src, dst) in enumerate(
            [(o, o_out), (dq, dq_out), (gak, gak_out), (gav, gav_out),
             (wide_k, gpk_out.at[0]), (wide_v, gpv_out.at[0])])
    ]
    for copy in copies[:4]:
        copy.start()
    wide_k[...] = gpk[...].astype(F32)
    copies[4].start()
    wide_v[...] = gpv[...].astype(F32)
    copies[5].start()
    for copy in copies:
        copy.wait()


def on_device(queries, answer_keys, answer_values, prompt_keys, prompt_values,
              output_gradient, prompt_len, response_len, response_prompt):
    devices, heads = lax.axis_size("dp"), lax.axis_size("head")
    slots = response_len.shape[0]
    token_rows, q_width = queries.shape
    rows = token_rows // slots
    width = answer_keys.shape[1]
    kvh = width // HEAD_SIZE
    group = q_width // width
    lanes = group * rows
    span, full = prompt_keys.shape[1:]
    dma = pltpu.SemaphoreType.DMA
    anywhere = pl.BlockSpec(memory_space=pl.ANY)
    hbm = pl.BlockSpec(memory_space=pltpu.HBM)
    vmem = pl.BlockSpec(memory_space=pltpu.VMEM)
    vm, sm = pltpu.VMEM, pltpu.SMEM
    block = (PLEN, HEAD_SIZE)
    wide = vm((token_rows, q_width), BF16)
    narrow = vm((token_rows, width), BF16)
    square = (PLEN + rows, lanes)
    bundle = [1, 1] + [2] * (kvh - 1)
    scratch = [
        sm(prompt_len.shape, jnp.int32), sm(response_len.shape, jnp.int32),
        sm(response_prompt.shape, jnp.int32),
        wide, wide, narrow, narrow, vm((slots,) + square, F32),
        vm((kvh, slots) + square, BF16), vm((kvh, slots) + square, BF16),
        vm((span, full), BF16), vm((span, full), BF16),
    ]
    scratch += [vm((REACH, count) + block, BF16) for count in bundle]
    for shape in [vm((slots,) + block, F32), vm((REACH - 1,) + block, BF16),
                  vm((REACH - 1,) + block, BF16), vm(block, F32), vm(block, BF16)]:
        scratch += [shape] * (kvh * 2)
    scratch += [
        dma((7,)),
        dma((kvh, 2, heads - 1)), dma((kvh, 2, heads - 1)), dma((2,)),
        dma((kvh + 1, heads, REACH - 1)), dma((kvh + 1, heads, REACH - 1)),
        dma((kvh, 2, REACH - 1)), dma((kvh, 2, REACH - 1)),
        dma((kvh, 2, heads - 1)), dma((kvh, 2, heads - 1)), dma((kvh, 2)),
    ]
    sds = jax.ShapeDtypeStruct
    rows_out = [
        sds((token_rows, q_width), BF16), sds((token_rows, q_width), BF16),
        sds((token_rows, width), BF16), sds((token_rows, width), BF16),
    ]
    results = pl.pallas_call(
        functools.partial(kernel, (devices, heads, slots, rows, kvh, group)),
        out_shape=rows_out + [sds((span, full), BF16), sds((span, full), BF16)],
        in_specs=[hbm] * 9,
        out_specs=[vmem] * 4 + [anywhere] * 2,
        scratch_shapes=scratch,
        compiler_params=pltpu.CompilerParams(
            collective_id=0, has_side_effects=True, vmem_limit_bytes=48 * 1024 * 1024),
    )(*[pltpu.with_memory_space_constraint(x, pltpu.HBM) for x in (
        prompt_len, response_len, response_prompt, queries, output_gradient,
        answer_keys, answer_values, prompt_keys.reshape(span, full),
        prompt_values.reshape(span, full))])
    return pl.pallas_call(
        finish,
        out_shape=rows_out + [sds((1, span, full), F32), sds((1, span, full), F32)],
        in_specs=[vmem] * 6,
        out_specs=[anywhere] * 6,
        scratch_shapes=[vm((span, full), F32), vm((span, full), F32), dma((6,))],
        compiler_params=pltpu.CompilerParams(vmem_limit_bytes=4 * 1024 * 1024),
    )(*[pltpu.with_memory_space_constraint(x, pltpu.VMEM) for x in results])


def solution(mesh):
    in_specs = (
        P("dp", "head"),
        P("dp", "head"),
        P("dp", "head"),
        P("dp", "head", None),
        P("dp", "head", None),
        P("dp", "head"),
        P(),
        P("dp"),
        P("dp"),
    )
    out_specs = (
        P("dp", "head"),
        P("dp", "head"),
        P("dp", "head"),
        P("dp", "head"),
        P("dp", "head", None),
        P("dp", "head", None),
    )
    return jax.shard_map(
        on_device, mesh=mesh, in_specs=in_specs, out_specs=out_specs, check_vma=False
    )
```

```python
import functools
import math

import jax
import jax.numpy as jnp
from jax import lax
from jax.experimental import pallas as pl
from jax.experimental.pallas import tpu as pltpu
from jax.sharding import PartitionSpec as P

HEAD_SIZE = 128
PLEN = 256
MAX_SPREAD = 2
REACH = 2 * MAX_SPREAD + 1
MESH = pl.DeviceIdType.MESH
SCALING = 1.0 / math.sqrt(HEAD_SIZE)
F32 = jnp.float32
BF16 = jnp.bfloat16


def dot(a, b, dims):
    return lax.dot_general(a, b, (dims, ((), ())), preferred_element_type=F32)


NN = ((1,), (0,))
NT = ((1,), (1,))
TN = ((0,), (0,))


def kernel(sizes, *refs):
    devices, heads, slots, rows, kvh, group = sizes
    pairs = [(hd, w) for hd in range(kvh) for w in range(2)]
    bundles = [[(0, 0)], [(0, 1)]] + [[(hd, 0), (hd, 1)] for hd in range(1, kvh)]
    place = {pair: (b, j) for b, bundle in enumerate(bundles) for j, pair in enumerate(bundle)}
    refs = list(refs)
    (plen_hbm, rlen_hbm, rprompt_hbm, q_hbm, do_hbm, ak_hbm, av_hbm, pk_hbm, pv_hbm,
     o_v, dq_v, gak_v, gav_v, gpk_out, gpv_out,
     plen_ref, rlen_ref, rprompt_ref,
     q_v, do_v, ak_v, av_v, p_v, w_v, ds_v, pk_v, pv_v, st_v, gt_v) = refs[:29]
    kv, refs = refs[29:29 + len(bundles)], refs[29 + len(bundles):]
    (part, y_out, y_in, own, x_out) = [
        dict(zip(pairs, refs[i * len(pairs):(i + 1) * len(pairs)])) for i in range(5)
    ]
    (in_sem, x_send, x_recv, x_own, y_send, y_recv,
     by_send, by_recv, bx_send, bx_recv, bx_own, bl_send, bl_recv) = refs[5 * len(pairs):]

    me = lax.axis_index("dp")
    h = lax.axis_index("head")
    offsets = [-2, 2, -1, 1]
    near = [lax.rem(me + devices + o, devices) for o in offsets]
    span = PLEN // heads
    width = kvh * HEAD_SIZE
    lanes = group * rows
    peers = [lax.rem(h + p, heads) for p in range(1, heads)]
    order = [p for p in range(1, heads) if p != heads // 2] + [heads // 2]
    mine = pl.ds(pl.multiple_of(h * span, span), span)

    prompt_loads = [
        pltpu.make_async_copy(src, dst, x_own.at[i])
        for i, (src, dst) in enumerate([(pk_hbm, pk_v), (pv_hbm, pv_v)])
    ]
    loads = [
        pltpu.make_async_copy(src, dst, in_sem.at[i])
        for i, (src, dst) in enumerate(
            [(q_hbm, q_v), (do_hbm, do_v), (ak_hbm, ak_v), (av_hbm, av_v),
             (plen_hbm, plen_ref), (rlen_hbm, rlen_ref), (rprompt_hbm, rprompt_ref)])
    ]
    for load in prompt_loads + loads:
        load.start()

    def remote(src, dst, send, recv, **where):
        return pltpu.make_async_remote_copy(
            src_ref=src, dst_ref=dst, send_sem=send, recv_sem=recv,
            device_id=where, device_id_type=MESH)

    barrier = pltpu.get_barrier_semaphore()
    for p in peers:
        pl.semaphore_signal(barrier, inc=1, device_id={"head": p}, device_id_type=MESH)
    for d in near:
        pl.semaphore_signal(barrier, inc=1, device_id={"dp": d}, device_id_type=MESH)
    for load in prompt_loads:
        load.wait()
    for hd, w in pairs:
        b, j = place[hd, w]
        cols = pl.ds(pl.multiple_of(h * width + hd * HEAD_SIZE, HEAD_SIZE), HEAD_SIZE)
        kv[b][MAX_SPREAD, j, mine] = (pk_v, pv_v)[w][:, cols]
    pl.semaphore_wait(barrier, len(peers) + len(near))

    x_in = {}

    def exchange(hd, w):
        b, j = place[hd, w]
        for p in order:
            to = peers[p - 1]
            cols = pl.ds(pl.multiple_of(to * width + hd * HEAD_SIZE, HEAD_SIZE), HEAD_SIZE)
            x_in[hd, w, p] = remote(
                (pk_v, pv_v)[w].at[:, cols], kv[b].at[MAX_SPREAD, j, mine],
                x_send.at[hd, w, p - 1], x_recv.at[hd, w, p - 1], head=to)
            x_in[hd, w, p].start()

    y_in_copies = {}

    def forward(b, piece):
        if piece > 0:
            for pair in bundles[b]:
                x_in[(*pair, piece)].wait_recv()
        source = lax.rem(h + heads - piece, heads)
        at = pl.ds(pl.multiple_of(source * span, span), span)
        for i, o in enumerate(offsets):
            copy = remote(
                kv[b].at[MAX_SPREAD, :, at], kv[b].at[MAX_SPREAD - o, :, at],
                y_send.at[b, piece, i], y_recv.at[b, piece, i], dp=near[i])
            y_in_copies[b, piece, i] = copy
            copy.start()

    def arrived(b):
        for piece in range(heads):
            for i in range(len(near)):
                y_in_copies[b, piece, i].wait_recv()

    def rows_of(s):
        return slice(s * rows, (s + 1) * rows)

    def columns(hd):
        first = hd * group
        return [slice((first + g) * HEAD_SIZE, (first + g + 1) * HEAD_SIZE) for g in range(group)]

    def stacked(ref, hd, s):
        return jnp.concatenate([ref[rows_of(s), col] for col in columns(hd)], axis=0)

    def relative(s):
        return lax.rem(rprompt_ref[s] - me + (devices + MAX_SPREAD), devices)

    def prompt_part(hd, w, s):
        b, j = place[hd, w]
        return kv[b][jnp.minimum(relative(s), REACH - 1), j]

    def answer_part(hd, w, s):
        return (ak_v, av_v)[w][rows_of(s), hd * HEAD_SIZE:(hd + 1) * HEAD_SIZE]

    def answer_scores(hd, s):
        seen = lax.broadcasted_iota(jnp.int32, (rows, lanes), 0) <= (
            lax.broadcasted_iota(jnp.int32, (rows, lanes), 1) & (rows - 1))
        scores = dot(answer_part(hd, 0, s), stacked(q_v, hd, s), NT)
        st_v[hd, s] = jnp.where(seen, scores, -jnp.inf)
        gt_v[hd, s] = dot(answer_part(hd, 1, s), stacked(do_v, hd, s), NT)

    def probabilities(hd, s):
        psize = plen_ref[rprompt_ref[s]]
        rlen = rlen_ref[s]
        live = ((lax.broadcasted_iota(jnp.int32, (1, lanes), 1) & (rows - 1)) < rlen).astype(F32)
        seen = lax.broadcasted_iota(jnp.int32, (PLEN, lanes), 0) < psize
        scores = dot(prompt_part(hd, 0, s), stacked(q_v, hd, s), NT)
        masked = jnp.concatenate([jnp.where(seen, scores, -jnp.inf), st_v[hd, s]], axis=0)
        top = jnp.max(masked, axis=0, keepdims=True)
        e = jnp.exp2((masked - top) * (SCALING * math.log2(math.e)))
        prob = e * (live / jnp.sum(e, axis=0, keepdims=True))
        p_v[s] = prob
        weights = prob.astype(BF16)
        w_v[hd, s] = weights
        part[hd, 1][s] = dot(weights[:PLEN], stacked(do_v, hd, s), NN)

    def gradients(hd, s):
        prob = p_v[s]
        gprob = jnp.concatenate([
            dot(prompt_part(hd, 1, s), stacked(do_v, hd, s), NT), gt_v[hd, s]], axis=0)
        delta = jnp.sum(prob * gprob, axis=0, keepdims=True)
        gscores = (prob * (gprob - delta)).astype(BF16)
        ds_v[hd, s] = gscores
        part[hd, 0][s] = dot(gscores[:PLEN], stacked(q_v, hd, s), NN) * SCALING

    def row_outputs(hd, s):
        keys_t = jnp.concatenate([prompt_part(hd, 0, s), answer_part(hd, 0, s)], axis=0).T
        values_t = jnp.concatenate([prompt_part(hd, 1, s), answer_part(hd, 1, s)], axis=0).T
        out = dot(values_t, w_v[hd, s], NN).astype(BF16).T
        dq = (dot(keys_t, ds_v[hd, s], NN) * SCALING).astype(BF16).T
        for g, col in enumerate(columns(hd)):
            o_v[rows_of(s), col] = out[g * rows:(g + 1) * rows]
            dq_v[rows_of(s), col] = dq[g * rows:(g + 1) * rows]
        cols = slice(hd * HEAD_SIZE, (hd + 1) * HEAD_SIZE)
        gav_v[rows_of(s), cols] = dot(
            w_v[hd, s, PLEN:], stacked(do_v, hd, s), NN).astype(BF16)
        gak_v[rows_of(s), cols] = (dot(
            ds_v[hd, s, PLEN:], stacked(q_v, hd, s), NN) * SCALING).astype(BF16)

    back_y, back_x, back_own = {}, {}, {}
    for hd, w in pairs:
        pair = hd, w
        back_y[pair] = [
            remote(y_out[pair].at[i], y_in[pair].at[i], by_send.at[hd, w, i],
                   by_recv.at[hd, w, i], dp=near[i]) for i in range(len(near))
        ]
        dst = (gpk_out, gpv_out)[w]
        cols = pl.ds(pl.multiple_of(h * width + hd * HEAD_SIZE, HEAD_SIZE), HEAD_SIZE)
        back_x[pair] = []
        for p in order:
            to = peers[p - 1]
            theirs = pl.ds(pl.multiple_of(to * span, span), span)
            back_x[pair].append(remote(
                x_out[pair].at[theirs], dst.at[:, cols],
                bx_send.at[hd, w, p - 1], bx_recv.at[hd, w, p - 1], head=to))
        back_own[pair] = pltpu.make_async_copy(
            x_out[pair].at[mine], dst.at[:, cols], bx_own.at[hd, w])

    last = kvh - 1, 0
    back_last = {}
    for p in range(heads):
        at = pl.ds(pl.multiple_of(lax.rem(h + p, heads) * span, span), span)
        for i in range(len(near)):
            back_last[p, i] = remote(
                y_out[last].at[i, at], y_in[last].at[i, at], bl_send.at[p, i],
                bl_recv.at[p, i], dp=near[i])

    def block_rows(p):
        return pl.ds(pl.multiple_of(lax.rem(h + p, heads) * span, span), span)

    def send_back(pair):
        for p in order + [0]:
            at = block_rows(p)
            terms = [part[pair][s, at] for s in range(slots)]
            for i, o in enumerate(offsets + [0]):
                total = None
                for s in range(slots):
                    term = terms[s] * picks[s, o]
                    total = term if total is None else total + term
                if o == 0:
                    own[pair][at] = total
                else:
                    y_out[pair][i, at] = total.astype(BF16)
                    if pair == last:
                        back_last[p, i].start()
        if pair != last:
            for copy in back_y[pair]:
                copy.start()

    def take_back(pair):
        if pair != last:
            for copy in back_y[pair]:
                copy.wait_recv()
        for p, copy in zip(order + [0], back_x[pair] + [back_own[pair]]):
            at = block_rows(p)
            total = own[pair][at]
            for i in range(len(near)):
                if pair == last:
                    back_last[p, i].wait_recv()
                total = total + y_in[pair][i, at].astype(F32)
            x_out[pair][at] = total.astype(BF16)
            copy.start()

    def each_slot(work, hd):
        for s in range(slots):
            work(hd, s)

    exchange(*pairs[0])
    forward(0, 0)
    for pair in pairs[1:]:
        exchange(*pair)
    for b in range(1, len(bundles)):
        forward(b, 0)
    for load in loads:
        load.wait()
    picks = {
        (s, o): jnp.where(relative(s) == MAX_SPREAD + o, 1.0, 0.0).astype(F32)
        for s in range(slots) for o in offsets + [0]
    }
    each_slot(answer_scores, 0)
    for b in range(len(bundles)):
        for p in order:
            forward(b, p)
    for hd in range(1, kvh):
        each_slot(answer_scores, hd)

    for hd in range(kvh):
        arrived(hd + 1 if hd > 0 else 0)
        each_slot(probabilities, hd)
        send_back((hd, 1))
        if hd == 0:
            arrived(1)
        each_slot(gradients, hd)
        send_back((hd, 0))

    for hd in range(kvh - 1):
        each_slot(row_outputs, hd)
        take_back((hd, 1))
        take_back((hd, 0))
    take_back((kvh - 1, 1))
    row_outputs(kvh - 1, 0)
    take_back(last)
    for s in range(1, slots):
        row_outputs(kvh - 1, s)

    for pair in pairs:
        for p in order:
            x_in[(*pair, p)].wait_send()
        if pair != last:
            for copy in back_y[pair]:
                copy.wait_send()
        for copy in back_x[pair]:
            copy.wait()
        back_own[pair].wait()
    for copy in [*y_in_copies.values(), *back_last.values()]:
        copy.wait_send()


def finish(o, dq, gak, gav, gpk, gpv, o_out, dq_out, gak_out, gav_out, gpk_out, gpv_out,
           wide_k, wide_v, sem):
    copies = [
        pltpu.make_async_copy(src, dst, sem.at[i])
        for i, (src, dst) in enumerate(
            [(o, o_out), (dq, dq_out), (gak, gak_out), (gav, gav_out),
             (wide_k, gpk_out.at[0]), (wide_v, gpv_out.at[0])])
    ]
    for copy in copies[:4]:
        copy.start()
    wide_k[...] = gpk[...].astype(F32)
    copies[4].start()
    wide_v[...] = gpv[...].astype(F32)
    copies[5].start()
    for copy in copies:
        copy.wait()


def on_device(queries, answer_keys, answer_values, prompt_keys, prompt_values,
              output_gradient, prompt_len, response_len, response_prompt):
    devices, heads = lax.axis_size("dp"), lax.axis_size("head")
    slots = response_len.shape[0]
    token_rows, q_width = queries.shape
    rows = token_rows // slots
    width = answer_keys.shape[1]
    kvh = width // HEAD_SIZE
    group = q_width // width
    lanes = group * rows
    span, full = prompt_keys.shape[1:]
    dma = pltpu.SemaphoreType.DMA
    anywhere = pl.BlockSpec(memory_space=pl.ANY)
    hbm = pl.BlockSpec(memory_space=pltpu.HBM)
    vmem = pl.BlockSpec(memory_space=pltpu.VMEM)
    vm, sm = pltpu.VMEM, pltpu.SMEM
    block = (PLEN, HEAD_SIZE)
    wide = vm((token_rows, q_width), BF16)
    narrow = vm((token_rows, width), BF16)
    square = (PLEN + rows, lanes)
    bundle = [1, 1] + [2] * (kvh - 1)
    scratch = [
        sm(prompt_len.shape, jnp.int32), sm(response_len.shape, jnp.int32),
        sm(response_prompt.shape, jnp.int32),
        wide, wide, narrow, narrow, vm((slots,) + square, F32),
        vm((kvh, slots) + square, BF16), vm((kvh, slots) + square, BF16),
        vm((span, full), BF16), vm((span, full), BF16),
        vm((kvh, slots, rows, lanes), F32), vm((kvh, slots, rows, lanes), F32),
    ]
    scratch += [vm((REACH, count) + block, BF16) for count in bundle]
    for shape in [vm((slots,) + block, F32), vm((REACH - 1,) + block, BF16),
                  vm((REACH - 1,) + block, BF16), vm(block, F32), vm(block, BF16)]:
        scratch += [shape] * (kvh * 2)
    scratch += [
        dma((7,)),
        dma((kvh, 2, heads - 1)), dma((kvh, 2, heads - 1)), dma((2,)),
        dma((kvh + 1, heads, REACH - 1)), dma((kvh + 1, heads, REACH - 1)),
        dma((kvh, 2, REACH - 1)), dma((kvh, 2, REACH - 1)),
        dma((kvh, 2, heads - 1)), dma((kvh, 2, heads - 1)), dma((kvh, 2)),
        dma((heads, REACH - 1)), dma((heads, REACH - 1)),
    ]
    sds = jax.ShapeDtypeStruct
    rows_out = [
        sds((token_rows, q_width), BF16), sds((token_rows, q_width), BF16),
        sds((token_rows, width), BF16), sds((token_rows, width), BF16),
    ]
    results = pl.pallas_call(
        functools.partial(kernel, (devices, heads, slots, rows, kvh, group)),
        out_shape=rows_out + [sds((span, full), BF16), sds((span, full), BF16)],
        in_specs=[hbm] * 9,
        out_specs=[vmem] * 4 + [anywhere] * 2,
        scratch_shapes=scratch,
        compiler_params=pltpu.CompilerParams(
            collective_id=0, has_side_effects=True, vmem_limit_bytes=48 * 1024 * 1024),
    )(*[pltpu.with_memory_space_constraint(x, pltpu.HBM) for x in (
        prompt_len, response_len, response_prompt, queries, output_gradient,
        answer_keys, answer_values, prompt_keys.reshape(span, full),
        prompt_values.reshape(span, full))])
    return pl.pallas_call(
        finish,
        out_shape=rows_out + [sds((1, span, full), F32), sds((1, span, full), F32)],
        in_specs=[vmem] * 6,
        out_specs=[anywhere] * 6,
        scratch_shapes=[vm((span, full), F32), vm((span, full), F32), dma((6,))],
        compiler_params=pltpu.CompilerParams(vmem_limit_bytes=4 * 1024 * 1024),
    )(*[pltpu.with_memory_space_constraint(x, pltpu.VMEM) for x in results])


def solution(mesh):
    in_specs = (
        P("dp", "head"),
        P("dp", "head"),
        P("dp", "head"),
        P("dp", "head", None),
        P("dp", "head", None),
        P("dp", "head"),
        P(),
        P("dp"),
        P("dp"),
    )
    out_specs = (
        P("dp", "head"),
        P("dp", "head"),
        P("dp", "head"),
        P("dp", "head"),
        P("dp", "head", None),
        P("dp", "head", None),
    )
    return jax.shard_map(
        on_device, mesh=mesh, in_specs=in_specs, out_specs=out_specs, check_vma=False
    )
```

```python
import functools
import math

import jax
import jax.numpy as jnp
from jax import lax
from jax.experimental import pallas as pl
from jax.experimental.pallas import tpu as pltpu
from jax.sharding import PartitionSpec as P

HEAD_SIZE = 128
PLEN = 256
MAX_SPREAD = 2
REACH = 2 * MAX_SPREAD + 1
MESH = pl.DeviceIdType.MESH
SCALING = 1.0 / math.sqrt(HEAD_SIZE)
F32 = jnp.float32
BF16 = jnp.bfloat16


def dot(a, b, dims):
    return lax.dot_general(a, b, (dims, ((), ())), preferred_element_type=F32)


NN = ((1,), (0,))
NT = ((1,), (1,))
TN = ((0,), (0,))


def kernel(sizes, *refs):
    devices, heads, slots, rows, kvh, group = sizes
    pairs = [(hd, w) for hd in range(kvh) for w in range(2)]
    bundles = [[(0, 0)], [(0, 1)]] + [[(hd, 0), (hd, 1)] for hd in range(1, kvh)]
    place = {pair: (b, j) for b, bundle in enumerate(bundles) for j, pair in enumerate(bundle)}
    refs = list(refs)
    (plen_hbm, rlen_hbm, rprompt_hbm, q_hbm, do_hbm, ak_hbm, av_hbm, pk_hbm, pv_hbm,
     o_v, dq_v, gak_v, gav_v, gpk_out, gpv_out,
     plen_ref, rlen_ref, rprompt_ref,
     q_v, do_v, ak_v, av_v, p_v, w_v, ds_v, pk_v, pv_v, st_v, gt_v) = refs[:29]
    kv, refs = refs[29:29 + len(bundles)], refs[29 + len(bundles):]
    (part, y_out, y_in, own, x_out) = [
        dict(zip(pairs, refs[i * len(pairs):(i + 1) * len(pairs)])) for i in range(5)
    ]
    (in_sem, x_send, x_recv, x_own, y_send, y_recv,
     by_send, by_recv, bx_send, bx_recv, bx_own, bl_send, bl_recv) = refs[5 * len(pairs):]

    me = lax.axis_index("dp")
    h = lax.axis_index("head")
    offsets = [-2, 2, -1, 1]
    near = [lax.rem(me + devices + o, devices) for o in offsets]
    span = PLEN // heads
    width = kvh * HEAD_SIZE
    lanes = group * rows
    peers = [lax.rem(h + p, heads) for p in range(1, heads)]
    order = [p for p in range(1, heads) if p != heads // 2] + [heads // 2]
    mine = pl.ds(pl.multiple_of(h * span, span), span)

    prompt_loads = [
        pltpu.make_async_copy(src, dst, x_own.at[i])
        for i, (src, dst) in enumerate([(pk_hbm, pk_v), (pv_hbm, pv_v)])
    ]
    loads = [
        pltpu.make_async_copy(src, dst, in_sem.at[i])
        for i, (src, dst) in enumerate(
            [(q_hbm, q_v), (do_hbm, do_v), (ak_hbm, ak_v), (av_hbm, av_v),
             (plen_hbm, plen_ref), (rlen_hbm, rlen_ref), (rprompt_hbm, rprompt_ref)])
    ]
    for load in prompt_loads + loads:
        load.start()

    def remote(src, dst, send, recv, **where):
        return pltpu.make_async_remote_copy(
            src_ref=src, dst_ref=dst, send_sem=send, recv_sem=recv,
            device_id=where, device_id_type=MESH)

    barrier = pltpu.get_barrier_semaphore()
    for p in peers:
        pl.semaphore_signal(barrier, inc=1, device_id={"head": p}, device_id_type=MESH)
    for d in near:
        pl.semaphore_signal(barrier, inc=1, device_id={"dp": d}, device_id_type=MESH)
    for load in prompt_loads:
        load.wait()
    for hd, w in pairs:
        b, j = place[hd, w]
        cols = pl.ds(pl.multiple_of(h * width + hd * HEAD_SIZE, HEAD_SIZE), HEAD_SIZE)
        kv[b][MAX_SPREAD, j, mine] = (pk_v, pv_v)[w][:, cols]
    pl.semaphore_wait(barrier, len(peers) + len(near))

    x_in = {}

    def exchange(hd, w):
        b, j = place[hd, w]
        for p in order:
            to = peers[p - 1]
            cols = pl.ds(pl.multiple_of(to * width + hd * HEAD_SIZE, HEAD_SIZE), HEAD_SIZE)
            x_in[hd, w, p] = remote(
                (pk_v, pv_v)[w].at[:, cols], kv[b].at[MAX_SPREAD, j, mine],
                x_send.at[hd, w, p - 1], x_recv.at[hd, w, p - 1], head=to)
            x_in[hd, w, p].start()

    y_in_copies = {}

    def forward(b, piece):
        if piece > 0:
            for pair in bundles[b]:
                x_in[(*pair, piece)].wait_recv()
        source = lax.rem(h + heads - piece, heads)
        at = pl.ds(pl.multiple_of(source * span, span), span)
        for i, o in enumerate(offsets):
            copy = remote(
                kv[b].at[MAX_SPREAD, :, at], kv[b].at[MAX_SPREAD - o, :, at],
                y_send.at[b, piece, i], y_recv.at[b, piece, i], dp=near[i])
            y_in_copies[b, piece, i] = copy
            copy.start()

    def arrived(b):
        for piece in range(heads):
            for i in range(len(near)):
                y_in_copies[b, piece, i].wait_recv()

    def rows_of(s):
        return slice(s * rows, (s + 1) * rows)

    def columns(hd):
        first = hd * group
        return [slice((first + g) * HEAD_SIZE, (first + g + 1) * HEAD_SIZE) for g in range(group)]

    def stacked(ref, hd, s):
        return jnp.concatenate([ref[rows_of(s), col] for col in columns(hd)], axis=0)

    def relative(s):
        return lax.rem(rprompt_ref[s] - me + (devices + MAX_SPREAD), devices)

    def prompt_part(hd, w, s):
        b, j = place[hd, w]
        return kv[b][jnp.minimum(relative(s), REACH - 1), j]

    def answer_part(hd, w, s):
        return (ak_v, av_v)[w][rows_of(s), hd * HEAD_SIZE:(hd + 1) * HEAD_SIZE]

    def answer_scores(hd, s):
        seen = lax.broadcasted_iota(jnp.int32, (rows, lanes), 0) <= (
            lax.broadcasted_iota(jnp.int32, (rows, lanes), 1) & (rows - 1))
        scores = dot(answer_part(hd, 0, s), stacked(q_v, hd, s), NT)
        st_v[hd, s] = jnp.where(seen, scores, -jnp.inf)
        gt_v[hd, s] = dot(answer_part(hd, 1, s), stacked(do_v, hd, s), NT)

    def probabilities(hd, s):
        psize = plen_ref[rprompt_ref[s]]
        rlen = rlen_ref[s]
        live = ((lax.broadcasted_iota(jnp.int32, (1, lanes), 1) & (rows - 1)) < rlen).astype(F32)
        seen = lax.broadcasted_iota(jnp.int32, (PLEN, lanes), 0) < psize
        scores = dot(prompt_part(hd, 0, s), stacked(q_v, hd, s), NT)
        masked = jnp.concatenate([jnp.where(seen, scores, -jnp.inf), st_v[hd, s]], axis=0)
        top = jnp.max(masked, axis=0, keepdims=True)
        e = jnp.exp2((masked - top) * (SCALING * math.log2(math.e)))
        prob = e * (live / jnp.sum(e, axis=0, keepdims=True))
        p_v[s] = prob
        weights = prob.astype(BF16)
        w_v[hd, s] = weights
        part[hd, 1][s] = dot(weights[:PLEN], stacked(do_v, hd, s), NN)

    def gradients(hd, s):
        prob = p_v[s]
        gprob = jnp.concatenate([
            dot(prompt_part(hd, 1, s), stacked(do_v, hd, s), NT), gt_v[hd, s]], axis=0)
        delta = jnp.sum(prob * gprob, axis=0, keepdims=True)
        gscores = (prob * (gprob - delta)).astype(BF16)
        ds_v[hd, s] = gscores
        part[hd, 0][s] = dot(gscores[:PLEN], stacked(q_v, hd, s), NN) * SCALING

    def row_outputs(hd, s):
        keys_t = jnp.concatenate([prompt_part(hd, 0, s), answer_part(hd, 0, s)], axis=0).T
        values_t = jnp.concatenate([prompt_part(hd, 1, s), answer_part(hd, 1, s)], axis=0).T
        out = dot(values_t, w_v[hd, s], NN).astype(BF16).T
        dq = (dot(keys_t, ds_v[hd, s], NN) * SCALING).astype(BF16).T
        for g, col in enumerate(columns(hd)):
            o_v[rows_of(s), col] = out[g * rows:(g + 1) * rows]
            dq_v[rows_of(s), col] = dq[g * rows:(g + 1) * rows]
        cols = slice(hd * HEAD_SIZE, (hd + 1) * HEAD_SIZE)
        gav_v[rows_of(s), cols] = dot(
            w_v[hd, s, PLEN:], stacked(do_v, hd, s), NN).astype(BF16)
        gak_v[rows_of(s), cols] = (dot(
            ds_v[hd, s, PLEN:], stacked(q_v, hd, s), NN) * SCALING).astype(BF16)

    back_y, back_x, back_own = {}, {}, {}
    for hd, w in pairs:
        pair = hd, w
        back_y[pair] = [
            remote(y_out[pair].at[i], y_in[pair].at[i], by_send.at[hd, w, i],
                   by_recv.at[hd, w, i], dp=near[i]) for i in range(len(near))
        ]
        dst = (gpk_out, gpv_out)[w]
        cols = pl.ds(pl.multiple_of(h * width + hd * HEAD_SIZE, HEAD_SIZE), HEAD_SIZE)
        back_x[pair] = []
        for p in order:
            to = peers[p - 1]
            theirs = pl.ds(pl.multiple_of(to * span, span), span)
            back_x[pair].append(remote(
                x_out[pair].at[theirs], dst.at[:, cols],
                bx_send.at[hd, w, p - 1], bx_recv.at[hd, w, p - 1], head=to))
        back_own[pair] = pltpu.make_async_copy(
            x_out[pair].at[mine], dst.at[:, cols], bx_own.at[hd, w])

    last = kvh - 1, 0
    back_last = {}
    for p in range(heads):
        at = pl.ds(pl.multiple_of(lax.rem(h + p, heads) * span, span), span)
        for i in range(len(near)):
            back_last[p, i] = remote(
                y_out[last].at[i, at], y_in[last].at[i, at], bl_send.at[p, i],
                bl_recv.at[p, i], dp=near[i])

    def block_rows(p):
        return pl.ds(pl.multiple_of(lax.rem(h + p, heads) * span, span), span)

    def send_back(pair):
        for p in order + [0]:
            at = block_rows(p)
            terms = [part[pair][s, at] for s in range(slots)]
            for i, o in enumerate(offsets + [0]):
                total = None
                for s in range(slots):
                    term = terms[s] * picks[s, o]
                    total = term if total is None else total + term
                if o == 0:
                    own[pair][at] = total
                else:
                    y_out[pair][i, at] = total.astype(BF16)
                    if pair == last:
                        back_last[p, i].start()
        if pair != last:
            for copy in back_y[pair]:
                copy.start()

    def take_back(pair):
        if pair != last:
            for copy in back_y[pair]:
                copy.wait_recv()
        for p, copy in zip(order + [0], back_x[pair] + [back_own[pair]]):
            at = block_rows(p)
            total = own[pair][at]
            for i in range(len(near)):
                if pair == last:
                    back_last[p, i].wait_recv()
                total = total + y_in[pair][i, at].astype(F32)
            x_out[pair][at] = total.astype(BF16)
            copy.start()

    def each_slot(work, hd):
        for s in range(slots):
            work(hd, s)

    exchange(*pairs[0])
    forward(0, 0)
    for pair in pairs[1:]:
        exchange(*pair)
    for b in range(1, len(bundles)):
        forward(b, 0)
    for load in loads:
        load.wait()
    picks = {
        (s, o): jnp.where(relative(s) == MAX_SPREAD + o, 1.0, 0.0).astype(F32)
        for s in range(slots) for o in offsets + [0]
    }
    each_slot(answer_scores, 0)
    for b in range(len(bundles)):
        for p in order:
            forward(b, p)
    for hd in range(1, kvh):
        each_slot(answer_scores, hd)

    for hd in range(kvh):
        if hd > 0:
            each_slot(row_outputs, hd - 1)
        arrived(hd + 1 if hd > 0 else 0)
        each_slot(probabilities, hd)
        send_back((hd, 1))
        if hd == 0:
            arrived(1)
        each_slot(gradients, hd)
        send_back((hd, 0))

    for hd in range(kvh - 1):
        take_back((hd, 1))
        take_back((hd, 0))
    row_outputs(kvh - 1, 0)
    row_outputs(kvh - 1, 1)
    take_back((kvh - 1, 1))
    row_outputs(kvh - 1, 2)
    take_back(last)
    for s in range(3, slots):
        row_outputs(kvh - 1, s)

    for pair in pairs:
        for p in order:
            x_in[(*pair, p)].wait_send()
        if pair != last:
            for copy in back_y[pair]:
                copy.wait_send()
        for copy in back_x[pair]:
            copy.wait()
        back_own[pair].wait()
    for copy in [*y_in_copies.values(), *back_last.values()]:
        copy.wait_send()


def finish(o, dq, gak, gav, gpk, gpv, o_out, dq_out, gak_out, gav_out, gpk_out, gpv_out,
           wide_k, wide_v, sem):
    copies = [
        pltpu.make_async_copy(src, dst, sem.at[i])
        for i, (src, dst) in enumerate(
            [(o, o_out), (dq, dq_out), (gak, gak_out), (gav, gav_out),
             (wide_k, gpk_out.at[0]), (wide_v, gpv_out.at[0])])
    ]
    for copy in copies[:4]:
        copy.start()
    wide_k[...] = gpk[...].astype(F32)
    copies[4].start()
    wide_v[...] = gpv[...].astype(F32)
    copies[5].start()
    for copy in copies:
        copy.wait()


def on_device(queries, answer_keys, answer_values, prompt_keys, prompt_values,
              output_gradient, prompt_len, response_len, response_prompt):
    devices, heads = lax.axis_size("dp"), lax.axis_size("head")
    slots = response_len.shape[0]
    token_rows, q_width = queries.shape
    rows = token_rows // slots
    width = answer_keys.shape[1]
    kvh = width // HEAD_SIZE
    group = q_width // width
    lanes = group * rows
    span, full = prompt_keys.shape[1:]
    dma = pltpu.SemaphoreType.DMA
    anywhere = pl.BlockSpec(memory_space=pl.ANY)
    hbm = pl.BlockSpec(memory_space=pltpu.HBM)
    vmem = pl.BlockSpec(memory_space=pltpu.VMEM)
    vm, sm = pltpu.VMEM, pltpu.SMEM
    block = (PLEN, HEAD_SIZE)
    wide = vm((token_rows, q_width), BF16)
    narrow = vm((token_rows, width), BF16)
    square = (PLEN + rows, lanes)
    bundle = [1, 1] + [2] * (kvh - 1)
    scratch = [
        sm(prompt_len.shape, jnp.int32), sm(response_len.shape, jnp.int32),
        sm(response_prompt.shape, jnp.int32),
        wide, wide, narrow, narrow, vm((slots,) + square, F32),
        vm((kvh, slots) + square, BF16), vm((kvh, slots) + square, BF16),
        vm((span, full), BF16), vm((span, full), BF16),
        vm((kvh, slots, rows, lanes), F32), vm((kvh, slots, rows, lanes), F32),
    ]
    scratch += [vm((REACH, count) + block, BF16) for count in bundle]
    for shape in [vm((slots,) + block, F32), vm((REACH - 1,) + block, BF16),
                  vm((REACH - 1,) + block, BF16), vm(block, F32), vm(block, BF16)]:
        scratch += [shape] * (kvh * 2)
    scratch += [
        dma((7,)),
        dma((kvh, 2, heads - 1)), dma((kvh, 2, heads - 1)), dma((2,)),
        dma((kvh + 1, heads, REACH - 1)), dma((kvh + 1, heads, REACH - 1)),
        dma((kvh, 2, REACH - 1)), dma((kvh, 2, REACH - 1)),
        dma((kvh, 2, heads - 1)), dma((kvh, 2, heads - 1)), dma((kvh, 2)),
        dma((heads, REACH - 1)), dma((heads, REACH - 1)),
    ]
    sds = jax.ShapeDtypeStruct
    rows_out = [
        sds((token_rows, q_width), BF16), sds((token_rows, q_width), BF16),
        sds((token_rows, width), BF16), sds((token_rows, width), BF16),
    ]
    results = pl.pallas_call(
        functools.partial(kernel, (devices, heads, slots, rows, kvh, group)),
        out_shape=rows_out + [sds((span, full), BF16), sds((span, full), BF16)],
        in_specs=[hbm] * 9,
        out_specs=[vmem] * 4 + [anywhere] * 2,
        scratch_shapes=scratch,
        compiler_params=pltpu.CompilerParams(
            collective_id=0, has_side_effects=True, vmem_limit_bytes=48 * 1024 * 1024),
    )(*[pltpu.with_memory_space_constraint(x, pltpu.HBM) for x in (
        prompt_len, response_len, response_prompt, queries, output_gradient,
        answer_keys, answer_values, prompt_keys.reshape(span, full),
        prompt_values.reshape(span, full))])
    return pl.pallas_call(
        finish,
        out_shape=rows_out + [sds((1, span, full), F32), sds((1, span, full), F32)],
        in_specs=[vmem] * 6,
        out_specs=[anywhere] * 6,
        scratch_shapes=[vm((span, full), F32), vm((span, full), F32), dma((6,))],
        compiler_params=pltpu.CompilerParams(vmem_limit_bytes=4 * 1024 * 1024),
    )(*[pltpu.with_memory_space_constraint(x, pltpu.VMEM) for x in results])


def solution(mesh):
    in_specs = (
        P("dp", "head"),
        P("dp", "head"),
        P("dp", "head"),
        P("dp", "head", None),
        P("dp", "head", None),
        P("dp", "head"),
        P(),
        P("dp"),
        P("dp"),
    )
    out_specs = (
        P("dp", "head"),
        P("dp", "head"),
        P("dp", "head"),
        P("dp", "head"),
        P("dp", "head", None),
        P("dp", "head", None),
    )
    return jax.shard_map(
        on_device, mesh=mesh, in_specs=in_specs, out_specs=out_specs, check_vma=False
    )
```

```python
import functools
import math

import jax
import jax.numpy as jnp
from jax import lax
from jax.experimental import pallas as pl
from jax.experimental.pallas import tpu as pltpu
from jax.sharding import PartitionSpec as P

HEAD_SIZE = 128
PLEN = 256
MAX_SPREAD = 2
REACH = 2 * MAX_SPREAD + 1
SIDE = 256
MESH = pl.DeviceIdType.MESH
SCALING = 1.0 / math.sqrt(HEAD_SIZE)
F32 = jnp.float32
BF16 = jnp.bfloat16


def dot(a, b, dims):
    return lax.dot_general(a, b, (dims, ((), ())), preferred_element_type=F32)


NN = ((1,), (0,))
NT = ((1,), (1,))
TN = ((0,), (0,))


def kernel(sizes, *refs):
    devices, heads, slots, rows, kvh, group = sizes
    pairs = [(hd, w) for hd in range(kvh) for w in range(2)]
    bundles = [[(0, 0)], [(0, 1)]] + [[(hd, 0), (hd, 1)] for hd in range(1, kvh)]
    place = {pair: (b, j) for b, bundle in enumerate(bundles) for j, pair in enumerate(bundle)}
    refs = list(refs)
    (plen_hbm, rlen_hbm, rprompt_hbm, q_hbm, do_hbm, ak_hbm, av_hbm, pk_hbm, pv_hbm,
     o_v, dq_v, gak_v, gav_v, gpk_out, gpv_out,
     plen_ref, rlen_ref, rprompt_ref,
     q_v, do_v, ak_v, av_v, p_v, w_v, ds_v, pk_v, pv_v, st_v, gt_v, id_v) = refs[:30]
    kv, refs = refs[30:30 + len(bundles)], refs[30 + len(bundles):]
    (part, y_out, y_in, own, x_out) = [
        dict(zip(pairs, refs[i * len(pairs):(i + 1) * len(pairs)])) for i in range(5)
    ]
    (in_sem, x_send, x_recv, x_own, y_send, y_recv,
     by_send, by_recv, bx_send, bx_recv, bx_own, bl_send, bl_recv) = refs[5 * len(pairs):]

    me = lax.axis_index("dp")
    h = lax.axis_index("head")
    offsets = [-2, 2, -1, 1]
    near = [lax.rem(me + devices + o, devices) for o in offsets]
    span = PLEN // heads
    width = kvh * HEAD_SIZE
    lanes = group * rows
    peers = [lax.rem(h + p, heads) for p in range(1, heads)]
    order = [p for p in range(1, heads) if p != heads // 2] + [heads // 2]
    mine = pl.ds(pl.multiple_of(h * span, span), span)

    prompt_loads = [
        pltpu.make_async_copy(src, dst, x_own.at[i])
        for i, (src, dst) in enumerate([(pk_hbm, pk_v), (pv_hbm, pv_v)])
    ]
    loads = [
        pltpu.make_async_copy(src, dst, in_sem.at[i])
        for i, (src, dst) in enumerate(
            [(q_hbm, q_v), (do_hbm, do_v), (ak_hbm, ak_v), (av_hbm, av_v),
             (plen_hbm, plen_ref), (rlen_hbm, rlen_ref), (rprompt_hbm, rprompt_ref)])
    ]
    for load in prompt_loads + loads:
        load.start()

    def remote(src, dst, send, recv, **where):
        return pltpu.make_async_remote_copy(
            src_ref=src, dst_ref=dst, send_sem=send, recv_sem=recv,
            device_id=where, device_id_type=MESH)

    barrier = pltpu.get_barrier_semaphore()
    for p in peers:
        pl.semaphore_signal(barrier, inc=1, device_id={"head": p}, device_id_type=MESH)
    for d in near:
        pl.semaphore_signal(barrier, inc=1, device_id={"dp": d}, device_id_type=MESH)
    id_v[...] = (lax.broadcasted_iota(jnp.int32, (SIDE, SIDE), 0)
                 == lax.broadcasted_iota(jnp.int32, (SIDE, SIDE), 1)).astype(F32).astype(BF16)
    for load in prompt_loads:
        load.wait()
    for hd, w in pairs:
        b, j = place[hd, w]
        cols = pl.ds(pl.multiple_of(h * width + hd * HEAD_SIZE, HEAD_SIZE), HEAD_SIZE)
        kv[b][MAX_SPREAD, j, mine] = (pk_v, pv_v)[w][:, cols]
    pl.semaphore_wait(barrier, len(peers) + len(near))

    x_in = {}

    def exchange(hd, w):
        b, j = place[hd, w]
        for p in order:
            to = peers[p - 1]
            cols = pl.ds(pl.multiple_of(to * width + hd * HEAD_SIZE, HEAD_SIZE), HEAD_SIZE)
            x_in[hd, w, p] = remote(
                (pk_v, pv_v)[w].at[:, cols], kv[b].at[MAX_SPREAD, j, mine],
                x_send.at[hd, w, p - 1], x_recv.at[hd, w, p - 1], head=to)
            x_in[hd, w, p].start()

    y_in_copies = {}

    def forward(b, piece):
        if piece > 0:
            for pair in bundles[b]:
                x_in[(*pair, piece)].wait_recv()
        source = lax.rem(h + heads - piece, heads)
        at = pl.ds(pl.multiple_of(source * span, span), span)
        for i, o in enumerate(offsets):
            copy = remote(
                kv[b].at[MAX_SPREAD, :, at], kv[b].at[MAX_SPREAD - o, :, at],
                y_send.at[b, piece, i], y_recv.at[b, piece, i], dp=near[i])
            y_in_copies[b, piece, i] = copy
            copy.start()

    def arrived(b):
        for piece in range(heads):
            for i in range(len(near)):
                y_in_copies[b, piece, i].wait_recv()

    def rows_of(s):
        return slice(s * rows, (s + 1) * rows)

    def columns(hd):
        first = hd * group
        return [slice((first + g) * HEAD_SIZE, (first + g + 1) * HEAD_SIZE) for g in range(group)]

    def stacked(ref, hd, s):
        return jnp.concatenate([ref[rows_of(s), col] for col in columns(hd)], axis=0)

    def relative(s):
        return lax.rem(rprompt_ref[s] - me + (devices + MAX_SPREAD), devices)

    def prompt_part(hd, w, s):
        b, j = place[hd, w]
        return kv[b][jnp.minimum(relative(s), REACH - 1), j]

    def answer_part(hd, w, s):
        return (ak_v, av_v)[w][rows_of(s), hd * HEAD_SIZE:(hd + 1) * HEAD_SIZE]

    def answer_scores(hd, s):
        seen = lax.broadcasted_iota(jnp.int32, (rows, lanes), 0) <= (
            lax.broadcasted_iota(jnp.int32, (rows, lanes), 1) & (rows - 1))
        scores = dot(answer_part(hd, 0, s), stacked(q_v, hd, s), NT)
        st_v[hd, s] = jnp.where(seen, scores, -jnp.inf)
        gt_v[hd, s] = dot(answer_part(hd, 1, s), stacked(do_v, hd, s), NT)

    def probabilities(hd, s):
        psize = plen_ref[rprompt_ref[s]]
        rlen = rlen_ref[s]
        live = ((lax.broadcasted_iota(jnp.int32, (1, lanes), 1) & (rows - 1)) < rlen).astype(F32)
        seen = lax.broadcasted_iota(jnp.int32, (PLEN, lanes), 0) < psize
        scores = dot(prompt_part(hd, 0, s), stacked(q_v, hd, s), NT)
        masked = jnp.concatenate([jnp.where(seen, scores, -jnp.inf), st_v[hd, s]], axis=0)
        top = jnp.max(masked, axis=0, keepdims=True)
        e = jnp.exp2((masked - top) * (SCALING * math.log2(math.e)))
        prob = e * (live / jnp.sum(e, axis=0, keepdims=True))
        p_v[s] = prob
        weights = prob.astype(BF16)
        w_v[hd, s] = weights
        part[hd, 1][s] = dot(weights[:PLEN], stacked(do_v, hd, s), NN)

    def gradients(hd, s):
        prob = p_v[s]
        gprob = jnp.concatenate([
            dot(prompt_part(hd, 1, s), stacked(do_v, hd, s), NT), gt_v[hd, s]], axis=0)
        delta = jnp.sum(prob * gprob, axis=0, keepdims=True)
        gscores = (prob * (gprob - delta)).astype(BF16)
        ds_v[hd, s] = gscores
        part[hd, 0][s] = dot(gscores[:PLEN], stacked(q_v, hd, s), NN) * SCALING

    def turned(x):
        side = x.shape[1]
        return dot(id_v[:side, :side], x, NT).astype(BF16)

    def row_outputs(hd, s):
        keys = jnp.concatenate([prompt_part(hd, 0, s), answer_part(hd, 0, s)], axis=0)
        values = jnp.concatenate([prompt_part(hd, 1, s), answer_part(hd, 1, s)], axis=0)
        out = dot(turned(values), w_v[hd, s], NN).astype(BF16)
        dq = (dot(turned(keys), ds_v[hd, s], NN) * SCALING).astype(BF16)
        per = SIDE // rows
        for c in range(lanes // SIDE):
            out_rows = turned(out[:, c * SIDE:(c + 1) * SIDE])
            dq_rows = turned(dq[:, c * SIDE:(c + 1) * SIDE])
            for g, col in enumerate(columns(hd)[c * per:(c + 1) * per]):
                o_v[rows_of(s), col] = out_rows[g * rows:(g + 1) * rows]
                dq_v[rows_of(s), col] = dq_rows[g * rows:(g + 1) * rows]
        cols = slice(hd * HEAD_SIZE, (hd + 1) * HEAD_SIZE)
        gav_v[rows_of(s), cols] = dot(
            w_v[hd, s, PLEN:], stacked(do_v, hd, s), NN).astype(BF16)
        gak_v[rows_of(s), cols] = (dot(
            ds_v[hd, s, PLEN:], stacked(q_v, hd, s), NN) * SCALING).astype(BF16)

    back_y, back_x, back_own = {}, {}, {}
    for hd, w in pairs:
        pair = hd, w
        back_y[pair] = [
            remote(y_out[pair].at[i], y_in[pair].at[i], by_send.at[hd, w, i],
                   by_recv.at[hd, w, i], dp=near[i]) for i in range(len(near))
        ]
        dst = (gpk_out, gpv_out)[w]
        cols = pl.ds(pl.multiple_of(h * width + hd * HEAD_SIZE, HEAD_SIZE), HEAD_SIZE)
        back_x[pair] = []
        for p in order:
            to = peers[p - 1]
            theirs = pl.ds(pl.multiple_of(to * span, span), span)
            back_x[pair].append(remote(
                x_out[pair].at[theirs], dst.at[:, cols],
                bx_send.at[hd, w, p - 1], bx_recv.at[hd, w, p - 1], head=to))
        back_own[pair] = pltpu.make_async_copy(
            x_out[pair].at[mine], dst.at[:, cols], bx_own.at[hd, w])

    last = kvh - 1, 0
    back_last = {}
    for p in range(heads):
        at = pl.ds(pl.multiple_of(lax.rem(h + p, heads) * span, span), span)
        for i in range(len(near)):
            back_last[p, i] = remote(
                y_out[last].at[i, at], y_in[last].at[i, at], bl_send.at[p, i],
                bl_recv.at[p, i], dp=near[i])

    def block_rows(p):
        return pl.ds(pl.multiple_of(lax.rem(h + p, heads) * span, span), span)

    def send_back(pair):
        for p in order + [0]:
            at = block_rows(p)
            terms = [part[pair][s, at] for s in range(slots)]
            for i, o in enumerate(offsets + [0]):
                total = None
                for s in range(slots):
                    term = terms[s] * picks[s, o]
                    total = term if total is None else total + term
                if o == 0:
                    own[pair][at] = total
                else:
                    y_out[pair][i, at] = total.astype(BF16)
                    if pair == last:
                        back_last[p, i].start()
        if pair != last:
            for copy in back_y[pair]:
                copy.start()

    def take_back(pair):
        if pair != last:
            for copy in back_y[pair]:
                copy.wait_recv()
        for p, copy in zip(order + [0], back_x[pair] + [back_own[pair]]):
            at = block_rows(p)
            total = own[pair][at]
            for i in range(len(near)):
                if pair == last:
                    back_last[p, i].wait_recv()
                total = total + y_in[pair][i, at].astype(F32)
            x_out[pair][at] = total.astype(BF16)
            copy.start()

    def each_slot(work, hd):
        for s in range(slots):
            work(hd, s)

    exchange(*pairs[0])
    forward(0, 0)
    for pair in pairs[1:]:
        exchange(*pair)
    for b in range(1, len(bundles)):
        forward(b, 0)
    for load in loads:
        load.wait()
    picks = {
        (s, o): jnp.where(relative(s) == MAX_SPREAD + o, 1.0, 0.0).astype(F32)
        for s in range(slots) for o in offsets + [0]
    }
    each_slot(answer_scores, 0)
    for b in range(len(bundles)):
        for p in order:
            forward(b, p)
    for hd in range(1, kvh):
        each_slot(answer_scores, hd)

    for hd in range(kvh):
        arrived(hd + 1 if hd > 0 else 0)
        each_slot(probabilities, hd)
        send_back((hd, 1))
        if hd == 0:
            arrived(1)
        each_slot(gradients, hd)
        send_back((hd, 0))

    for hd in range(kvh - 1):
        each_slot(row_outputs, hd)
        take_back((hd, 1))
        take_back((hd, 0))
    take_back((kvh - 1, 1))
    row_outputs(kvh - 1, 0)
    take_back(last)
    for s in range(1, slots):
        row_outputs(kvh - 1, s)

    for pair in pairs:
        for p in order:
            x_in[(*pair, p)].wait_send()
        if pair != last:
            for copy in back_y[pair]:
                copy.wait_send()
        for copy in back_x[pair]:
            copy.wait()
        back_own[pair].wait()
    for copy in [*y_in_copies.values(), *back_last.values()]:
        copy.wait_send()


def finish(o, dq, gak, gav, gpk, gpv, o_out, dq_out, gak_out, gav_out, gpk_out, gpv_out,
           wide_k, wide_v, sem):
    copies = [
        pltpu.make_async_copy(src, dst, sem.at[i])
        for i, (src, dst) in enumerate(
            [(o, o_out), (dq, dq_out), (gak, gak_out), (gav, gav_out),
             (wide_k, gpk_out.at[0]), (wide_v, gpv_out.at[0])])
    ]
    for copy in copies[:4]:
        copy.start()
    wide_k[...] = gpk[...].astype(F32)
    copies[4].start()
    wide_v[...] = gpv[...].astype(F32)
    copies[5].start()
    for copy in copies:
        copy.wait()


def on_device(queries, answer_keys, answer_values, prompt_keys, prompt_values,
              output_gradient, prompt_len, response_len, response_prompt):
    devices, heads = lax.axis_size("dp"), lax.axis_size("head")
    slots = response_len.shape[0]
    token_rows, q_width = queries.shape
    rows = token_rows // slots
    width = answer_keys.shape[1]
    kvh = width // HEAD_SIZE
    group = q_width // width
    lanes = group * rows
    span, full = prompt_keys.shape[1:]
    dma = pltpu.SemaphoreType.DMA
    anywhere = pl.BlockSpec(memory_space=pl.ANY)
    hbm = pl.BlockSpec(memory_space=pltpu.HBM)
    vmem = pl.BlockSpec(memory_space=pltpu.VMEM)
    vm, sm = pltpu.VMEM, pltpu.SMEM
    block = (PLEN, HEAD_SIZE)
    wide = vm((token_rows, q_width), BF16)
    narrow = vm((token_rows, width), BF16)
    square = (PLEN + rows, lanes)
    bundle = [1, 1] + [2] * (kvh - 1)
    scratch = [
        sm(prompt_len.shape, jnp.int32), sm(response_len.shape, jnp.int32),
        sm(response_prompt.shape, jnp.int32),
        wide, wide, narrow, narrow, vm((slots,) + square, F32),
        vm((kvh, slots) + square, BF16), vm((kvh, slots) + square, BF16),
        vm((span, full), BF16), vm((span, full), BF16),
        vm((kvh, slots, rows, lanes), F32), vm((kvh, slots, rows, lanes), F32),
        vm((SIDE, SIDE), BF16),
    ]
    scratch += [vm((REACH, count) + block, BF16) for count in bundle]
    for shape in [vm((slots,) + block, F32), vm((REACH - 1,) + block, BF16),
                  vm((REACH - 1,) + block, BF16), vm(block, F32), vm(block, BF16)]:
        scratch += [shape] * (kvh * 2)
    scratch += [
        dma((7,)),
        dma((kvh, 2, heads - 1)), dma((kvh, 2, heads - 1)), dma((2,)),
        dma((kvh + 1, heads, REACH - 1)), dma((kvh + 1, heads, REACH - 1)),
        dma((kvh, 2, REACH - 1)), dma((kvh, 2, REACH - 1)),
        dma((kvh, 2, heads - 1)), dma((kvh, 2, heads - 1)), dma((kvh, 2)),
        dma((heads, REACH - 1)), dma((heads, REACH - 1)),
    ]
    sds = jax.ShapeDtypeStruct
    rows_out = [
        sds((token_rows, q_width), BF16), sds((token_rows, q_width), BF16),
        sds((token_rows, width), BF16), sds((token_rows, width), BF16),
    ]
    results = pl.pallas_call(
        functools.partial(kernel, (devices, heads, slots, rows, kvh, group)),
        out_shape=rows_out + [sds((span, full), BF16), sds((span, full), BF16)],
        in_specs=[hbm] * 9,
        out_specs=[vmem] * 4 + [anywhere] * 2,
        scratch_shapes=scratch,
        compiler_params=pltpu.CompilerParams(
            collective_id=0, has_side_effects=True, vmem_limit_bytes=48 * 1024 * 1024),
    )(*[pltpu.with_memory_space_constraint(x, pltpu.HBM) for x in (
        prompt_len, response_len, response_prompt, queries, output_gradient,
        answer_keys, answer_values, prompt_keys.reshape(span, full),
        prompt_values.reshape(span, full))])
    return pl.pallas_call(
        finish,
        out_shape=rows_out + [sds((1, span, full), F32), sds((1, span, full), F32)],
        in_specs=[vmem] * 6,
        out_specs=[anywhere] * 6,
        scratch_shapes=[vm((span, full), F32), vm((span, full), F32), dma((6,))],
        compiler_params=pltpu.CompilerParams(vmem_limit_bytes=4 * 1024 * 1024),
    )(*[pltpu.with_memory_space_constraint(x, pltpu.VMEM) for x in results])


def solution(mesh):
    in_specs = (
        P("dp", "head"),
        P("dp", "head"),
        P("dp", "head"),
        P("dp", "head", None),
        P("dp", "head", None),
        P("dp", "head"),
        P(),
        P("dp"),
        P("dp"),
    )
    out_specs = (
        P("dp", "head"),
        P("dp", "head"),
        P("dp", "head"),
        P("dp", "head"),
        P("dp", "head", None),
        P("dp", "head", None),
    )
    return jax.shard_map(
        on_device, mesh=mesh, in_specs=in_specs, out_specs=out_specs, check_vma=False
    )
```

```python
import functools
import math

import jax
import jax.numpy as jnp
from jax import lax
from jax.experimental import pallas as pl
from jax.experimental.pallas import tpu as pltpu
from jax.sharding import PartitionSpec as P

HEAD_SIZE = 128
PLEN = 256
MAX_SPREAD = 2
REACH = 2 * MAX_SPREAD + 1
MESH = pl.DeviceIdType.MESH
SCALING = 1.0 / math.sqrt(HEAD_SIZE)
F32 = jnp.float32
BF16 = jnp.bfloat16


def dot(a, b, dims):
    return lax.dot_general(a, b, (dims, ((), ())), preferred_element_type=F32)


NN = ((1,), (0,))
NT = ((1,), (1,))
TN = ((0,), (0,))


def kernel(sizes, *refs):
    devices, heads, slots, rows, kvh, group = sizes
    span = PLEN // heads
    width = kvh * HEAD_SIZE
    lanes = group * rows
    inward = [(0, 0, kvh)] + [(1, hd, 1) for hd in range(kvh)]
    outward = [(1, 0, kvh)] + [(0, hd, 1) for hd in range(kvh)]
    refs = list(refs)
    (plen_hbm, rlen_hbm, rprompt_hbm, q_hbm, do_hbm, ak_hbm, av_hbm, pk_hbm, pv_hbm,
     o_v, dq_v, gak_v, gav_v, gpk_out, gpv_out,
     plen_ref, rlen_ref, rprompt_ref,
     q_v, do_v, ak_v, av_v, p_v, w_v, ds_v, pk_v, pv_v, st_v, gt_v) = refs[:29]
    kv, refs = refs[29:29 + len(inward)], refs[29 + len(inward):]
    (part, y_out, y_in, own, x_out) = [
        refs[i * len(outward):(i + 1) * len(outward)] for i in range(5)
    ]
    (in_sem, x_send, x_recv, x_own, y_send, y_recv,
     by_send, by_recv, bx_send, bx_recv, bx_own) = refs[5 * len(outward):]

    me = lax.axis_index("dp")
    h = lax.axis_index("head")
    offsets = [-2, 2, -1, 1]
    near = [lax.rem(me + devices + o, devices) for o in offsets]
    peers = [lax.rem(h + p, heads) for p in range(1, heads)]
    order = [p for p in range(1, heads) if p != heads // 2] + [heads // 2]
    mine = pl.ds(pl.multiple_of(h * span, span), span)

    prompt_loads = [
        pltpu.make_async_copy(src, dst, x_own.at[i])
        for i, (src, dst) in enumerate([(pk_hbm, pk_v), (pv_hbm, pv_v)])
    ]
    loads = [
        pltpu.make_async_copy(src, dst, in_sem.at[i])
        for i, (src, dst) in enumerate(
            [(q_hbm, q_v), (do_hbm, do_v), (ak_hbm, ak_v), (av_hbm, av_v),
             (plen_hbm, plen_ref), (rlen_hbm, rlen_ref), (rprompt_hbm, rprompt_ref)])
    ]
    for load in prompt_loads + loads:
        load.start()

    def remote(src, dst, send, recv, **where):
        return pltpu.make_async_remote_copy(
            src_ref=src, dst_ref=dst, send_sem=send, recv_sem=recv,
            device_id=where, device_id_type=MESH)

    def columns_at(holder, hd, count):
        return pl.ds(
            pl.multiple_of(holder * width + hd * HEAD_SIZE, HEAD_SIZE), count * HEAD_SIZE)

    barrier = pltpu.get_barrier_semaphore()
    for p in peers:
        pl.semaphore_signal(barrier, inc=1, device_id={"head": p}, device_id_type=MESH)
    for d in near:
        pl.semaphore_signal(barrier, inc=1, device_id={"dp": d}, device_id_type=MESH)
    for load in prompt_loads:
        load.wait()
    for b, (w, hd, count) in enumerate(inward):
        kv[b][MAX_SPREAD, mine] = (pk_v, pv_v)[w][:, columns_at(h, hd, count)]
    pl.semaphore_wait(barrier, len(peers) + len(near))

    x_in = {}

    def exchange(b):
        w, hd, count = inward[b]
        for p in order:
            to = peers[p - 1]
            x_in[b, p] = remote(
                (pk_v, pv_v)[w].at[:, columns_at(to, hd, count)], kv[b].at[MAX_SPREAD, mine],
                x_send.at[b, p - 1], x_recv.at[b, p - 1], head=to)
            x_in[b, p].start()

    y_in_copies = {}

    def to_neighbours(b, piece, at):
        for i, o in enumerate(offsets):
            copy = remote(
                kv[b].at[MAX_SPREAD, at], kv[b].at[MAX_SPREAD - o, at],
                y_send.at[b, piece, i], y_recv.at[b, piece, i], dp=near[i])
            y_in_copies[b, piece, i] = copy
            copy.start()

    def forward(b, piece):
        if piece > 0:
            x_in[b, piece].wait_recv()
        source = lax.rem(h + heads - piece, heads)
        to_neighbours(b, piece, pl.ds(pl.multiple_of(source * span, span), span))

    def forward_whole(b):
        for p in order:
            x_in[b, p].wait_recv()
        to_neighbours(b, 0, pl.ds(0, PLEN))

    def arrived(b):
        for key, copy in y_in_copies.items():
            if key[0] == b:
                copy.wait_recv()

    def rows_of(s):
        return slice(s * rows, (s + 1) * rows)

    def columns(hd):
        first = hd * group
        return [slice((first + g) * HEAD_SIZE, (first + g + 1) * HEAD_SIZE) for g in range(group)]

    def stacked(ref, hd, s):
        return jnp.concatenate([ref[rows_of(s), col] for col in columns(hd)], axis=0)

    def relative(s):
        return lax.rem(rprompt_ref[s] - me + (devices + MAX_SPREAD), devices)

    def prompt_part(hd, w, s):
        rel = jnp.minimum(relative(s), REACH - 1)
        if w == 1:
            return kv[1 + hd][rel]
        return kv[0][rel, :, hd * HEAD_SIZE:(hd + 1) * HEAD_SIZE]

    def answer_part(hd, w, s):
        return (ak_v, av_v)[w][rows_of(s), hd * HEAD_SIZE:(hd + 1) * HEAD_SIZE]

    def answer_scores(hd, s):
        seen = lax.broadcasted_iota(jnp.int32, (rows, lanes), 0) <= (
            lax.broadcasted_iota(jnp.int32, (rows, lanes), 1) & (rows - 1))
        scores = dot(answer_part(hd, 0, s), stacked(q_v, hd, s), NT)
        st_v[hd, s] = jnp.where(seen, scores, -jnp.inf)
        gt_v[hd, s] = dot(answer_part(hd, 1, s), stacked(do_v, hd, s), NT)

    def probabilities(hd, s):
        psize = plen_ref[rprompt_ref[s]]
        rlen = rlen_ref[s]
        live = ((lax.broadcasted_iota(jnp.int32, (1, lanes), 1) & (rows - 1)) < rlen).astype(F32)
        seen = lax.broadcasted_iota(jnp.int32, (PLEN, lanes), 0) < psize
        scores = dot(prompt_part(hd, 0, s), stacked(q_v, hd, s), NT)
        masked = jnp.concatenate([jnp.where(seen, scores, -jnp.inf), st_v[hd, s]], axis=0)
        top = jnp.max(masked, axis=0, keepdims=True)
        e = jnp.exp2((masked - top) * (SCALING * math.log2(math.e)))
        prob = e * (live / jnp.sum(e, axis=0, keepdims=True))
        p_v[hd, s] = prob
        weights = prob.astype(BF16)
        w_v[hd, s] = weights
        part[0][s, :, hd * HEAD_SIZE:(hd + 1) * HEAD_SIZE] = dot(
            weights[:PLEN], stacked(do_v, hd, s), NN)

    def gradients(hd, s):
        prob = p_v[hd, s]
        gprob = jnp.concatenate([
            dot(prompt_part(hd, 1, s), stacked(do_v, hd, s), NT), gt_v[hd, s]], axis=0)
        delta = jnp.sum(prob * gprob, axis=0, keepdims=True)
        gscores = (prob * (gprob - delta)).astype(BF16)
        ds_v[hd, s] = gscores
        part[1 + hd][s] = dot(gscores[:PLEN], stacked(q_v, hd, s), NN) * SCALING

    def row_outputs(hd, s):
        keys_t = jnp.concatenate([prompt_part(hd, 0, s), answer_part(hd, 0, s)], axis=0).T
        values_t = jnp.concatenate([prompt_part(hd, 1, s), answer_part(hd, 1, s)], axis=0).T
        out = dot(values_t, w_v[hd, s], NN).astype(BF16).T
        dq = (dot(keys_t, ds_v[hd, s], NN) * SCALING).astype(BF16).T
        for g, col in enumerate(columns(hd)):
            o_v[rows_of(s), col] = out[g * rows:(g + 1) * rows]
            dq_v[rows_of(s), col] = dq[g * rows:(g + 1) * rows]
        cols = slice(hd * HEAD_SIZE, (hd + 1) * HEAD_SIZE)
        gav_v[rows_of(s), cols] = dot(
            w_v[hd, s, PLEN:], stacked(do_v, hd, s), NN).astype(BF16)
        gak_v[rows_of(s), cols] = (dot(
            ds_v[hd, s, PLEN:], stacked(q_v, hd, s), NN) * SCALING).astype(BF16)

    def block_rows(p):
        return pl.ds(pl.multiple_of(lax.rem(h + p, heads) * span, span), span)

    back_y, back_x, back_own = [], [], []
    for b, (w, hd, count) in enumerate(outward):
        back_y.append([
            remote(y_out[b].at[i], y_in[b].at[i], by_send.at[b, i], by_recv.at[b, i], dp=near[i])
            for i in range(len(near))
        ])
        dst = (gpk_out, gpv_out)[w].at[:, columns_at(h, hd, count)]
        back_x.append([
            remote(x_out[b].at[block_rows(p)], dst, bx_send.at[b, p - 1], bx_recv.at[b, p - 1],
                   head=peers[p - 1]) for p in order
        ])
        back_own.append(pltpu.make_async_copy(x_out[b].at[mine], dst, bx_own.at[b]))

    def summed(b, o):
        total = None
        for s in range(slots):
            term = part[b][s] * picks[s, o]
            total = term if total is None else total + term
        return total

    def send_back(b):
        for i, o in enumerate(offsets):
            y_out[b][i] = summed(b, o).astype(BF16)
            back_y[b][i].start()
        own[b][...] = summed(b, 0)

    def take_back(b):
        for copy in back_y[b]:
            copy.wait_recv()
        for p, copy in zip(order + [0], back_x[b] + [back_own[b]]):
            at = block_rows(p)
            total = own[b][at]
            for i in range(len(near)):
                total = total + y_in[b][i, at].astype(F32)
            x_out[b][at] = total.astype(BF16)
            copy.start()

    def each_slot(work, hd):
        for s in range(slots):
            work(hd, s)

    count_in = len(inward)
    exchange(0)
    forward(0, 0)
    for b in range(1, count_in):
        exchange(b)
    forward(1, 0)
    for b in range(2):
        for p in order:
            forward(b, p)
    for b in range(2, count_in):
        forward_whole(b)
    for load in loads:
        load.wait()
    picks = {
        (s, o): jnp.where(relative(s) == MAX_SPREAD + o, 1.0, 0.0).astype(F32)
        for s in range(slots) for o in offsets + [0]
    }
    for hd in range(kvh):
        each_slot(answer_scores, hd)

    arrived(0)
    for hd in range(kvh):
        each_slot(probabilities, hd)
    send_back(0)
    for hd in range(kvh):
        arrived(1 + hd)
        each_slot(gradients, hd)
        send_back(1 + hd)

    for hd in range(kvh - 1):
        each_slot(row_outputs, hd)
    for b in range(len(outward) - 1):
        take_back(b)
    row_outputs(kvh - 1, 0)
    take_back(len(outward) - 1)
    for s in range(1, slots):
        row_outputs(kvh - 1, s)

    for copy in [*x_in.values(), *y_in_copies.values()]:
        copy.wait_send()
    for b in range(len(outward)):
        for copy in back_y[b]:
            copy.wait_send()
        for copy in back_x[b]:
            copy.wait()
        back_own[b].wait()


def finish(o, dq, gak, gav, gpk, gpv, o_out, dq_out, gak_out, gav_out, gpk_out, gpv_out,
           wide_k, wide_v, sem):
    copies = [
        pltpu.make_async_copy(src, dst, sem.at[i])
        for i, (src, dst) in enumerate(
            [(o, o_out), (dq, dq_out), (gak, gak_out), (gav, gav_out),
             (wide_k, gpk_out.at[0]), (wide_v, gpv_out.at[0])])
    ]
    for copy in copies[:4]:
        copy.start()
    wide_k[...] = gpk[...].astype(F32)
    copies[4].start()
    wide_v[...] = gpv[...].astype(F32)
    copies[5].start()
    for copy in copies:
        copy.wait()


def on_device(queries, answer_keys, answer_values, prompt_keys, prompt_values,
              output_gradient, prompt_len, response_len, response_prompt):
    devices, heads = lax.axis_size("dp"), lax.axis_size("head")
    slots = response_len.shape[0]
    token_rows, q_width = queries.shape
    rows = token_rows // slots
    width = answer_keys.shape[1]
    kvh = width // HEAD_SIZE
    group = q_width // width
    lanes = group * rows
    span, full = prompt_keys.shape[1:]
    dma = pltpu.SemaphoreType.DMA
    anywhere = pl.BlockSpec(memory_space=pl.ANY)
    hbm = pl.BlockSpec(memory_space=pltpu.HBM)
    vmem = pl.BlockSpec(memory_space=pltpu.VMEM)
    vm, sm = pltpu.VMEM, pltpu.SMEM
    wide = vm((token_rows, q_width), BF16)
    narrow = vm((token_rows, width), BF16)
    square = (PLEN + rows, lanes)
    scratch = [
        sm(prompt_len.shape, jnp.int32), sm(response_len.shape, jnp.int32),
        sm(response_prompt.shape, jnp.int32),
        wide, wide, narrow, narrow, vm((kvh, slots) + square, F32),
        vm((kvh, slots) + square, BF16), vm((kvh, slots) + square, BF16),
        vm((span, full), BF16), vm((span, full), BF16),
        vm((kvh, slots, rows, lanes), F32), vm((kvh, slots, rows, lanes), F32),
    ]
    shapes = [(PLEN, width)] + [(PLEN, HEAD_SIZE)] * kvh
    scratch += [vm((REACH,) + shape, BF16) for shape in shapes]
    for lead, kind in [((slots,), F32), ((REACH - 1,), BF16), ((REACH - 1,), BF16),
                       ((), F32), ((), BF16)]:
        scratch += [vm(lead + shape, kind) for shape in shapes]
    scratch += [
        dma((7,)),
        dma((kvh + 1, heads - 1)), dma((kvh + 1, heads - 1)), dma((2,)),
        dma((kvh + 1, heads, REACH - 1)), dma((kvh + 1, heads, REACH - 1)),
        dma((kvh + 1, REACH - 1)), dma((kvh + 1, REACH - 1)),
        dma((kvh + 1, heads - 1)), dma((kvh + 1, heads - 1)), dma((kvh + 1,)),
    ]
    sds = jax.ShapeDtypeStruct
    rows_out = [
        sds((token_rows, q_width), BF16), sds((token_rows, q_width), BF16),
        sds((token_rows, width), BF16), sds((token_rows, width), BF16),
    ]
    results = pl.pallas_call(
        functools.partial(kernel, (devices, heads, slots, rows, kvh, group)),
        out_shape=rows_out + [sds((span, full), BF16), sds((span, full), BF16)],
        in_specs=[hbm] * 9,
        out_specs=[vmem] * 4 + [anywhere] * 2,
        scratch_shapes=scratch,
        compiler_params=pltpu.CompilerParams(
            collective_id=0, has_side_effects=True, vmem_limit_bytes=48 * 1024 * 1024),
    )(*[pltpu.with_memory_space_constraint(x, pltpu.HBM) for x in (
        prompt_len, response_len, response_prompt, queries, output_gradient,
        answer_keys, answer_values, prompt_keys.reshape(span, full),
        prompt_values.reshape(span, full))])
    return pl.pallas_call(
        finish,
        out_shape=rows_out + [sds((1, span, full), F32), sds((1, span, full), F32)],
        in_specs=[vmem] * 6,
        out_specs=[anywhere] * 6,
        scratch_shapes=[vm((span, full), F32), vm((span, full), F32), dma((6,))],
        compiler_params=pltpu.CompilerParams(vmem_limit_bytes=4 * 1024 * 1024),
    )(*[pltpu.with_memory_space_constraint(x, pltpu.VMEM) for x in results])


def solution(mesh):
    in_specs = (
        P("dp", "head"),
        P("dp", "head"),
        P("dp", "head"),
        P("dp", "head", None),
        P("dp", "head", None),
        P("dp", "head"),
        P(),
        P("dp"),
        P("dp"),
    )
    out_specs = (
        P("dp", "head"),
        P("dp", "head"),
        P("dp", "head"),
        P("dp", "head"),
        P("dp", "head", None),
        P("dp", "head", None),
    )
    return jax.shard_map(
        on_device, mesh=mesh, in_specs=in_specs, out_specs=out_specs, check_vma=False
    )
```

```python
import functools
import math

import jax
import jax.numpy as jnp
from jax import lax
from jax.experimental import pallas as pl
from jax.experimental.pallas import tpu as pltpu
from jax.sharding import PartitionSpec as P

HEAD_SIZE = 128
PLEN = 256
MAX_SPREAD = 2
REACH = 2 * MAX_SPREAD + 1
MESH = pl.DeviceIdType.MESH
SCALING = 1.0 / math.sqrt(HEAD_SIZE)
F32 = jnp.float32
BF16 = jnp.bfloat16


def dot(a, b, dims):
    return lax.dot_general(a, b, (dims, ((), ())), preferred_element_type=F32)


NN = ((1,), (0,))
NT = ((1,), (1,))
TN = ((0,), (0,))


def kernel(sizes, *refs):
    devices, heads, slots, rows, kvh, group = sizes
    pairs = [(hd, w) for hd in range(kvh) for w in range(2)]
    bundles = [[(0, 0)], [(0, 1)]] + [[(hd, 0), (hd, 1)] for hd in range(1, kvh)]
    place = {pair: (b, j) for b, bundle in enumerate(bundles) for j, pair in enumerate(bundle)}
    refs = list(refs)
    (plen_hbm, rlen_hbm, rprompt_hbm, q_hbm, do_hbm, ak_hbm, av_hbm, pk_hbm, pv_hbm,
     o_v, dq_v, gak_v, gav_v, gpk_out, gpv_out,
     plen_ref, rlen_ref, rprompt_ref,
     q_v, do_v, ak_v, av_v, p_v, w_v, ds_v, pk_v, pv_v, s_v) = refs[:28]
    kv, refs = refs[28:28 + len(bundles)], refs[28 + len(bundles):]
    (part, y_out, y_in, own, x_out) = [
        dict(zip(pairs, refs[i * len(pairs):(i + 1) * len(pairs)])) for i in range(5)
    ]
    (in_sem, x_send, x_recv, x_own, y_send, y_recv,
     by_send, by_recv, bx_send, bx_recv, bx_own) = refs[5 * len(pairs):]

    me = lax.axis_index("dp")
    h = lax.axis_index("head")
    offsets = [-2, 2, -1, 1]
    near = [lax.rem(me + devices + o, devices) for o in offsets]
    span = PLEN // heads
    width = kvh * HEAD_SIZE
    lanes = group * rows
    peers = [lax.rem(h + p, heads) for p in range(1, heads)]
    order = [p for p in range(1, heads) if p != heads // 2] + [heads // 2]
    mine = pl.ds(pl.multiple_of(h * span, span), span)

    prompt_loads = [
        pltpu.make_async_copy(src, dst, x_own.at[i])
        for i, (src, dst) in enumerate([(pk_hbm, pk_v), (pv_hbm, pv_v)])
    ]
    loads = [
        pltpu.make_async_copy(src, dst, in_sem.at[i])
        for i, (src, dst) in enumerate(
            [(q_hbm, q_v), (do_hbm, do_v), (ak_hbm, ak_v), (av_hbm, av_v),
             (plen_hbm, plen_ref), (rlen_hbm, rlen_ref), (rprompt_hbm, rprompt_ref)])
    ]
    for load in prompt_loads + loads:
        load.start()

    def remote(src, dst, send, recv, **where):
        return pltpu.make_async_remote_copy(
            src_ref=src, dst_ref=dst, send_sem=send, recv_sem=recv,
            device_id=where, device_id_type=MESH)

    barrier = pltpu.get_barrier_semaphore()
    for p in peers:
        pl.semaphore_signal(barrier, inc=1, device_id={"head": p}, device_id_type=MESH)
    for d in near:
        pl.semaphore_signal(barrier, inc=1, device_id={"dp": d}, device_id_type=MESH)
    for load in prompt_loads:
        load.wait()
    for hd, w in pairs:
        b, j = place[hd, w]
        cols = pl.ds(pl.multiple_of(h * width + hd * HEAD_SIZE, HEAD_SIZE), HEAD_SIZE)
        kv[b][MAX_SPREAD, j, mine] = (pk_v, pv_v)[w][:, cols]
    pl.semaphore_wait(barrier, len(peers) + len(near))

    x_in = {}

    def exchange(hd, w):
        b, j = place[hd, w]
        for p in order:
            to = peers[p - 1]
            cols = pl.ds(pl.multiple_of(to * width + hd * HEAD_SIZE, HEAD_SIZE), HEAD_SIZE)
            x_in[hd, w, p] = remote(
                (pk_v, pv_v)[w].at[:, cols], kv[b].at[MAX_SPREAD, j, mine],
                x_send.at[hd, w, p - 1], x_recv.at[hd, w, p - 1], head=to)
            x_in[hd, w, p].start()

    y_in_copies = {}

    def forward(b, piece):
        if piece > 0:
            for pair in bundles[b]:
                x_in[(*pair, piece)].wait_recv()
        source = lax.rem(h + heads - piece, heads)
        at = pl.ds(pl.multiple_of(source * span, span), span)
        for i, o in enumerate(offsets):
            copy = remote(
                kv[b].at[MAX_SPREAD, :, at], kv[b].at[MAX_SPREAD - o, :, at],
                y_send.at[b, piece, i], y_recv.at[b, piece, i], dp=near[i])
            y_in_copies[b, piece, i] = copy
            copy.start()

    def arrived(b):
        for piece in range(heads):
            for i in range(len(near)):
                y_in_copies[b, piece, i].wait_recv()

    def rows_of(s):
        return slice(s * rows, (s + 1) * rows)

    def columns(hd):
        first = hd * group
        return [slice((first + g) * HEAD_SIZE, (first + g + 1) * HEAD_SIZE) for g in range(group)]

    def stacked(ref, hd, s):
        return jnp.concatenate([ref[rows_of(s), col] for col in columns(hd)], axis=0)

    def relative(s):
        return lax.rem(rprompt_ref[s] - me + (devices + MAX_SPREAD), devices)

    def prompt_part(hd, w, s):
        b, j = place[hd, w]
        return kv[b][jnp.minimum(relative(s), REACH - 1), j]

    def answer_part(hd, w, s):
        return (ak_v, av_v)[w][rows_of(s), hd * HEAD_SIZE:(hd + 1) * HEAD_SIZE]

    def everything(hd, w, s):
        return jnp.concatenate([prompt_part(hd, w, s), answer_part(hd, w, s)], axis=0)

    lane_chunks = [slice(c, c + 128) for c in range(0, lanes, 128)]
    row_chunks = [slice(r, r + rows) for r in range(0, PLEN + rows, rows)]

    def probabilities(hd, s):
        psize = plen_ref[rprompt_ref[s]]
        rlen = rlen_ref[s]
        s_v[s] = dot(everything(hd, 0, s), stacked(q_v, hd, s), NT)
        column = lax.broadcasted_iota(jnp.int32, (rows, 128), 1) & (rows - 1)
        row = lax.broadcasted_iota(jnp.int32, (rows, 128), 0)
        live = (column[:1] < rlen).astype(F32)
        for at in lane_chunks:
            masked = jnp.concatenate([
                jnp.where(row < psize - r.start if r.start < PLEN else row <= column,
                          s_v[s, r, at], -jnp.inf) for r in row_chunks], axis=0)
            top = jnp.max(masked, axis=0, keepdims=True)
            e = jnp.exp2((masked - top) * (SCALING * math.log2(math.e)))
            prob = e * (live / jnp.sum(e, axis=0, keepdims=True))
            p_v[s, :, at] = prob
            w_v[hd, s, :, at] = prob.astype(BF16)
        part[hd, 1][s] = dot(w_v[hd, s, :PLEN], stacked(do_v, hd, s), NN)

    def gradients(hd, s):
        s_v[s] = dot(everything(hd, 1, s), stacked(do_v, hd, s), NT)
        for at in lane_chunks:
            delta = jnp.zeros((rows, 128), F32)
            for r in row_chunks:
                delta = delta + p_v[s, r, at] * s_v[s, r, at]
            delta = jnp.sum(delta, axis=0, keepdims=True)
            for r in row_chunks:
                ds_v[hd, s, r, at] = (p_v[s, r, at] * (s_v[s, r, at] - delta)).astype(BF16)
        part[hd, 0][s] = dot(ds_v[hd, s, :PLEN], stacked(q_v, hd, s), NN) * SCALING

    def row_outputs(hd, s):
        keys_t = everything(hd, 0, s).T
        values_t = everything(hd, 1, s).T
        out = dot(values_t, w_v[hd, s], NN).astype(BF16).T
        dq = (dot(keys_t, ds_v[hd, s], NN) * SCALING).astype(BF16).T
        for g, col in enumerate(columns(hd)):
            o_v[rows_of(s), col] = out[g * rows:(g + 1) * rows]
            dq_v[rows_of(s), col] = dq[g * rows:(g + 1) * rows]
        cols = slice(hd * HEAD_SIZE, (hd + 1) * HEAD_SIZE)
        gav_v[rows_of(s), cols] = dot(
            w_v[hd, s, PLEN:], stacked(do_v, hd, s), NN).astype(BF16)
        gak_v[rows_of(s), cols] = (dot(
            ds_v[hd, s, PLEN:], stacked(q_v, hd, s), NN) * SCALING).astype(BF16)

    back_y, back_x, back_own = {}, {}, {}
    for hd, w in pairs:
        pair = hd, w
        back_y[pair] = [
            remote(y_out[pair].at[i], y_in[pair].at[i], by_send.at[hd, w, i],
                   by_recv.at[hd, w, i], dp=near[i]) for i in range(len(near))
        ]
        dst = (gpk_out, gpv_out)[w]
        cols = pl.ds(pl.multiple_of(h * width + hd * HEAD_SIZE, HEAD_SIZE), HEAD_SIZE)
        back_x[pair] = []
        for p in order:
            to = peers[p - 1]
            theirs = pl.ds(pl.multiple_of(to * span, span), span)
            back_x[pair].append(remote(
                x_out[pair].at[theirs], dst.at[:, cols],
                bx_send.at[hd, w, p - 1], bx_recv.at[hd, w, p - 1], head=to))
        back_own[pair] = pltpu.make_async_copy(
            x_out[pair].at[mine], dst.at[:, cols], bx_own.at[hd, w])

    last = kvh - 1, 0

    def block_rows(p):
        return pl.ds(pl.multiple_of(lax.rem(h + p, heads) * span, span), span)

    def send_back(pair):
        for i, o in enumerate(offsets + [0]):
            for r in row_chunks[:-1]:
                total = None
                for s in range(slots):
                    term = part[pair][s, r] * picks[s, o]
                    total = term if total is None else total + term
                if o == 0:
                    own[pair][r] = total
                else:
                    y_out[pair][i, r] = total.astype(BF16)
            if o != 0:
                back_y[pair][i].start()

    def take_back(pair):
        for copy in back_y[pair]:
            copy.wait_recv()
        for p, copy in zip(order + [0], back_x[pair] + [back_own[pair]]):
            at = block_rows(p)
            total = own[pair][at]
            for i in range(len(near)):
                total = total + y_in[pair][i, at].astype(F32)
            x_out[pair][at] = total.astype(BF16)
            copy.start()

    def each_slot(work, hd):
        for s in range(slots):
            work(hd, s)

    exchange(*pairs[0])
    forward(0, 0)
    for pair in pairs[1:]:
        exchange(*pair)
    for b in range(1, len(bundles)):
        forward(b, 0)
    for b in range(len(bundles)):
        for p in order:
            forward(b, p)
    for load in loads:
        load.wait()
    picks = {
        (s, o): jnp.where(relative(s) == MAX_SPREAD + o, 1.0, 0.0).astype(F32)
        for s in range(slots) for o in offsets + [0]
    }

    for hd in range(kvh):
        arrived(hd + 1 if hd > 0 else 0)
        each_slot(probabilities, hd)
        send_back((hd, 1))
        if hd == 0:
            arrived(1)
        each_slot(gradients, hd)
        send_back((hd, 0))

    for hd in range(kvh - 1):
        each_slot(row_outputs, hd)
        take_back((hd, 1))
        take_back((hd, 0))
    take_back((kvh - 1, 1))
    row_outputs(kvh - 1, 0)
    take_back(last)
    for s in range(1, slots):
        row_outputs(kvh - 1, s)

    for pair in pairs:
        for p in order:
            x_in[(*pair, p)].wait_send()
        for copy in back_y[pair]:
            copy.wait_send()
        for copy in back_x[pair]:
            copy.wait()
        back_own[pair].wait()
    for copy in y_in_copies.values():
        copy.wait_send()


def finish(o, dq, gak, gav, gpk, gpv, o_out, dq_out, gak_out, gav_out, gpk_out, gpv_out,
           wide_k, wide_v, sem):
    copies = [
        pltpu.make_async_copy(src, dst, sem.at[i])
        for i, (src, dst) in enumerate(
            [(o, o_out), (dq, dq_out), (gak, gak_out), (gav, gav_out),
             (wide_k, gpk_out.at[0]), (wide_v, gpv_out.at[0])])
    ]
    for copy in copies[:4]:
        copy.start()
    wide_k[...] = gpk[...].astype(F32)
    copies[4].start()
    wide_v[...] = gpv[...].astype(F32)
    copies[5].start()
    for copy in copies:
        copy.wait()


def on_device(queries, answer_keys, answer_values, prompt_keys, prompt_values,
              output_gradient, prompt_len, response_len, response_prompt):
    devices, heads = lax.axis_size("dp"), lax.axis_size("head")
    slots = response_len.shape[0]
    token_rows, q_width = queries.shape
    rows = token_rows // slots
    width = answer_keys.shape[1]
    kvh = width // HEAD_SIZE
    group = q_width // width
    lanes = group * rows
    span, full = prompt_keys.shape[1:]
    dma = pltpu.SemaphoreType.DMA
    anywhere = pl.BlockSpec(memory_space=pl.ANY)
    hbm = pl.BlockSpec(memory_space=pltpu.HBM)
    vmem = pl.BlockSpec(memory_space=pltpu.VMEM)
    vm, sm = pltpu.VMEM, pltpu.SMEM
    block = (PLEN, HEAD_SIZE)
    wide = vm((token_rows, q_width), BF16)
    narrow = vm((token_rows, width), BF16)
    square = (PLEN + rows, lanes)
    bundle = [1, 1] + [2] * (kvh - 1)
    scratch = [
        sm(prompt_len.shape, jnp.int32), sm(response_len.shape, jnp.int32),
        sm(response_prompt.shape, jnp.int32),
        wide, wide, narrow, narrow, vm((slots,) + square, F32),
        vm((kvh, slots) + square, BF16), vm((kvh, slots) + square, BF16),
        vm((span, full), BF16), vm((span, full), BF16),
        vm((slots,) + square, F32),
    ]
    scratch += [vm((REACH, count) + block, BF16) for count in bundle]
    for shape in [vm((slots,) + block, F32), vm((REACH - 1,) + block, BF16),
                  vm((REACH - 1,) + block, BF16), vm(block, F32), vm(block, BF16)]:
        scratch += [shape] * (kvh * 2)
    scratch += [
        dma((7,)),
        dma((kvh, 2, heads - 1)), dma((kvh, 2, heads - 1)), dma((2,)),
        dma((kvh + 1, heads, REACH - 1)), dma((kvh + 1, heads, REACH - 1)),
        dma((kvh, 2, REACH - 1)), dma((kvh, 2, REACH - 1)),
        dma((kvh, 2, heads - 1)), dma((kvh, 2, heads - 1)), dma((kvh, 2)),
    ]
    sds = jax.ShapeDtypeStruct
    rows_out = [
        sds((token_rows, q_width), BF16), sds((token_rows, q_width), BF16),
        sds((token_rows, width), BF16), sds((token_rows, width), BF16),
    ]
    results = pl.pallas_call(
        functools.partial(kernel, (devices, heads, slots, rows, kvh, group)),
        out_shape=rows_out + [sds((span, full), BF16), sds((span, full), BF16)],
        in_specs=[hbm] * 9,
        out_specs=[vmem] * 4 + [anywhere] * 2,
        scratch_shapes=scratch,
        compiler_params=pltpu.CompilerParams(
            collective_id=0, has_side_effects=True, vmem_limit_bytes=48 * 1024 * 1024),
    )(*[pltpu.with_memory_space_constraint(x, pltpu.HBM) for x in (
        prompt_len, response_len, response_prompt, queries, output_gradient,
        answer_keys, answer_values, prompt_keys.reshape(span, full),
        prompt_values.reshape(span, full))])
    return pl.pallas_call(
        finish,
        out_shape=rows_out + [sds((1, span, full), F32), sds((1, span, full), F32)],
        in_specs=[vmem] * 6,
        out_specs=[anywhere] * 6,
        scratch_shapes=[vm((span, full), F32), vm((span, full), F32), dma((6,))],
        compiler_params=pltpu.CompilerParams(vmem_limit_bytes=4 * 1024 * 1024),
    )(*[pltpu.with_memory_space_constraint(x, pltpu.VMEM) for x in results])


def solution(mesh):
    in_specs = (
        P("dp", "head"),
        P("dp", "head"),
        P("dp", "head"),
        P("dp", "head", None),
        P("dp", "head", None),
        P("dp", "head"),
        P(),
        P("dp"),
        P("dp"),
    )
    out_specs = (
        P("dp", "head"),
        P("dp", "head"),
        P("dp", "head"),
        P("dp", "head"),
        P("dp", "head", None),
        P("dp", "head", None),
    )
    return jax.shard_map(
        on_device, mesh=mesh, in_specs=in_specs, out_specs=out_specs, check_vma=False
    )
```

```python
import functools
import math

import jax
import jax.numpy as jnp
from jax import lax
from jax.experimental import pallas as pl
from jax.experimental.pallas import tpu as pltpu
from jax.sharding import PartitionSpec as P

HEAD_SIZE = 128
PLEN = 256
MAX_SPREAD = 2
REACH = 2 * MAX_SPREAD + 1
MESH = pl.DeviceIdType.MESH
SCALING = 1.0 / math.sqrt(HEAD_SIZE)
F32 = jnp.float32
BF16 = jnp.bfloat16


def dot(a, b, dims):
    return lax.dot_general(a, b, (dims, ((), ())), preferred_element_type=F32)


NN = ((1,), (0,))
NT = ((1,), (1,))
TN = ((0,), (0,))


def kernel(sizes, *refs):
    devices, heads, slots, rows, kvh, group = sizes
    pairs = [(hd, w) for hd in range(kvh) for w in range(2)]
    bundles = [[(0, 0)], [(0, 1)]] + [[(hd, 0), (hd, 1)] for hd in range(1, kvh)]
    place = {pair: (b, j) for b, bundle in enumerate(bundles) for j, pair in enumerate(bundle)}
    refs = list(refs)
    (plen_hbm, rlen_hbm, rprompt_hbm, q_hbm, do_hbm, ak_hbm, av_hbm, pk_hbm, pv_hbm,
     o_v, dq_v, gak_v, gav_v, gpk_out, gpv_out,
     plen_ref, rlen_ref, rprompt_ref,
     q_v, do_v, ak_v, av_v, p_v, w_v, ds_v, pk_v, pv_v) = refs[:27]
    kv, refs = refs[27:27 + len(bundles)], refs[27 + len(bundles):]
    (part, y_out, y_in, own, x_out) = [
        dict(zip(pairs, refs[i * len(pairs):(i + 1) * len(pairs)])) for i in range(5)
    ]
    (in_sem, x_send, x_recv, x_own, y_send, y_recv,
     by_send, by_recv, bx_send, bx_recv, bx_own) = refs[5 * len(pairs):]

    me = lax.axis_index("dp")
    h = lax.axis_index("head")
    offsets = [-2, 2, -1, 1]
    near = [lax.rem(me + devices + o, devices) for o in offsets]
    span = PLEN // heads
    width = kvh * HEAD_SIZE
    lanes = group * rows
    chunk = min(512, lanes)
    per = chunk // rows
    all_rows = PLEN + rows
    peers = [lax.rem(h + p, heads) for p in range(1, heads)]
    order = [p for p in range(1, heads) if p != heads // 2] + [heads // 2]
    mine = pl.ds(pl.multiple_of(h * span, span), span)

    prompt_loads = [
        pltpu.make_async_copy(src, dst, x_own.at[i])
        for i, (src, dst) in enumerate([(pk_hbm, pk_v), (pv_hbm, pv_v)])
    ]
    loads = [
        pltpu.make_async_copy(src, dst, in_sem.at[i])
        for i, (src, dst) in enumerate(
            [(q_hbm, q_v), (do_hbm, do_v), (ak_hbm, ak_v), (av_hbm, av_v),
             (plen_hbm, plen_ref), (rlen_hbm, rlen_ref), (rprompt_hbm, rprompt_ref)])
    ]
    for load in prompt_loads + loads:
        load.start()

    def remote(src, dst, send, recv, **where):
        return pltpu.make_async_remote_copy(
            src_ref=src, dst_ref=dst, send_sem=send, recv_sem=recv,
            device_id=where, device_id_type=MESH)

    barrier = pltpu.get_barrier_semaphore()
    for p in peers:
        pl.semaphore_signal(barrier, inc=1, device_id={"head": p}, device_id_type=MESH)
    for d in near:
        pl.semaphore_signal(barrier, inc=1, device_id={"dp": d}, device_id_type=MESH)
    for load in prompt_loads:
        load.wait()
    for hd, w in pairs:
        b, j = place[hd, w]
        cols = pl.ds(pl.multiple_of(h * width + hd * HEAD_SIZE, HEAD_SIZE), HEAD_SIZE)
        kv[b][MAX_SPREAD, j, mine] = (pk_v, pv_v)[w][:, cols]
    pl.semaphore_wait(barrier, len(peers) + len(near))

    x_in = {}

    def exchange(hd, w):
        b, j = place[hd, w]
        for p in order:
            to = peers[p - 1]
            cols = pl.ds(pl.multiple_of(to * width + hd * HEAD_SIZE, HEAD_SIZE), HEAD_SIZE)
            x_in[hd, w, p] = remote(
                (pk_v, pv_v)[w].at[:, cols], kv[b].at[MAX_SPREAD, j, mine],
                x_send.at[hd, w, p - 1], x_recv.at[hd, w, p - 1], head=to)
            x_in[hd, w, p].start()

    y_in_copies = {}

    def forward(b, piece):
        if piece > 0:
            for pair in bundles[b]:
                x_in[(*pair, piece)].wait_recv()
        source = lax.rem(h + heads - piece, heads)
        at = pl.ds(pl.multiple_of(source * span, span), span)
        for i, o in enumerate(offsets):
            copy = remote(
                kv[b].at[MAX_SPREAD, :, at], kv[b].at[MAX_SPREAD - o, :, at],
                y_send.at[b, piece, i], y_recv.at[b, piece, i], dp=near[i])
            y_in_copies[b, piece, i] = copy
            copy.start()

    def arrived(b):
        for piece in range(heads):
            for i in range(len(near)):
                y_in_copies[b, piece, i].wait_recv()

    exchange(*pairs[0])
    forward(0, 0)
    for pair in pairs[1:]:
        exchange(*pair)
    for b in range(1, len(bundles)):
        forward(b, 0)
    for b in range(len(bundles)):
        for p in order:
            forward(b, p)
    for load in loads:
        load.wait()

    def rows_of(s):
        return slice(s * rows, (s + 1) * rows)

    def columns(hd, c):
        first = hd * group + c * per
        return [slice((first + g) * HEAD_SIZE, (first + g + 1) * HEAD_SIZE) for g in range(per)]

    def stacked(ref, hd, s, c):
        return jnp.concatenate([ref[rows_of(s), col] for col in columns(hd, c)], axis=0)

    def relative(s):
        return lax.rem(rprompt_ref[s] - me + (devices + MAX_SPREAD), devices)

    def both(hd, w, s):
        rel = jnp.minimum(relative(s), REACH - 1)
        tail = (ak_v, av_v)[w][rows_of(s), hd * HEAD_SIZE:(hd + 1) * HEAD_SIZE]
        b, j = place[hd, w]
        return jnp.concatenate([kv[b][rel, j], tail], axis=0)

    def lanes_of(c):
        return slice(c * chunk, (c + 1) * chunk)

    def probabilities(hd, s):
        psize = plen_ref[rprompt_ref[s]]
        rlen = rlen_ref[s]
        keys = both(hd, 0, s)
        live = ((lax.broadcasted_iota(jnp.int32, (1, chunk), 1) & (rows - 1)) < rlen).astype(F32)
        head_seen = lax.broadcasted_iota(jnp.int32, (PLEN, chunk), 0) < psize
        tail_seen = lax.broadcasted_iota(jnp.int32, (rows, chunk), 0) <= (
            lax.broadcasted_iota(jnp.int32, (rows, chunk), 1) & (rows - 1))
        dv = jnp.zeros((all_rows, HEAD_SIZE), F32)
        for c in range(lanes // chunk):
            scores = dot(keys, stacked(q_v, hd, s, c), NT)
            masked = jnp.concatenate([
                jnp.where(head_seen, scores[:PLEN], -jnp.inf),
                jnp.where(tail_seen, scores[PLEN:], -jnp.inf)], axis=0)
            top = jnp.max(masked, axis=0, keepdims=True)
            e = jnp.exp2((masked - top) * (SCALING * math.log2(math.e)))
            prob = e * (live / jnp.sum(e, axis=0, keepdims=True))
            p_v[s, :, lanes_of(c)] = prob
            weights = prob.astype(BF16)
            w_v[hd, s, :, lanes_of(c)] = weights
            dv += dot(weights, stacked(do_v, hd, s, c), NN)
        part[hd, 1][s] = dv[:PLEN]
        gav_v[rows_of(s), hd * HEAD_SIZE:(hd + 1) * HEAD_SIZE] = dv[PLEN:].astype(BF16)

    def gradients(hd, s):
        values = both(hd, 1, s)
        dk = jnp.zeros((all_rows, HEAD_SIZE), F32)
        for c in range(lanes // chunk):
            prob = p_v[s, :, lanes_of(c)]
            gprob = dot(values, stacked(do_v, hd, s, c), NT)
            delta = jnp.sum(prob * gprob, axis=0, keepdims=True)
            gscores = (prob * (gprob - delta)).astype(BF16)
            ds_v[hd, s, :, lanes_of(c)] = gscores
            dk += dot(gscores, stacked(q_v, hd, s, c), NN)
        dk = dk * SCALING
        part[hd, 0][s] = dk[:PLEN]
        gak_v[rows_of(s), hd * HEAD_SIZE:(hd + 1) * HEAD_SIZE] = dk[PLEN:].astype(BF16)

    def row_outputs(hd, s):
        keys_t = both(hd, 0, s).T
        values_t = both(hd, 1, s).T
        for c in range(lanes // chunk):
            out = dot(values_t, w_v[hd, s, :, lanes_of(c)], NN).astype(BF16).T
            dq = (dot(keys_t, ds_v[hd, s, :, lanes_of(c)], NN) * SCALING).astype(BF16).T
            for g, col in enumerate(columns(hd, c)):
                o_v[rows_of(s), col] = out[g * rows:(g + 1) * rows]
                dq_v[rows_of(s), col] = dq[g * rows:(g + 1) * rows]

    def summed(pair, offset):
        total = None
        for s in range(slots):
            pick = jnp.where(relative(s) == offset, 1.0, 0.0).astype(F32)
            term = part[pair][s] * pick
            total = term if total is None else total + term
        return total

    last = kvh - 1, 0
    core = lax.rem(me, 2)
    sibling = me + 1 - 2 * core
    direct_to = lax.rem(me + devices - 2 + 4 * core, devices)
    relay_to = lax.rem(me + devices + 2 - 4 * core, devices)
    back_y, back_x, back_own = {}, {}, {}
    for hd, w in pairs:
        pair = hd, w
        if pair == last:
            back_y[pair] = [
                remote(y_out[pair].at[i], y_in[pair].at[i], by_send.at[hd, w, i],
                       by_recv.at[hd, w, i], dp=near[i]) for i in range(len(near))
            ]
        else:
            back_y[pair] = [
                remote(y_out[pair].at[core], y_in[pair].at[core], by_send.at[hd, w, 0],
                       by_recv.at[hd, w, core], dp=direct_to),
                remote(y_out[pair].at[1 - core], y_in[pair].at[1 - core], by_send.at[hd, w, 1],
                       by_recv.at[hd, w, 1 - core], dp=relay_to),
                remote(y_out[pair].at[2:4], y_in[pair].at[2:4], by_send.at[hd, w, 2],
                       by_recv.at[hd, w, 2], dp=sibling),
            ]
        dst = (gpk_out, gpv_out)[w]
        cols = pl.ds(pl.multiple_of(h * width + hd * HEAD_SIZE, HEAD_SIZE), HEAD_SIZE)
        back_x[pair] = []
        for p in order:
            to = peers[p - 1]
            theirs = pl.ds(pl.multiple_of(to * span, span), span)
            back_x[pair].append(remote(
                x_out[pair].at[theirs], dst.at[:, cols],
                bx_send.at[hd, w, p - 1], bx_recv.at[hd, w, p - 1], head=to))
        back_own[pair] = pltpu.make_async_copy(
            x_out[pair].at[mine], dst.at[:, cols], bx_own.at[hd, w])

    def send_back(pair):
        if pair == last:
            for i, o in enumerate(offsets):
                y_out[pair][i] = summed(pair, MAX_SPREAD + o).astype(BF16)
                back_y[pair][i].start()
        else:
            for i in (2, 3):
                y_out[pair][i] = summed(pair, MAX_SPREAD + offsets[i]).astype(BF16)
            back_y[pair][2].start()
            y_out[pair][core] = summed(pair, 4 * core).astype(BF16)
            back_y[pair][0].start()
        own[pair][...] = summed(pair, MAX_SPREAD)

    def relay_back(pair):
        carry = summed(pair, 4 - 4 * core)
        back_y[pair][2].wait_recv()
        y_out[pair][1 - core] = (carry + y_in[pair][3 - core].astype(F32)).astype(BF16)
        back_y[pair][1].start()

    def take_back(pair):
        if pair == last:
            for copy in back_y[pair]:
                copy.wait_recv()
            came = [0, 1, 2, 3]
        else:
            for copy in back_y[pair][:2]:
                copy.wait_recv()
            came = [0, 1, 2 + core]
        for p, copy in zip(order + [0], back_x[pair] + [back_own[pair]]):
            at = pl.ds(pl.multiple_of(lax.rem(h + p, heads) * span, span), span)
            total = own[pair][at]
            for i in came:
                total = total + y_in[pair][i, at].astype(F32)
            x_out[pair][at] = total.astype(BF16)
            copy.start()

    def each_slot(work, hd, at={}):
        for s in range(slots):
            for what, *args in at.get(s, ()):
                what(*args)
            work(hd, s)

    half = slots // 2
    for hd in range(kvh):
        arrived(hd + 1 if hd > 0 else 0)
        each_slot(probabilities, hd, {half: [(relay_back, (hd - 1, 0))]} if hd > 0 else {})
        send_back((hd, 1))
        if hd == 0:
            arrived(1)
        each_slot(gradients, hd, {half: [(relay_back, (hd, 1))]})
        send_back((hd, 0))

    end = kvh - 1
    for hd in range(kvh):
        if hd < end:
            each_slot(row_outputs, hd)
            take_back((hd, 1))
            take_back((hd, 0))
        else:
            each_slot(row_outputs, hd, {1: [(take_back, (end, 1)), (take_back, last)]})

    for pair in pairs:
        for p in order:
            x_in[(*pair, p)].wait_send()
        for copy in back_y[pair]:
            copy.wait_send()
        for copy in back_x[pair]:
            copy.wait()
        back_own[pair].wait()
    for copy in y_in_copies.values():
        copy.wait_send()


def finish(o, dq, gak, gav, gpk, gpv, o_out, dq_out, gak_out, gav_out, gpk_out, gpv_out,
           wide_k, wide_v, sem):
    copies = [
        pltpu.make_async_copy(src, dst, sem.at[i])
        for i, (src, dst) in enumerate(
            [(o, o_out), (dq, dq_out), (gak, gak_out), (gav, gav_out),
             (wide_k, gpk_out.at[0]), (wide_v, gpv_out.at[0])])
    ]
    for copy in copies[:4]:
        copy.start()
    wide_k[...] = gpk[...].astype(F32)
    copies[4].start()
    wide_v[...] = gpv[...].astype(F32)
    copies[5].start()
    for copy in copies:
        copy.wait()


def on_device(queries, answer_keys, answer_values, prompt_keys, prompt_values,
              output_gradient, prompt_len, response_len, response_prompt):
    devices, heads = lax.axis_size("dp"), lax.axis_size("head")
    slots = response_len.shape[0]
    token_rows, q_width = queries.shape
    rows = token_rows // slots
    width = answer_keys.shape[1]
    kvh = width // HEAD_SIZE
    group = q_width // width
    lanes = group * rows
    span, full = prompt_keys.shape[1:]
    dma = pltpu.SemaphoreType.DMA
    anywhere = pl.BlockSpec(memory_space=pl.ANY)
    hbm = pl.BlockSpec(memory_space=pltpu.HBM)
    vmem = pl.BlockSpec(memory_space=pltpu.VMEM)
    vm, sm = pltpu.VMEM, pltpu.SMEM
    block = (PLEN, HEAD_SIZE)
    wide = vm((token_rows, q_width), BF16)
    narrow = vm((token_rows, width), BF16)
    square = (PLEN + rows, lanes)
    bundle = [1, 1] + [2] * (kvh - 1)
    scratch = [
        sm(prompt_len.shape, jnp.int32), sm(response_len.shape, jnp.int32),
        sm(response_prompt.shape, jnp.int32),
        wide, wide, narrow, narrow, vm((slots,) + square, F32),
        vm((kvh, slots) + square, BF16), vm((kvh, slots) + square, BF16),
        vm((span, full), BF16), vm((span, full), BF16),
    ]
    scratch += [vm((REACH, count) + block, BF16) for count in bundle]
    for shape in [vm((slots,) + block, F32), vm((REACH - 1,) + block, BF16),
                  vm((REACH - 1,) + block, BF16), vm(block, F32), vm(block, BF16)]:
        scratch += [shape] * (kvh * 2)
    scratch += [
        dma((7,)),
        dma((kvh, 2, heads - 1)), dma((kvh, 2, heads - 1)), dma((2,)),
        dma((kvh + 1, heads, REACH - 1)), dma((kvh + 1, heads, REACH - 1)),
        dma((kvh, 2, REACH - 1)), dma((kvh, 2, REACH - 1)),
        dma((kvh, 2, heads - 1)), dma((kvh, 2, heads - 1)), dma((kvh, 2)),
    ]
    sds = jax.ShapeDtypeStruct
    rows_out = [
        sds((token_rows, q_width), BF16), sds((token_rows, q_width), BF16),
        sds((token_rows, width), BF16), sds((token_rows, width), BF16),
    ]
    results = pl.pallas_call(
        functools.partial(kernel, (devices, heads, slots, rows, kvh, group)),
        out_shape=rows_out + [sds((span, full), BF16), sds((span, full), BF16)],
        in_specs=[hbm] * 9,
        out_specs=[vmem] * 4 + [anywhere] * 2,
        scratch_shapes=scratch,
        compiler_params=pltpu.CompilerParams(
            collective_id=0, has_side_effects=True, vmem_limit_bytes=48 * 1024 * 1024),
    )(*[pltpu.with_memory_space_constraint(x, pltpu.HBM) for x in (
        prompt_len, response_len, response_prompt, queries, output_gradient,
        answer_keys, answer_values, prompt_keys.reshape(span, full),
        prompt_values.reshape(span, full))])
    return pl.pallas_call(
        finish,
        out_shape=rows_out + [sds((1, span, full), F32), sds((1, span, full), F32)],
        in_specs=[vmem] * 6,
        out_specs=[anywhere] * 6,
        scratch_shapes=[vm((span, full), F32), vm((span, full), F32), dma((6,))],
        compiler_params=pltpu.CompilerParams(vmem_limit_bytes=4 * 1024 * 1024),
    )(*[pltpu.with_memory_space_constraint(x, pltpu.VMEM) for x in results])


def solution(mesh):
    in_specs = (
        P("dp", "head"),
        P("dp", "head"),
        P("dp", "head"),
        P("dp", "head", None),
        P("dp", "head", None),
        P("dp", "head"),
        P(),
        P("dp"),
        P("dp"),
    )
    out_specs = (
        P("dp", "head"),
        P("dp", "head"),
        P("dp", "head"),
        P("dp", "head"),
        P("dp", "head", None),
        P("dp", "head", None),
    )
    return jax.shard_map(
        on_device, mesh=mesh, in_specs=in_specs, out_specs=out_specs, check_vma=False
    )
```

```python
import functools
import math

import jax
import jax.numpy as jnp
from jax import lax
from jax.experimental import pallas as pl
from jax.experimental.pallas import tpu as pltpu
from jax.sharding import PartitionSpec as P

HEAD_SIZE = 128
PLEN = 256
MAX_SPREAD = 2
REACH = 2 * MAX_SPREAD + 1
MESH = pl.DeviceIdType.MESH
SCALING = 1.0 / math.sqrt(HEAD_SIZE)
F32 = jnp.float32
BF16 = jnp.bfloat16


def dot(a, b, dims):
    return lax.dot_general(a, b, (dims, ((), ())), preferred_element_type=F32)


NN = ((1,), (0,))
NT = ((1,), (1,))
TN = ((0,), (0,))


def kernel(sizes, *refs):
    devices, heads, slots, rows, kvh, group = sizes
    pairs = [(hd, w) for hd in range(kvh) for w in range(2)]
    bundles = [[(0, 0)], [(0, 1)]] + [[(hd, 0), (hd, 1)] for hd in range(1, kvh)]
    place = {pair: (b, j) for b, bundle in enumerate(bundles) for j, pair in enumerate(bundle)}
    refs = list(refs)
    (plen_hbm, rlen_hbm, rprompt_hbm, q_hbm, do_hbm, ak_hbm, av_hbm, pk_hbm, pv_hbm,
     o_v, dq_v, gak_v, gav_v, gpk_out, gpv_out,
     plen_ref, rlen_ref, rprompt_ref,
     q_v, do_v, ak_v, av_v, p_v, w_v, ds_v, pk_v, pv_v) = refs[:27]
    kv, refs = refs[27:27 + len(bundles)], refs[27 + len(bundles):]
    (part, y_out, y_in, own, x_out) = [
        dict(zip(pairs, refs[i * len(pairs):(i + 1) * len(pairs)])) for i in range(5)
    ]
    (in_sem, x_send, x_recv, x_own, y_send, y_recv,
     by_send, by_recv, bx_send, bx_recv, bx_own) = refs[5 * len(pairs):]

    me = lax.axis_index("dp")
    h = lax.axis_index("head")
    offsets = [-2, 2, -1, 1]
    near = [lax.rem(me + devices + o, devices) for o in offsets]
    span = PLEN // heads
    width = kvh * HEAD_SIZE
    lanes = group * rows
    chunk = min(512, lanes)
    per = chunk // rows
    all_rows = PLEN + rows
    peers = [lax.rem(h + p, heads) for p in range(1, heads)]
    order = [p for p in range(1, heads) if p != heads // 2] + [heads // 2]
    mine = pl.ds(pl.multiple_of(h * span, span), span)

    prompt_loads = [
        pltpu.make_async_copy(src, dst, x_own.at[i])
        for i, (src, dst) in enumerate([(pk_hbm, pk_v), (pv_hbm, pv_v)])
    ]
    loads = [
        pltpu.make_async_copy(src, dst, in_sem.at[i])
        for i, (src, dst) in enumerate(
            [(q_hbm, q_v), (do_hbm, do_v), (ak_hbm, ak_v), (av_hbm, av_v),
             (plen_hbm, plen_ref), (rlen_hbm, rlen_ref), (rprompt_hbm, rprompt_ref)])
    ]
    for load in prompt_loads + loads:
        load.start()

    def remote(src, dst, send, recv, **where):
        return pltpu.make_async_remote_copy(
            src_ref=src, dst_ref=dst, send_sem=send, recv_sem=recv,
            device_id=where, device_id_type=MESH)

    barrier = pltpu.get_barrier_semaphore()
    for p in peers:
        pl.semaphore_signal(barrier, inc=1, device_id={"head": p}, device_id_type=MESH)
    for d in near:
        pl.semaphore_signal(barrier, inc=1, device_id={"dp": d}, device_id_type=MESH)
    for load in prompt_loads:
        load.wait()
    for hd, w in pairs:
        b, j = place[hd, w]
        cols = pl.ds(pl.multiple_of(h * width + hd * HEAD_SIZE, HEAD_SIZE), HEAD_SIZE)
        kv[b][MAX_SPREAD, j, mine] = (pk_v, pv_v)[w][:, cols]
    pl.semaphore_wait(barrier, len(peers) + len(near))

    x_in = {}

    def exchange(hd, w):
        b, j = place[hd, w]
        for p in order:
            to = peers[p - 1]
            cols = pl.ds(pl.multiple_of(to * width + hd * HEAD_SIZE, HEAD_SIZE), HEAD_SIZE)
            x_in[hd, w, p] = remote(
                (pk_v, pv_v)[w].at[:, cols], kv[b].at[MAX_SPREAD, j, mine],
                x_send.at[hd, w, p - 1], x_recv.at[hd, w, p - 1], head=to)
            x_in[hd, w, p].start()

    y_in_copies = {}

    def forward(b, piece):
        if piece > 0:
            for pair in bundles[b]:
                x_in[(*pair, piece)].wait_recv()
        source = lax.rem(h + heads - piece, heads)
        at = pl.ds(pl.multiple_of(source * span, span), span)
        for i, o in enumerate(offsets[:2] if b >= 2 else offsets):
            copy = remote(
                kv[b].at[MAX_SPREAD, :, at], kv[b].at[MAX_SPREAD - o, :, at],
                y_send.at[b, piece, i], y_recv.at[b, piece, i], dp=near[i])
            y_in_copies[b, piece, i] = copy
            copy.start()

    core = lax.rem(me, 2)
    sibling = me + 1 - 2 * core

    def to_sibling(b):
        y_in_copies[b, 0, 2] = remote(
            kv[b].at[MAX_SPREAD], kv[b].at[1 + 2 * core], y_send.at[b, 0, 2], y_recv.at[b, 0, 2],
            dp=sibling)
        y_in_copies[b, 0, 2].start()

    def relay_in(b):
        for piece in range(heads):
            for i in range(2):
                y_in_copies[b, piece, i].wait_recv()
        y_in_copies[b, 0, 3] = remote(
            kv[b].at[4 - 4 * core], kv[b].at[3 - 2 * core], y_send.at[b, 0, 3],
            y_recv.at[b, 0, 3], dp=sibling)
        y_in_copies[b, 0, 3].start()

    def arrived(b):
        if b >= 2:
            y_in_copies[b, 0, 2].wait_recv()
            y_in_copies[b, 0, 3].wait_recv()
            return
        for piece in range(heads):
            for i in range(len(near)):
                y_in_copies[b, piece, i].wait_recv()

    exchange(*pairs[0])
    forward(0, 0)
    for pair in pairs[1:]:
        exchange(*pair)
    for b in range(1, len(bundles)):
        forward(b, 0)
    for b in range(len(bundles)):
        for p in order:
            forward(b, p)
        if b >= 2:
            to_sibling(b)
    for load in loads:
        load.wait()

    def rows_of(s):
        return slice(s * rows, (s + 1) * rows)

    def columns(hd, c):
        first = hd * group + c * per
        return [slice((first + g) * HEAD_SIZE, (first + g + 1) * HEAD_SIZE) for g in range(per)]

    def stacked(ref, hd, s, c):
        return jnp.concatenate([ref[rows_of(s), col] for col in columns(hd, c)], axis=0)

    def relative(s):
        return lax.rem(rprompt_ref[s] - me + (devices + MAX_SPREAD), devices)

    def both(hd, w, s):
        rel = jnp.minimum(relative(s), REACH - 1)
        tail = (ak_v, av_v)[w][rows_of(s), hd * HEAD_SIZE:(hd + 1) * HEAD_SIZE]
        b, j = place[hd, w]
        return jnp.concatenate([kv[b][rel, j], tail], axis=0)

    def lanes_of(c):
        return slice(c * chunk, (c + 1) * chunk)

    def probabilities(hd, s):
        psize = plen_ref[rprompt_ref[s]]
        rlen = rlen_ref[s]
        keys = both(hd, 0, s)
        live = ((lax.broadcasted_iota(jnp.int32, (1, chunk), 1) & (rows - 1)) < rlen).astype(F32)
        head_seen = lax.broadcasted_iota(jnp.int32, (PLEN, chunk), 0) < psize
        tail_seen = lax.broadcasted_iota(jnp.int32, (rows, chunk), 0) <= (
            lax.broadcasted_iota(jnp.int32, (rows, chunk), 1) & (rows - 1))
        dv = jnp.zeros((all_rows, HEAD_SIZE), F32)
        for c in range(lanes // chunk):
            scores = dot(keys, stacked(q_v, hd, s, c), NT)
            masked = jnp.concatenate([
                jnp.where(head_seen, scores[:PLEN], -jnp.inf),
                jnp.where(tail_seen, scores[PLEN:], -jnp.inf)], axis=0)
            top = jnp.max(masked, axis=0, keepdims=True)
            e = jnp.exp2((masked - top) * (SCALING * math.log2(math.e)))
            prob = e * (live / jnp.sum(e, axis=0, keepdims=True))
            p_v[s, :, lanes_of(c)] = prob
            weights = prob.astype(BF16)
            w_v[hd, s, :, lanes_of(c)] = weights
            dv += dot(weights, stacked(do_v, hd, s, c), NN)
        part[hd, 1][s] = dv[:PLEN]
        gav_v[rows_of(s), hd * HEAD_SIZE:(hd + 1) * HEAD_SIZE] = dv[PLEN:].astype(BF16)

    def gradients(hd, s):
        values = both(hd, 1, s)
        dk = jnp.zeros((all_rows, HEAD_SIZE), F32)
        for c in range(lanes // chunk):
            prob = p_v[s, :, lanes_of(c)]
            gprob = dot(values, stacked(do_v, hd, s, c), NT)
            delta = jnp.sum(prob * gprob, axis=0, keepdims=True)
            gscores = (prob * (gprob - delta)).astype(BF16)
            ds_v[hd, s, :, lanes_of(c)] = gscores
            dk += dot(gscores, stacked(q_v, hd, s, c), NN)
        dk = dk * SCALING
        part[hd, 0][s] = dk[:PLEN]
        gak_v[rows_of(s), hd * HEAD_SIZE:(hd + 1) * HEAD_SIZE] = dk[PLEN:].astype(BF16)

    def row_outputs(hd, s):
        keys_t = both(hd, 0, s).T
        values_t = both(hd, 1, s).T
        for c in range(lanes // chunk):
            out = dot(values_t, w_v[hd, s, :, lanes_of(c)], NN).astype(BF16).T
            dq = (dot(keys_t, ds_v[hd, s, :, lanes_of(c)], NN) * SCALING).astype(BF16).T
            for g, col in enumerate(columns(hd, c)):
                o_v[rows_of(s), col] = out[g * rows:(g + 1) * rows]
                dq_v[rows_of(s), col] = dq[g * rows:(g + 1) * rows]

    def summed(pair, offset):
        total = None
        for s in range(slots):
            pick = jnp.where(relative(s) == offset, 1.0, 0.0).astype(F32)
            term = part[pair][s] * pick
            total = term if total is None else total + term
        return total

    last = kvh - 1, 0
    direct_to = lax.rem(me + devices - 2 + 4 * core, devices)
    relay_to = lax.rem(me + devices + 2 - 4 * core, devices)
    back_y, back_x, back_own = {}, {}, {}
    for hd, w in pairs:
        pair = hd, w
        if pair == last:
            back_y[pair] = [
                remote(y_out[pair].at[i], y_in[pair].at[i], by_send.at[hd, w, i],
                       by_recv.at[hd, w, i], dp=near[i]) for i in range(len(near))
            ]
        else:
            back_y[pair] = [
                remote(y_out[pair].at[core], y_in[pair].at[core], by_send.at[hd, w, 0],
                       by_recv.at[hd, w, core], dp=direct_to),
                remote(y_out[pair].at[1 - core], y_in[pair].at[1 - core], by_send.at[hd, w, 1],
                       by_recv.at[hd, w, 1 - core], dp=relay_to),
                remote(y_out[pair].at[2:4], y_in[pair].at[2:4], by_send.at[hd, w, 2],
                       by_recv.at[hd, w, 2], dp=sibling),
            ]
        dst = (gpk_out, gpv_out)[w]
        cols = pl.ds(pl.multiple_of(h * width + hd * HEAD_SIZE, HEAD_SIZE), HEAD_SIZE)
        back_x[pair] = []
        for p in order:
            to = peers[p - 1]
            theirs = pl.ds(pl.multiple_of(to * span, span), span)
            back_x[pair].append(remote(
                x_out[pair].at[theirs], dst.at[:, cols],
                bx_send.at[hd, w, p - 1], bx_recv.at[hd, w, p - 1], head=to))
        back_own[pair] = pltpu.make_async_copy(
            x_out[pair].at[mine], dst.at[:, cols], bx_own.at[hd, w])

    def send_back(pair):
        if pair == last:
            for i, o in enumerate(offsets):
                y_out[pair][i] = summed(pair, MAX_SPREAD + o).astype(BF16)
                back_y[pair][i].start()
        else:
            for i in (2, 3):
                y_out[pair][i] = summed(pair, MAX_SPREAD + offsets[i]).astype(BF16)
            back_y[pair][2].start()
            y_out[pair][core] = summed(pair, 4 * core).astype(BF16)
            back_y[pair][0].start()
        own[pair][...] = summed(pair, MAX_SPREAD)

    def relay_back(pair):
        carry = summed(pair, 4 - 4 * core)
        back_y[pair][2].wait_recv()
        y_out[pair][1 - core] = (carry + y_in[pair][3 - core].astype(F32)).astype(BF16)
        back_y[pair][1].start()

    def take_back(pair):
        if pair == last:
            for copy in back_y[pair]:
                copy.wait_recv()
            came = [0, 1, 2, 3]
        else:
            for copy in back_y[pair][:2]:
                copy.wait_recv()
            came = [0, 1, 2 + core]
        for p, copy in zip(order + [0], back_x[pair] + [back_own[pair]]):
            at = pl.ds(pl.multiple_of(lax.rem(h + p, heads) * span, span), span)
            total = own[pair][at]
            for i in came:
                total = total + y_in[pair][i, at].astype(F32)
            x_out[pair][at] = total.astype(BF16)
            copy.start()

    def each_slot(work, hd, at={}):
        for s in range(slots):
            for what, *args in at.get(s, ()):
                what(*args)
            work(hd, s)

    half = slots // 2
    for hd in range(kvh):
        arrived(hd + 1 if hd > 0 else 0)
        each_slot(probabilities, hd, {half: [(relay_back, (hd - 1, 0))]} if hd > 0 else {})
        send_back((hd, 1))
        if hd == 0:
            arrived(1)
        at = {half: [(relay_back, (hd, 1))]}
        if hd + 1 < kvh:
            at[slots - 1] = at.get(slots - 1, []) + [(relay_in, hd + 2)]
        each_slot(gradients, hd, at)
        send_back((hd, 0))

    end = kvh - 1
    for hd in range(kvh):
        if hd < end:
            each_slot(row_outputs, hd)
            take_back((hd, 1))
            take_back((hd, 0))
        else:
            each_slot(row_outputs, hd, {1: [(take_back, (end, 1)), (take_back, last)]})

    for pair in pairs:
        for p in order:
            x_in[(*pair, p)].wait_send()
        for copy in back_y[pair]:
            copy.wait_send()
        for copy in back_x[pair]:
            copy.wait()
        back_own[pair].wait()
    for copy in y_in_copies.values():
        copy.wait_send()


def finish(o, dq, gak, gav, gpk, gpv, o_out, dq_out, gak_out, gav_out, gpk_out, gpv_out,
           wide_k, wide_v, sem):
    copies = [
        pltpu.make_async_copy(src, dst, sem.at[i])
        for i, (src, dst) in enumerate(
            [(o, o_out), (dq, dq_out), (gak, gak_out), (gav, gav_out),
             (wide_k, gpk_out.at[0]), (wide_v, gpv_out.at[0])])
    ]
    for copy in copies[:4]:
        copy.start()
    wide_k[...] = gpk[...].astype(F32)
    copies[4].start()
    wide_v[...] = gpv[...].astype(F32)
    copies[5].start()
    for copy in copies:
        copy.wait()


def on_device(queries, answer_keys, answer_values, prompt_keys, prompt_values,
              output_gradient, prompt_len, response_len, response_prompt):
    devices, heads = lax.axis_size("dp"), lax.axis_size("head")
    slots = response_len.shape[0]
    token_rows, q_width = queries.shape
    rows = token_rows // slots
    width = answer_keys.shape[1]
    kvh = width // HEAD_SIZE
    group = q_width // width
    lanes = group * rows
    span, full = prompt_keys.shape[1:]
    dma = pltpu.SemaphoreType.DMA
    anywhere = pl.BlockSpec(memory_space=pl.ANY)
    hbm = pl.BlockSpec(memory_space=pltpu.HBM)
    vmem = pl.BlockSpec(memory_space=pltpu.VMEM)
    vm, sm = pltpu.VMEM, pltpu.SMEM
    block = (PLEN, HEAD_SIZE)
    wide = vm((token_rows, q_width), BF16)
    narrow = vm((token_rows, width), BF16)
    square = (PLEN + rows, lanes)
    bundle = [1, 1] + [2] * (kvh - 1)
    scratch = [
        sm(prompt_len.shape, jnp.int32), sm(response_len.shape, jnp.int32),
        sm(response_prompt.shape, jnp.int32),
        wide, wide, narrow, narrow, vm((slots,) + square, F32),
        vm((kvh, slots) + square, BF16), vm((kvh, slots) + square, BF16),
        vm((span, full), BF16), vm((span, full), BF16),
    ]
    scratch += [vm((REACH, count) + block, BF16) for count in bundle]
    for shape in [vm((slots,) + block, F32), vm((REACH - 1,) + block, BF16),
                  vm((REACH - 1,) + block, BF16), vm(block, F32), vm(block, BF16)]:
        scratch += [shape] * (kvh * 2)
    scratch += [
        dma((7,)),
        dma((kvh, 2, heads - 1)), dma((kvh, 2, heads - 1)), dma((2,)),
        dma((kvh + 1, heads, REACH - 1)), dma((kvh + 1, heads, REACH - 1)),
        dma((kvh, 2, REACH - 1)), dma((kvh, 2, REACH - 1)),
        dma((kvh, 2, heads - 1)), dma((kvh, 2, heads - 1)), dma((kvh, 2)),
    ]
    sds = jax.ShapeDtypeStruct
    rows_out = [
        sds((token_rows, q_width), BF16), sds((token_rows, q_width), BF16),
        sds((token_rows, width), BF16), sds((token_rows, width), BF16),
    ]
    results = pl.pallas_call(
        functools.partial(kernel, (devices, heads, slots, rows, kvh, group)),
        out_shape=rows_out + [sds((span, full), BF16), sds((span, full), BF16)],
        in_specs=[hbm] * 9,
        out_specs=[vmem] * 4 + [anywhere] * 2,
        scratch_shapes=scratch,
        compiler_params=pltpu.CompilerParams(
            collective_id=0, has_side_effects=True, vmem_limit_bytes=48 * 1024 * 1024),
    )(*[pltpu.with_memory_space_constraint(x, pltpu.HBM) for x in (
        prompt_len, response_len, response_prompt, queries, output_gradient,
        answer_keys, answer_values, prompt_keys.reshape(span, full),
        prompt_values.reshape(span, full))])
    return pl.pallas_call(
        finish,
        out_shape=rows_out + [sds((1, span, full), F32), sds((1, span, full), F32)],
        in_specs=[vmem] * 6,
        out_specs=[anywhere] * 6,
        scratch_shapes=[vm((span, full), F32), vm((span, full), F32), dma((6,))],
        compiler_params=pltpu.CompilerParams(vmem_limit_bytes=4 * 1024 * 1024),
    )(*[pltpu.with_memory_space_constraint(x, pltpu.VMEM) for x in results])


def solution(mesh):
    in_specs = (
        P("dp", "head"),
        P("dp", "head"),
        P("dp", "head"),
        P("dp", "head", None),
        P("dp", "head", None),
        P("dp", "head"),
        P(),
        P("dp"),
        P("dp"),
    )
    out_specs = (
        P("dp", "head"),
        P("dp", "head"),
        P("dp", "head"),
        P("dp", "head"),
        P("dp", "head", None),
        P("dp", "head", None),
    )
    return jax.shard_map(
        on_device, mesh=mesh, in_specs=in_specs, out_specs=out_specs, check_vma=False
    )
```

```python
import functools
import math

import jax
import jax.numpy as jnp
from jax import lax
from jax.experimental import pallas as pl
from jax.experimental.pallas import tpu as pltpu
from jax.sharding import PartitionSpec as P

HEAD_SIZE = 128
PLEN = 256
MAX_SPREAD = 2
REACH = 2 * MAX_SPREAD + 1
MESH = pl.DeviceIdType.MESH
SCALING = 1.0 / math.sqrt(HEAD_SIZE)
F32 = jnp.float32
BF16 = jnp.bfloat16


def dot(a, b, dims):
    return lax.dot_general(a, b, (dims, ((), ())), preferred_element_type=F32)


NN = ((1,), (0,))
NT = ((1,), (1,))
TN = ((0,), (0,))


def kernel(sizes, *refs):
    devices, heads, slots, rows, kvh, group = sizes
    pairs = [(hd, w) for hd in range(kvh) for w in range(2)]
    bundles = [[pair] for pair in pairs]
    place = {pair: (b, j) for b, bundle in enumerate(bundles) for j, pair in enumerate(bundle)}
    refs = list(refs)
    (plen_hbm, rlen_hbm, rprompt_hbm, q_hbm, do_hbm, ak_hbm, av_hbm, pk_hbm, pv_hbm,
     o_v, dq_v, gak_v, gav_v, gpk_out, gpv_out,
     plen_ref, rlen_ref, rprompt_ref,
     q_v, do_v, ak_v, av_v, p_v, w_v, ds_v, pk_v, pv_v) = refs[:27]
    kv, refs = refs[27:27 + len(bundles)], refs[27 + len(bundles):]
    (part, y_out, y_in, own, x_out) = [
        dict(zip(pairs, refs[i * len(pairs):(i + 1) * len(pairs)])) for i in range(5)
    ]
    (in_sem, x_send, x_recv, x_own, y_send, y_recv,
     by_send, by_recv, bx_send, bx_recv, bx_own) = refs[5 * len(pairs):]

    me = lax.axis_index("dp")
    h = lax.axis_index("head")
    offsets = [-2, 2, -1, 1]
    near = [lax.rem(me + devices + o, devices) for o in offsets]
    span = PLEN // heads
    width = kvh * HEAD_SIZE
    lanes = group * rows
    chunk = min(512, lanes)
    per = chunk // rows
    all_rows = PLEN + rows
    peers = [lax.rem(h + p, heads) for p in range(1, heads)]
    order = [p for p in range(1, heads) if p != heads // 2] + [heads // 2]
    mine = pl.ds(pl.multiple_of(h * span, span), span)

    prompt_loads = [
        pltpu.make_async_copy(src, dst, x_own.at[i])
        for i, (src, dst) in enumerate([(pk_hbm, pk_v), (pv_hbm, pv_v)])
    ]
    loads = [
        pltpu.make_async_copy(src, dst, in_sem.at[i])
        for i, (src, dst) in enumerate(
            [(q_hbm, q_v), (do_hbm, do_v), (ak_hbm, ak_v), (av_hbm, av_v),
             (plen_hbm, plen_ref), (rlen_hbm, rlen_ref), (rprompt_hbm, rprompt_ref)])
    ]
    for load in prompt_loads + loads:
        load.start()

    def remote(src, dst, send, recv, **where):
        return pltpu.make_async_remote_copy(
            src_ref=src, dst_ref=dst, send_sem=send, recv_sem=recv,
            device_id=where, device_id_type=MESH)

    barrier = pltpu.get_barrier_semaphore()
    for p in peers:
        pl.semaphore_signal(barrier, inc=1, device_id={"head": p}, device_id_type=MESH)
    for d in near:
        pl.semaphore_signal(barrier, inc=1, device_id={"dp": d}, device_id_type=MESH)
    for load in prompt_loads:
        load.wait()
    for hd, w in pairs:
        b, j = place[hd, w]
        cols = pl.ds(pl.multiple_of(h * width + hd * HEAD_SIZE, HEAD_SIZE), HEAD_SIZE)
        kv[b][MAX_SPREAD, j, mine] = (pk_v, pv_v)[w][:, cols]
    pl.semaphore_wait(barrier, len(peers) + len(near))

    x_in = {}

    def exchange(hd, w):
        b, j = place[hd, w]
        for p in order:
            to = peers[p - 1]
            cols = pl.ds(pl.multiple_of(to * width + hd * HEAD_SIZE, HEAD_SIZE), HEAD_SIZE)
            x_in[hd, w, p] = remote(
                (pk_v, pv_v)[w].at[:, cols], kv[b].at[MAX_SPREAD, j, mine],
                x_send.at[hd, w, p - 1], x_recv.at[hd, w, p - 1], head=to)
            x_in[hd, w, p].start()

    y_in_copies = {}

    def forward(b, piece):
        if piece > 0:
            for pair in bundles[b]:
                x_in[(*pair, piece)].wait_recv()
        source = lax.rem(h + heads - piece, heads)
        at = pl.ds(pl.multiple_of(source * span, span), span)
        for i, o in enumerate(offsets):
            copy = remote(
                kv[b].at[MAX_SPREAD, :, at], kv[b].at[MAX_SPREAD - o, :, at],
                y_send.at[b, piece, i], y_recv.at[b, piece, i], dp=near[i])
            y_in_copies[b, piece, i] = copy
            copy.start()

    def arrived(b):
        for piece in range(heads):
            for i in range(len(near)):
                y_in_copies[b, piece, i].wait_recv()

    exchange(*pairs[0])
    forward(0, 0)
    for pair in pairs[1:]:
        exchange(*pair)
    for b in range(1, len(bundles)):
        forward(b, 0)
    for b in range(len(bundles)):
        for p in order:
            forward(b, p)
    for load in loads:
        load.wait()

    def rows_of(s):
        return slice(s * rows, (s + 1) * rows)

    def columns(hd, c):
        first = hd * group + c * per
        return [slice((first + g) * HEAD_SIZE, (first + g + 1) * HEAD_SIZE) for g in range(per)]

    def stacked(ref, hd, s, c):
        return jnp.concatenate([ref[rows_of(s), col] for col in columns(hd, c)], axis=0)

    def relative(s):
        return lax.rem(rprompt_ref[s] - me + (devices + MAX_SPREAD), devices)

    def both(hd, w, s):
        rel = jnp.minimum(relative(s), REACH - 1)
        tail = (ak_v, av_v)[w][rows_of(s), hd * HEAD_SIZE:(hd + 1) * HEAD_SIZE]
        b, j = place[hd, w]
        return jnp.concatenate([kv[b][rel, j], tail], axis=0)

    def lanes_of(c):
        return slice(c * chunk, (c + 1) * chunk)

    def probabilities(hd, s):
        psize = plen_ref[rprompt_ref[s]]
        rlen = rlen_ref[s]
        keys = both(hd, 0, s)
        live = ((lax.broadcasted_iota(jnp.int32, (1, chunk), 1) & (rows - 1)) < rlen).astype(F32)
        head_seen = lax.broadcasted_iota(jnp.int32, (PLEN, chunk), 0) < psize
        tail_seen = lax.broadcasted_iota(jnp.int32, (rows, chunk), 0) <= (
            lax.broadcasted_iota(jnp.int32, (rows, chunk), 1) & (rows - 1))
        dv = jnp.zeros((all_rows, HEAD_SIZE), F32)
        for c in range(lanes // chunk):
            scores = dot(keys, stacked(q_v, hd, s, c), NT)
            masked = jnp.concatenate([
                jnp.where(head_seen, scores[:PLEN], -jnp.inf),
                jnp.where(tail_seen, scores[PLEN:], -jnp.inf)], axis=0)
            top = jnp.max(masked, axis=0, keepdims=True)
            e = jnp.exp2((masked - top) * (SCALING * math.log2(math.e)))
            prob = e * (live / jnp.sum(e, axis=0, keepdims=True))
            p_v[s, :, lanes_of(c)] = prob
            weights = prob.astype(BF16)
            w_v[hd, s, :, lanes_of(c)] = weights
            dv += dot(weights, stacked(do_v, hd, s, c), NN)
        part[hd, 1][s] = dv[:PLEN]
        gav_v[rows_of(s), hd * HEAD_SIZE:(hd + 1) * HEAD_SIZE] = dv[PLEN:].astype(BF16)

    def gradients(hd, s):
        values = both(hd, 1, s)
        dk = jnp.zeros((all_rows, HEAD_SIZE), F32)
        for c in range(lanes // chunk):
            prob = p_v[s, :, lanes_of(c)]
            gprob = dot(values, stacked(do_v, hd, s, c), NT)
            delta = jnp.sum(prob * gprob, axis=0, keepdims=True)
            gscores = (prob * (gprob - delta)).astype(BF16)
            ds_v[hd, s, :, lanes_of(c)] = gscores
            dk += dot(gscores, stacked(q_v, hd, s, c), NN)
        dk = dk * SCALING
        part[hd, 0][s] = dk[:PLEN]
        gak_v[rows_of(s), hd * HEAD_SIZE:(hd + 1) * HEAD_SIZE] = dk[PLEN:].astype(BF16)

    def row_outputs(hd, s):
        keys_t = both(hd, 0, s).T
        values_t = both(hd, 1, s).T
        for c in range(lanes // chunk):
            out = dot(values_t, w_v[hd, s, :, lanes_of(c)], NN).astype(BF16).T
            dq = (dot(keys_t, ds_v[hd, s, :, lanes_of(c)], NN) * SCALING).astype(BF16).T
            for g, col in enumerate(columns(hd, c)):
                o_v[rows_of(s), col] = out[g * rows:(g + 1) * rows]
                dq_v[rows_of(s), col] = dq[g * rows:(g + 1) * rows]

    def summed(pair, offset):
        total = None
        for s in range(slots):
            pick = jnp.where(relative(s) == offset, 1.0, 0.0).astype(F32)
            term = part[pair][s] * pick
            total = term if total is None else total + term
        return total

    last = kvh - 1, 0
    core = lax.rem(me, 2)
    sibling = me + 1 - 2 * core
    direct_to = lax.rem(me + devices - 2 + 4 * core, devices)
    relay_to = lax.rem(me + devices + 2 - 4 * core, devices)
    back_y, back_x, back_own = {}, {}, {}
    for hd, w in pairs:
        pair = hd, w
        if pair == last:
            back_y[pair] = [
                remote(y_out[pair].at[i], y_in[pair].at[i], by_send.at[hd, w, i],
                       by_recv.at[hd, w, i], dp=near[i]) for i in range(len(near))
            ]
        else:
            back_y[pair] = [
                remote(y_out[pair].at[core], y_in[pair].at[core], by_send.at[hd, w, 0],
                       by_recv.at[hd, w, core], dp=direct_to),
                remote(y_out[pair].at[1 - core], y_in[pair].at[1 - core], by_send.at[hd, w, 1],
                       by_recv.at[hd, w, 1 - core], dp=relay_to),
                remote(y_out[pair].at[2:4], y_in[pair].at[2:4], by_send.at[hd, w, 2],
                       by_recv.at[hd, w, 2], dp=sibling),
            ]
        dst = (gpk_out, gpv_out)[w]
        cols = pl.ds(pl.multiple_of(h * width + hd * HEAD_SIZE, HEAD_SIZE), HEAD_SIZE)
        back_x[pair] = []
        for p in order:
            to = peers[p - 1]
            theirs = pl.ds(pl.multiple_of(to * span, span), span)
            back_x[pair].append(remote(
                x_out[pair].at[theirs], dst.at[:, cols],
                bx_send.at[hd, w, p - 1], bx_recv.at[hd, w, p - 1], head=to))
        back_own[pair] = pltpu.make_async_copy(
            x_out[pair].at[mine], dst.at[:, cols], bx_own.at[hd, w])

    def send_back(pair):
        if pair == last:
            for i, o in enumerate(offsets):
                y_out[pair][i] = summed(pair, MAX_SPREAD + o).astype(BF16)
                back_y[pair][i].start()
        else:
            for i in (2, 3):
                y_out[pair][i] = summed(pair, MAX_SPREAD + offsets[i]).astype(BF16)
            back_y[pair][2].start()
            y_out[pair][core] = summed(pair, 4 * core).astype(BF16)
            back_y[pair][0].start()
        own[pair][...] = summed(pair, MAX_SPREAD)

    def relay_back(pair):
        carry = summed(pair, 4 - 4 * core)
        back_y[pair][2].wait_recv()
        y_out[pair][1 - core] = (carry + y_in[pair][3 - core].astype(F32)).astype(BF16)
        back_y[pair][1].start()

    def take_back(pair):
        if pair == last:
            for copy in back_y[pair]:
                copy.wait_recv()
            came = [0, 1, 2, 3]
        else:
            for copy in back_y[pair][:2]:
                copy.wait_recv()
            came = [0, 1, 2 + core]
        for p, copy in zip(order + [0], back_x[pair] + [back_own[pair]]):
            at = pl.ds(pl.multiple_of(lax.rem(h + p, heads) * span, span), span)
            total = own[pair][at]
            for i in came:
                total = total + y_in[pair][i, at].astype(F32)
            x_out[pair][at] = total.astype(BF16)
            copy.start()

    def each_slot(work, hd, at={}):
        for s in range(slots):
            for what, *args in at.get(s, ()):
                what(*args)
            work(hd, s)

    half = slots // 2
    for hd in range(kvh):
        arrived(2 * hd)
        each_slot(probabilities, hd, {half: [(relay_back, (hd - 1, 0))]} if hd > 0 else {})
        send_back((hd, 1))
        arrived(2 * hd + 1)
        each_slot(gradients, hd, {half: [(relay_back, (hd, 1))]})
        send_back((hd, 0))

    end = kvh - 1
    for hd in range(kvh):
        if hd < end:
            each_slot(row_outputs, hd)
            take_back((hd, 1))
            take_back((hd, 0))
        else:
            each_slot(row_outputs, hd, {1: [(take_back, (end, 1)), (take_back, last)]})

    for pair in pairs:
        for p in order:
            x_in[(*pair, p)].wait_send()
        for copy in back_y[pair]:
            copy.wait_send()
        for copy in back_x[pair]:
            copy.wait()
        back_own[pair].wait()
    for copy in y_in_copies.values():
        copy.wait_send()


def finish(o, dq, gak, gav, gpk, gpv, o_out, dq_out, gak_out, gav_out, gpk_out, gpv_out,
           wide_k, wide_v, sem):
    copies = [
        pltpu.make_async_copy(src, dst, sem.at[i])
        for i, (src, dst) in enumerate(
            [(o, o_out), (dq, dq_out), (gak, gak_out), (gav, gav_out),
             (wide_k, gpk_out.at[0]), (wide_v, gpv_out.at[0])])
    ]
    for copy in copies[:4]:
        copy.start()
    wide_k[...] = gpk[...].astype(F32)
    copies[4].start()
    wide_v[...] = gpv[...].astype(F32)
    copies[5].start()
    for copy in copies:
        copy.wait()


def on_device(queries, answer_keys, answer_values, prompt_keys, prompt_values,
              output_gradient, prompt_len, response_len, response_prompt):
    devices, heads = lax.axis_size("dp"), lax.axis_size("head")
    slots = response_len.shape[0]
    token_rows, q_width = queries.shape
    rows = token_rows // slots
    width = answer_keys.shape[1]
    kvh = width // HEAD_SIZE
    group = q_width // width
    lanes = group * rows
    span, full = prompt_keys.shape[1:]
    dma = pltpu.SemaphoreType.DMA
    anywhere = pl.BlockSpec(memory_space=pl.ANY)
    hbm = pl.BlockSpec(memory_space=pltpu.HBM)
    vmem = pl.BlockSpec(memory_space=pltpu.VMEM)
    vm, sm = pltpu.VMEM, pltpu.SMEM
    block = (PLEN, HEAD_SIZE)
    wide = vm((token_rows, q_width), BF16)
    narrow = vm((token_rows, width), BF16)
    square = (PLEN + rows, lanes)
    bundle = [1] * (2 * kvh)
    scratch = [
        sm(prompt_len.shape, jnp.int32), sm(response_len.shape, jnp.int32),
        sm(response_prompt.shape, jnp.int32),
        wide, wide, narrow, narrow, vm((slots,) + square, F32),
        vm((kvh, slots) + square, BF16), vm((kvh, slots) + square, BF16),
        vm((span, full), BF16), vm((span, full), BF16),
    ]
    scratch += [vm((REACH, count) + block, BF16) for count in bundle]
    for shape in [vm((slots,) + block, F32), vm((REACH - 1,) + block, BF16),
                  vm((REACH - 1,) + block, BF16), vm(block, F32), vm(block, BF16)]:
        scratch += [shape] * (kvh * 2)
    scratch += [
        dma((7,)),
        dma((kvh, 2, heads - 1)), dma((kvh, 2, heads - 1)), dma((2,)),
        dma((2 * kvh, heads, REACH - 1)), dma((2 * kvh, heads, REACH - 1)),
        dma((kvh, 2, REACH - 1)), dma((kvh, 2, REACH - 1)),
        dma((kvh, 2, heads - 1)), dma((kvh, 2, heads - 1)), dma((kvh, 2)),
    ]
    sds = jax.ShapeDtypeStruct
    rows_out = [
        sds((token_rows, q_width), BF16), sds((token_rows, q_width), BF16),
        sds((token_rows, width), BF16), sds((token_rows, width), BF16),
    ]
    results = pl.pallas_call(
        functools.partial(kernel, (devices, heads, slots, rows, kvh, group)),
        out_shape=rows_out + [sds((span, full), BF16), sds((span, full), BF16)],
        in_specs=[hbm] * 9,
        out_specs=[vmem] * 4 + [anywhere] * 2,
        scratch_shapes=scratch,
        compiler_params=pltpu.CompilerParams(
            collective_id=0, has_side_effects=True, vmem_limit_bytes=48 * 1024 * 1024),
    )(*[pltpu.with_memory_space_constraint(x, pltpu.HBM) for x in (
        prompt_len, response_len, response_prompt, queries, output_gradient,
        answer_keys, answer_values, prompt_keys.reshape(span, full),
        prompt_values.reshape(span, full))])
    return pl.pallas_call(
        finish,
        out_shape=rows_out + [sds((1, span, full), F32), sds((1, span, full), F32)],
        in_specs=[vmem] * 6,
        out_specs=[anywhere] * 6,
        scratch_shapes=[vm((span, full), F32), vm((span, full), F32), dma((6,))],
        compiler_params=pltpu.CompilerParams(vmem_limit_bytes=4 * 1024 * 1024),
    )(*[pltpu.with_memory_space_constraint(x, pltpu.VMEM) for x in results])


def solution(mesh):
    in_specs = (
        P("dp", "head"),
        P("dp", "head"),
        P("dp", "head"),
        P("dp", "head", None),
        P("dp", "head", None),
        P("dp", "head"),
        P(),
        P("dp"),
        P("dp"),
    )
    out_specs = (
        P("dp", "head"),
        P("dp", "head"),
        P("dp", "head"),
        P("dp", "head"),
        P("dp", "head", None),
        P("dp", "head", None),
    )
    return jax.shard_map(
        on_device, mesh=mesh, in_specs=in_specs, out_specs=out_specs, check_vma=False
    )
```
